512 devices in a mesh: enc: 16 (over x, z_hi), lat: 4 (over z_lo, core), lon: 8 (over y).
Axes of the slice: x: 4, y: 8, z: 8 (z_hi: 4, z_lo: 2; z = z_hi * 2 + z_lo), core: 2. Of those that a mesh axis runs over, the one named last changes fastest.
Arguments:
- atmos: bfloat16 [96, 192, 13, 500], P('enc', ('lon', 'lat')), may hold values from -6 to 6
- land_sea: int32 [96, 192, 100], P('enc', ('lon', 'lat')), may hold values 0 or 1
- level_count: int32 [96, 192], P('enc', ('lon', 'lat')), may hold values from 8 to 13
- atm_weight: bfloat16 [500, 512], replicated, may hold values from -0.25 to 0.25
- land_weight: bfloat16 [100, 512], replicated, may hold values from -1.25 to 1.25
- level_embed: float32 [13, 512], replicated, may hold values from -6 to 6
- latent_query: bfloat16 [3, 512], replicated, may hold values from -6 to 6
- key_weight: bfloat16 [512, 512], replicated, may hold values from -0.25 to 0.25
- value_weight: bfloat16 [512, 512], replicated, may hold values from -0.25 to 0.25
- merge_weight: bfloat16 [2048, 1024], replicated, may hold values from -0.125 to 0.125
- lat_shift: int32 [1], replicated, may hold values from 1 to 5
- lon_shift: int32 [1], replicated, may hold values from 1 to 11
- qkv_weight: bfloat16 [1024, 3072], P(None, 'enc'), may hold values from -1 to 1
- proj_weight: bfloat16 [1024, 1024], P('enc'), may hold values from -0.75 to 0.75
- cotangent: bfloat16 [3, 48, 96, 1024], P(None, 'lat', 'lon'), may hold values from -6 to 6
Outputs:
- grad_latent: bfloat16 [3, 48, 96, 1024], P(None, 'lat', 'lon', 'enc')
- grad_qkv: float32 [1024, 3072], P(('lat', 'lon'), 'enc')
- grad_proj: float32 [1024, 1024], P('enc', ('lat', 'lon'))
The draws below stay inside these ranges and needn't reach their ends.
Inputs may be any that keep to these rules, and one draw needn't show every extreme that they name: Levels 0 to level_count - 1 of a fine patch lie above ground; the others carry no data.
All inputs are finite; a program needn't handle non-finite values. No bound on the sum of `land_sea` on one device may be relied on, other than what follows from the above.
Results may differ from the reference program's by a relative error of at most 0.033.
Values may be sent and summed in bfloat16 or wider, within the bound.
A program may use at most 128 MiB of HBM per device.

```python
import jax
import jax.numpy as jnp
from jax import lax

D_ENC = 512
D = 1024
HEADS = 16
PHEADS = 16
LEVELS = 13
VARS_ATM = 5
PATCH = 10
LATENTS = 3
WIN_LAT = 6
WIN_LON = 12
HD = 64
PROWS = 48
PCOLS = 96


def draw_qkv_weight(key, part):
    key = jax.random.fold_in(key, 11)
    base_key, offset_key = jax.random.split(key)
    spread = D ** (-0.5)
    base = jax.random.truncated_normal(base_key, -6.0, 6.0, (D, 3 * D), jnp.float32) * spread
    offset = jax.random.truncated_normal(offset_key, -6.0, 6.0, (1, 3 * D), jnp.float32) * spread
    return (base + offset).astype(jnp.bfloat16)


def with_ends(drawn, rng, low, high):
    extent = drawn.shape
    place = [jax.random.randint(jax.random.fold_in(rng, axis), (), 0, extent[axis]) for axis in range(len(extent))]
    drawn = drawn.at[tuple(place)].set(low)
    longest = extent.index(max(extent))
    place[longest] = (place[longest] + 1) % extent[longest]
    return drawn.at[tuple(place)].set(high)


def block_scale(stream_key, extent, cuts, least, largest):
    loudness, own = 1.0, jax.random.fold_in(stream_key, 6)
    for axis_at, parts in cuts:
        steps = jnp.exp(jax.random.uniform(jax.random.fold_in(own, axis_at), (parts,), jnp.float32, least / len(cuts), largest / len(cuts)))
        loudness = loudness * jnp.repeat(steps, extent[axis_at] // parts).reshape([-1 if axis == axis_at else 1 for axis in range(len(extent))])
    return loudness


def noise(stream_key, shape, scale, limit, cuts=(), kind=jnp.bfloat16):
    entries = scale * jax.random.normal(stream_key, shape, jnp.float32)
    if cuts:
        entries = entries * block_scale(stream_key, shape, cuts, -0.22, 0.18)
    return jnp.clip(entries, -limit, limit).astype(kind)


def setup_inputs(seed: int = 0) -> dict:
    splits = jax.random.split(jax.random.key(seed), 16)
    return {
        "atmos": noise(splits[0], (2 * PROWS, 2 * PCOLS, LEVELS, VARS_ATM * PATCH * PATCH), 1.0, 6.0, ((0, 16), (1, 32))),
        "land_sea": with_ends((jax.random.randint(splits[1], (2 * PROWS, 2 * PCOLS, PATCH * PATCH), 0, 10) < 3).astype(jnp.int32), jax.random.fold_in(splits[1], 1), 0, 1),
        "level_count": with_ends(jax.random.randint(splits[2], (2 * PROWS, 2 * PCOLS), 8, LEVELS + 1), jax.random.fold_in(splits[2], 1), 8, LEVELS).astype(jnp.int32),
        "atm_weight": noise(splits[3], (VARS_ATM * PATCH * PATCH, D_ENC), (VARS_ATM * PATCH * PATCH) ** -0.5, 0.25),
        "land_weight": noise(splits[4], (PATCH * PATCH, D_ENC), (PATCH * PATCH // 4) ** -0.5, 1.25),
        "level_embed": noise(splits[5], (LEVELS, D_ENC), 1.0, 6.0, (), jnp.float32),
        "latent_query": noise(splits[6], (LATENTS, D_ENC), 1.0, 6.0),
        "key_weight": noise(splits[7], (D_ENC, D_ENC), D_ENC ** -0.5, 0.25),
        "value_weight": noise(splits[8], (D_ENC, D_ENC), D_ENC ** -0.5, 0.25),
        "merge_weight": noise(splits[9], (4 * D_ENC, D), (4 * D_ENC) ** -0.5, 0.125),
        "lat_shift": jax.random.randint(splits[10], (1,), 1, WIN_LAT).astype(jnp.int32),
        "lon_shift": jax.random.randint(splits[11], (1,), 1, WIN_LON).astype(jnp.int32),
        "qkv_weight": draw_qkv_weight(jax.random.fold_in(splits[15], 71), 0),
        "proj_weight": noise(splits[13], (D, D), HD ** -0.5, 0.75, ((0, 16),)),
        "cotangent": noise(splits[14], (LATENTS, PROWS, PCOLS, D), 1.0, 6.0, ((1, 4), (2, 8))),
    }


epsilon = 1e-05

def layer_norm(values):
    centre = lax.optimization_barrier(jnp.mean(values, axis=-1, keepdims=True))
    centred = values - centre
    variance = lax.optimization_barrier(jnp.mean(centred * centred, axis=-1, keepdims=True))
    inverse = lax.rsqrt(variance + epsilon)
    return (centred * inverse, inverse)

def encode(atmos, land_sea, level_count, atm_weight, land_weight, level_embed, latent_query, key_weight, value_weight):
    row_count, col_count, levels, pixels = atmos.shape
    patches = row_count * col_count
    embedded = jnp.dot(atmos.reshape(patches * levels, pixels), atm_weight, preferred_element_type=jnp.float32)
    embedded = embedded.reshape(patches, levels, -1)
    static = jnp.dot(land_sea.reshape(patches, -1).astype(jnp.bfloat16), land_weight, preferred_element_type=jnp.float32)
    embedded = embedded + level_embed[None, :, :] + static[:, None, :]
    normed, unused_scale = layer_norm(embedded)
    tokens = normed.astype(jnp.bfloat16).reshape(patches * levels, -1)
    key_rows = jnp.dot(tokens, key_weight, preferred_element_type=jnp.float32).astype(jnp.bfloat16)
    value_rows = jnp.dot(tokens, value_weight, preferred_element_type=jnp.float32).astype(jnp.bfloat16)
    key_rows = key_rows.reshape(patches, levels, PHEADS, -1)
    value_rows = value_rows.reshape(patches, levels, PHEADS, -1)
    queries = latent_query.reshape(latent_query.shape[0], PHEADS, -1)
    score_scale = key_rows.shape[-1] ** (-0.5)
    scores = jnp.einsum('mhc,plhc->phml', queries.astype(jnp.float32), key_rows.astype(jnp.float32)) * score_scale
    present = jnp.arange(levels, dtype=jnp.int32)[None, :] < level_count.reshape(patches, 1)
    weights = jnp.where(present[:, None, None, :], jnp.exp(scores), 0.0)
    level_probs = (weights / lax.optimization_barrier(jnp.sum(weights, axis=-1, keepdims=True))).astype(jnp.bfloat16)
    attended = jnp.einsum('phml,plhc->pmhc', level_probs.astype(jnp.float32), value_rows.astype(jnp.float32))
    attended = attended.astype(jnp.bfloat16).reshape(row_count, col_count, queries.shape[0], -1)
    return attended.transpose(2, 0, 1, 3)

def merge_patches(fine, merge_weight):
    levels, row_count, col_count, width = fine.shape
    grouped = fine.reshape(levels, row_count // 2, 2, col_count // 2, 2, width).transpose(0, 1, 3, 4, 2, 5)
    grouped = grouped.reshape(levels, row_count // 2, col_count // 2, 4 * width)
    merge_in = layer_norm(grouped.astype(jnp.float32))[0].astype(jnp.bfloat16)
    merged = jnp.dot(merge_in.reshape(-1, 4 * width), merge_weight, preferred_element_type=jnp.float32).astype(jnp.bfloat16)
    return merged.reshape(levels, row_count // 2, col_count // 2, -1)

def split_windows(field, head_count):
    levels, row_count, col_count, unused = field.shape
    pieces = field.reshape(levels, row_count // WIN_LAT, WIN_LAT, col_count // WIN_LON, WIN_LON, head_count, -1)
    pieces = pieces.transpose(1, 3, 5, 0, 2, 4, 6)
    return pieces.reshape(row_count // WIN_LAT, col_count // WIN_LON, head_count, levels * WIN_LAT * WIN_LON, -1)

def join_windows(pieces, levels):
    row_windows, col_windows, head_count, unused, channels = pieces.shape
    field = pieces.reshape(row_windows, col_windows, head_count, levels, WIN_LAT, WIN_LON, channels)
    field = field.transpose(3, 0, 4, 1, 5, 2, 6)
    return field.reshape(levels, row_windows * WIN_LAT, col_windows * WIN_LON, head_count * channels)

def token_sides(row_sides, levels):
    row_windows = row_sides.shape[0] // WIN_LAT
    token_side = jnp.broadcast_to(row_sides.reshape(row_windows, 1, WIN_LAT, 1), (row_windows, levels, WIN_LAT, WIN_LON))
    return token_side.reshape(row_windows, levels * WIN_LAT * WIN_LON)

def window_pass(qkv_win, grad_win, side_win):
    head_dim = grad_win.shape[-1]
    queries = qkv_win[..., :head_dim].astype(jnp.float32)
    key_part = qkv_win[..., head_dim:2 * head_dim].astype(jnp.float32)
    value_part = qkv_win[..., 2 * head_dim:].astype(jnp.float32)
    grad_heads = grad_win.astype(jnp.float32)
    score_scale = head_dim ** (-0.5)
    scores = jnp.einsum('...td,...ud->...tu', queries, key_part) * score_scale
    same_side = side_win[..., :, None] == side_win[..., None, :]
    weights = jnp.where(same_side, jnp.exp(scores), 0.0)
    probs = weights / lax.optimization_barrier(jnp.sum(weights, axis=-1, keepdims=True))
    probs_low = probs.astype(jnp.bfloat16).astype(jnp.float32)
    heads_out = jnp.einsum('...tu,...ud->...td', probs_low, value_part).astype(jnp.bfloat16)
    grad_probs = jnp.einsum('...td,...ud->...tu', grad_heads, value_part)
    grad_values = jnp.einsum('...tu,...td->...ud', probs_low, grad_heads).astype(jnp.bfloat16)
    grad_scores = probs * (grad_probs - lax.optimization_barrier(jnp.sum(grad_probs * probs, axis=-1, keepdims=True)))
    grad_low = grad_scores.astype(jnp.bfloat16).astype(jnp.float32)
    grad_query = (jnp.einsum('...tu,...ud->...td', grad_low, key_part) * score_scale).astype(jnp.bfloat16)
    grad_keys = (jnp.einsum('...tu,...td->...ud', grad_low, queries) * score_scale).astype(jnp.bfloat16)
    return (heads_out, jnp.concatenate([grad_query, grad_keys, grad_values], axis=-1))

def reference(atmos, land_sea, level_count, atm_weight, land_weight, level_embed, latent_query, key_weight, value_weight, merge_weight, lat_shift, lon_shift, qkv_weight, proj_weight, cotangent):
    half_rows = atmos.shape[0] // 2
    fine_cols = atmos.shape[1]
    atmos_pairs = atmos.reshape(half_rows, 2, fine_cols, atmos.shape[2], atmos.shape[3])
    land_pairs = land_sea.reshape(half_rows, 2, fine_cols, land_sea.shape[2])
    count_pairs = level_count.reshape(half_rows, 2, fine_cols)

    def one_row(packed):
        fine = encode(packed[0], packed[1], packed[2], atm_weight, land_weight, level_embed, latent_query, key_weight, value_weight)
        return merge_patches(fine, merge_weight)[:, 0]
    merged_rows = lax.map(one_row, (atmos_pairs, land_pairs, count_pairs))
    latents = merged_rows.transpose(1, 0, 2, 3)
    levels, row_total, col_total, unused = latents.shape
    row_shift = lat_shift[0]
    col_shift = lon_shift[0]
    normed, inverse = layer_norm(latents.astype(jnp.float32))
    hidden = normed.astype(jnp.bfloat16)
    hidden_flat = hidden.reshape(-1, D)
    qkv_all = jnp.dot(hidden_flat, qkv_weight, preferred_element_type=jnp.float32).astype(jnp.bfloat16)
    qkv_all = qkv_all.reshape(levels, row_total, col_total, 3 * D)
    cot_flat = cotangent.reshape(-1, D)
    head_grad = jnp.dot(cot_flat, proj_weight.T, preferred_element_type=jnp.float32).astype(jnp.bfloat16)
    head_grad = head_grad.reshape(levels, row_total, col_total, D)
    rolled_qkv = jnp.roll(qkv_all, (row_shift, col_shift), axis=(1, 2))
    rolled_grad = jnp.roll(head_grad, (row_shift, col_shift), axis=(1, 2))
    row_sides = jnp.arange(row_total, dtype=jnp.int32) < row_shift
    side_rows = token_sides(row_sides, levels)
    outputs, gradients = lax.map(lambda packed: window_pass(packed[0], packed[1], packed[2]), (split_windows(rolled_qkv, HEADS), split_windows(rolled_grad, HEADS), side_rows))
    heads_out = jnp.roll(join_windows(outputs, levels), (-row_shift, -col_shift), axis=(1, 2))
    grad_rows = jnp.roll(join_windows(gradients, levels), (-row_shift, -col_shift), axis=(1, 2))
    grad_flat = grad_rows.reshape(-1, 3 * D)
    factor = (levels * row_total * col_total) ** (-0.5)
    grad_qkv = jnp.dot(hidden_flat.T, grad_flat, preferred_element_type=jnp.float32) * factor
    grad_proj = jnp.dot(heads_out.reshape(-1, D).T, cot_flat, preferred_element_type=jnp.float32) * factor
    grad_hidden = jnp.dot(grad_flat, qkv_weight.T, preferred_element_type=jnp.float32)
    grad_hidden = grad_hidden.reshape(levels, row_total, col_total, D)
    mean_grad = lax.optimization_barrier(jnp.mean(grad_hidden, axis=-1, keepdims=True))
    mean_cross = lax.optimization_barrier(jnp.mean(grad_hidden * normed, axis=-1, keepdims=True))
    grad_latent = cotangent.astype(jnp.float32) + inverse * (grad_hidden - mean_grad - normed * mean_cross)
    return (grad_latent.astype(jnp.bfloat16), grad_qkv, grad_proj)
```

```python
import functools

import jax
import jax.numpy as jnp
import numpy as np
from jax import lax
from jax.experimental import pallas as pl
from jax.experimental.pallas import tpu as pltpu
from jax.sharding import PartitionSpec as P

PHEADS = 16
WIN_LAT = 6
WIN_LON = 12
HD = 64
LEVELS = 3
MESH = pl.DeviceIdType.MESH

epsilon = 1e-05
F32 = jnp.float32
BF16 = jnp.bfloat16


def layer_norm(values):
    centre = jnp.mean(values, axis=-1, keepdims=True)
    centred = values - centre
    variance = jnp.mean(centred * centred, axis=-1, keepdims=True)
    inverse = lax.rsqrt(variance + epsilon)
    return (centred * inverse, inverse)


def encode(
    atmos,
    land_sea,
    level_count,
    atm_weight,
    land_weight,
    level_embed,
    latent_query,
    key_weight,
    value_weight,
):
    row_count, col_count, levels, pixels = atmos.shape
    patches = row_count * col_count
    embedded = jnp.dot(
        atmos.reshape(patches * levels, pixels), atm_weight, preferred_element_type=jnp.float32
    )
    embedded = embedded.reshape(patches, levels, -1)
    static = jnp.dot(
        land_sea.reshape(patches, -1).astype(jnp.bfloat16),
        land_weight,
        preferred_element_type=jnp.float32,
    )
    embedded = embedded + level_embed[None, :, :] + static[:, None, :]
    normed, unused_scale = layer_norm(embedded)
    tokens = normed.astype(jnp.bfloat16).reshape(patches * levels, -1)
    key_rows = jnp.dot(tokens, key_weight, preferred_element_type=jnp.float32).astype(jnp.bfloat16)
    value_rows = jnp.dot(tokens, value_weight, preferred_element_type=jnp.float32).astype(
        jnp.bfloat16
    )
    key_rows = key_rows.reshape(patches, levels, PHEADS, -1)
    value_rows = value_rows.reshape(patches, levels, PHEADS, -1)
    queries = latent_query.reshape(latent_query.shape[0], PHEADS, -1)
    score_scale = key_rows.shape[-1] ** (-0.5)
    scores = (
        jnp.einsum("mhc,plhc->phml", queries, key_rows, preferred_element_type=jnp.float32)
        * score_scale
    )
    present = jnp.arange(levels, dtype=jnp.int32)[None, :] < level_count.reshape(patches, 1)
    weights = jnp.where(present[:, None, None, :], jnp.exp(scores), 0.0)
    level_probs = (weights / jnp.sum(weights, axis=-1, keepdims=True)).astype(jnp.bfloat16)
    attended = jnp.einsum(
        "phml,plhc->pmhc", level_probs, value_rows, preferred_element_type=jnp.float32
    )
    attended = attended.astype(jnp.bfloat16).reshape(row_count, col_count, queries.shape[0], -1)
    return attended.transpose(2, 0, 1, 3)


def merge_patches(fine, merge_weight):
    levels, row_count, col_count, width = fine.shape
    grouped = fine.reshape(levels, row_count // 2, 2, col_count // 2, 2, width).transpose(
        0, 1, 3, 4, 2, 5
    )
    grouped = grouped.reshape(levels, row_count // 2, col_count // 2, 4 * width)
    merge_in = layer_norm(grouped.astype(jnp.float32))[0].astype(jnp.bfloat16)
    merged = jnp.dot(
        merge_in.reshape(-1, 4 * width), merge_weight, preferred_element_type=jnp.float32
    ).astype(jnp.bfloat16)
    return merged.reshape(levels, row_count // 2, col_count // 2, -1)


class Sizes:
    def __init__(self, enc, lat, lon, band, block, width):
        self.enc, self.lat, self.lon = enc, lat, lon
        self.band, self.block, self.width = band, block, width
        self.share = enc // lat
        self.rows, self.cols = self.share * band, lat * block
        self.slots = self.share * lat
        self.block_tokens = LEVELS * band * block
        self.block_rows = -(-self.block_tokens // 16) * 16
        self.row_tokens = LEVELS * self.cols
        self.tokens = self.rows * self.row_tokens
        self.half = self.tokens // 2
        self.packed = -(-self.half // 16) * 16
        self.group = lat * lon
        self.chunk = width // self.group
        self.total_rows = self.rows * lat


def block_order(size):
    matrix = np.zeros((size.tokens, size.slots * size.block_rows), np.float32)
    for a in range(size.rows):
        for level in range(LEVELS):
            for b in range(size.cols):
                slot = (a // size.band) * size.lat + b // size.block
                inner = (level * size.band + a % size.band) * size.block + b % size.block
                token = a * size.row_tokens + level * size.cols + b
                matrix[token, slot * size.block_rows + inner] = 1.0
    return matrix


def token_place(size, token):
    row = ((token.astype(F32) + 0.5) * (1.0 / size.row_tokens)).astype(jnp.int32)
    rest = token - row * size.row_tokens
    level = ((rest.astype(F32) + 0.5) * (1.0 / size.cols)).astype(jnp.int32)
    return row, level, rest - level * size.cols


def dot(a, b):
    return jnp.dot(a, b, preferred_element_type=F32)


def dot_tb(a, b):
    return lax.dot_general(a, b, (((1,), (1,)), ((), ())), preferred_element_type=F32)


def dot_ta(a, b):
    return lax.dot_general(a, b, (((0,), (0,)), ((), ())), preferred_element_type=F32)


def pack_pair(values, odd, half):
    top, bottom = values[:half], values[half:]
    left = lax.broadcasted_iota(jnp.int32, top.shape, 1) < HD
    if odd:
        return jnp.where(left, pltpu.roll(top, HD, 1), bottom)
    return jnp.where(left, top, pltpu.roll(bottom, HD, 1))


def layer_kernel(
    size,
    factor,
    lat_shift,
    lon_shift,
    x_ref,
    order_ref,
    wqkv_ref,
    proj_ref,
    cot_ref,
    latent_out,
    weight_out,
    lat_buf,
    normed_ref,
    inv_ref,
    hid_ref,
    halo_f,
    halo,
    halo_left,
    halo_up,
    halo_diag,
    back_f,
    back,
    back_right,
    back_down,
    back_diag,
    msg,
    msg_in,
    grad,
    grad_in,
    multi_send,
    multi_recv,
    halo_send,
    halo_recv,
    back_send,
    back_recv,
    msg_send,
    msg_recv,
    grad_send,
    grad_recv,
):
    enc, lat, lon = lax.axis_index("enc"), lax.axis_index("lat"), lax.axis_index("lon")
    n_enc, n_lat, n_lon, group = size.enc, size.lat, size.lon, size.group
    home = enc // size.share
    tokens, half, packed = size.tokens, size.half, size.packed
    away = home != lat

    barrier = pltpu.get_barrier_semaphore()

    def greet(*device):
        pl.semaphore_signal(barrier, inc=1, device_id=device, device_id_type=MESH)

    def greet_heads(k, carry):
        greet((enc + k) % n_enc, lat, lon)
        return carry

    lax.fori_loop(1, n_enc, greet_heads, 0)
    member = lat * n_lon + lon

    def greet_tiles(k, carry):
        other = (member + k) % group
        greet(enc, other // n_lon, other % n_lon)
        return carry

    lax.fori_loop(1, group, greet_tiles, 0)

    def greet_targets(k, carry):
        greet(k, home, lon)
        return carry

    @pl.when(away)
    def _():
        lax.fori_loop(0, n_enc, greet_targets, 0)

    def greet_sources(k, carry):
        source = lat * size.share + k // (n_lat - 1)
        greet(source, (lat + 1 + k % (n_lat - 1)) % n_lat, lon)
        return carry

    lax.fori_loop(0, size.share * (n_lat - 1), greet_sources, 0)
    expected = n_enc - 1 + group - 1 + size.share * (n_lat - 1)
    pl.semaphore_wait(barrier, jnp.where(away, expected + n_enc, expected))

    slot = (enc % size.share) * n_lat + lat

    def multicast(k, place):
        return pltpu.make_async_remote_copy(
            src_ref=x_ref,
            dst_ref=lat_buf.at[place],
            send_sem=multi_send.at[k],
            recv_sem=multi_recv.at[place],
            device_id=((enc + k) % n_enc, home, lon),
            device_id_type=MESH,
        )

    own_block = pltpu.make_async_copy(x_ref, lat_buf.at[slot], multi_recv.at[slot])

    @pl.when(away)
    def _():
        multicast(0, slot).start()

    @pl.when(jnp.logical_not(away))
    def _():
        own_block.start()

    def send_block(k, carry):
        multicast(k, slot).start()
        return carry

    lax.fori_loop(1, n_enc, send_block, 0)

    halo_f[:, 3 * HD :] = dot_tb(cot_ref[...], proj_ref[...])
    row_shift, col_shift = lat_shift[0], lon_shift[0]

    def rolled_source(token):
        row, level, col = token_place(size, token)
        row, col = row - row_shift, col - col_shift
        row = jnp.where(row < 0, row + size.rows, row)
        col = jnp.where(col < 0, col + size.cols, col)
        return row * size.row_tokens + level * size.cols + col

    square = (tokens, tokens)
    roll_from = rolled_source(lax.broadcasted_iota(jnp.int32, (tokens, 1), 0))
    roll_matrix = jnp.where(
        roll_from == lax.broadcasted_iota(jnp.int32, square, 1), 1.0, 0.0
    ).astype(BF16)
    roll_to = rolled_source(lax.broadcasted_iota(jnp.int32, (1, tokens), 1))
    unroll_matrix = jnp.where(
        roll_to == lax.broadcasted_iota(jnp.int32, square, 0), 1.0, 0.0
    ).astype(BF16)
    row_of, unused, col_of = token_place(size, lax.broadcasted_iota(jnp.int32, (tokens, 1), 0))

    def arrive(k, carry):
        local_slot = jnp.logical_and(k == slot, jnp.logical_not(away))

        @pl.when(local_slot)
        def _():
            own_block.wait()

        @pl.when(jnp.logical_not(local_slot))
        def _():
            multicast(0, k).wait_recv()

        return carry

    lax.fori_loop(0, size.slots, arrive, 0)

    step_rows = tokens // 3
    blocks = lat_buf[...].reshape(size.slots * size.block_rows, size.width)

    def normalise(k, carry):
        rows = pl.ds(pl.multiple_of(k * step_rows, 16), step_rows)
        values = dot(order_ref[rows, :], blocks)
        normed, inverse = layer_norm(values)
        normed_ref[rows, :] = normed
        inv_ref[rows, :] = jnp.broadcast_to(inverse, (step_rows, 128))
        hidden = normed.astype(BF16)
        hid_ref[rows, :] = hidden
        halo_f[rows, : 3 * HD] = dot(hidden, wqkv_ref[...])
        return carry

    lax.fori_loop(0, 3, normalise, 0)
    halo[...] = halo_f[...].astype(BF16)

    next_lat, last_lat = (lat + 1) % n_lat, (lat + n_lat - 1) % n_lat
    next_lon, last_lon = (lon + 1) % n_lon, (lon + n_lon - 1) % n_lon
    upper = tokens - packed

    def exchange(source, target, send, recv, k, *place):
        return pltpu.make_async_remote_copy(
            src_ref=source,
            dst_ref=target,
            send_sem=send.at[k],
            recv_sem=recv.at[k],
            device_id=(enc, *place),
            device_id_type=MESH,
        )

    lower_rows = halo.at[pl.ds(upper, packed)]
    halo_copies = [
        exchange(halo, halo_left, halo_send, halo_recv, 0, lat, next_lon),
        exchange(lower_rows, halo_diag, halo_send, halo_recv, 1, next_lat, next_lon),
        exchange(lower_rows, halo_up, halo_send, halo_recv, 2, next_lat, lon),
    ]
    for copy in halo_copies:
        copy.start()
    for copy in halo_copies:
        copy.wait_recv()

    own_row = row_of < size.rows - row_shift
    own_col = col_of < size.cols - col_shift
    near = jnp.where(own_col, halo[...].astype(F32), halo_left[...].astype(F32))
    far = jnp.where(own_col[upper:], halo_up[...].astype(F32), halo_diag[...].astype(F32))
    spread = jnp.concatenate([near[:upper], jnp.where(own_row[upper:], near[upper:], far)], axis=0)
    rolled = dot(roll_matrix, spread.astype(BF16))

    win = size.half
    score_scale = HD ** (-0.5)
    window_rows = WIN_LAT * size.row_tokens
    for w in range(tokens // window_rows):
        part = rolled[w * win : (w + 1) * win].astype(BF16)
        queries, keys = part[:, :HD], part[:, HD : 2 * HD]
        values, grads = part[:, 2 * HD : 3 * HD], part[:, 3 * HD :]
        first = lat * size.rows + w * WIN_LAT
        row_a = token_place(size, lax.broadcasted_iota(jnp.int32, (win, 1), 0))[0]
        row_b = token_place(size, lax.broadcasted_iota(jnp.int32, (1, win), 1))[0]
        side_a = jnp.where(row_a + first < row_shift, 1, 0)
        side_b = jnp.where(row_b + first < row_shift, 1, 0)
        scores = dot_tb(queries, keys) * score_scale
        weights = jnp.where(side_a == side_b, jnp.exp(scores), 0.0)
        probs = weights / jnp.sum(weights, axis=-1, keepdims=True)
        low = probs.astype(BF16)
        grad_probs = dot_tb(grads, values)
        grad_scores = probs * (
            grad_probs - jnp.sum(grad_probs * probs, axis=-1, keepdims=True)
        )
        grad_low = grad_scores.astype(BF16)
        there = pl.ds(w * win, win)
        back_f[there, :HD] = dot(grad_low, keys) * score_scale
        back_f[there, HD : 2 * HD] = dot_ta(grad_low, queries) * score_scale
        back_f[there, 2 * HD : 3 * HD] = dot_ta(low, grads)
        back_f[there, 3 * HD :] = dot(low, values)
    back[...] = back_f[...].astype(BF16)

    upper_rows = back.at[pl.ds(0, packed)]
    back_copies = [
        exchange(back, back_right, back_send, back_recv, 0, lat, last_lon),
        exchange(upper_rows, back_diag, back_send, back_recv, 1, last_lat, last_lon),
        exchange(upper_rows, back_down, back_send, back_recv, 2, last_lat, lon),
    ]
    for copy in back_copies:
        copy.start()
    for copy in back_copies:
        copy.wait_recv()

    own_row = row_of >= row_shift
    own_col = col_of >= col_shift
    near = jnp.where(own_col, back[...].astype(F32), back_right[...].astype(F32))
    far = jnp.where(own_col[:packed], back_down[...].astype(F32), back_diag[...].astype(F32))
    spread = jnp.concatenate(
        [jnp.where(own_row[:packed], near[:packed], far), near[packed:]], axis=0
    )
    own = dot(unroll_matrix, spread.astype(BF16)).astype(BF16)
    grad_rows, heads_out = own[:, : 3 * HD], own[:, 3 * HD :]

    head_part = dot_tb(grad_rows, wqkv_ref[...])
    ones = jnp.ones((8, size.width), BF16)
    sums = dot_tb(ones, head_part.astype(BF16))
    cross = dot_tb(ones, (head_part * normed_ref[...]).astype(BF16))
    lanes = 4 * 128
    pad = jnp.zeros((8, lanes - tokens), F32)
    sums = jnp.concatenate([sums, pad], axis=1)
    cross = jnp.concatenate([cross, pad], axis=1)
    index = lax.broadcasted_iota(jnp.int32, (8, 128), 0)
    extra = jnp.zeros((8, 128), F32)
    for k in range(4):
        columns = slice(k * 128, (k + 1) * 128)
        extra = jnp.where(index == k, sums[:, columns], extra)
        extra = jnp.where(index == k + 4, cross[:, columns], extra)
    for pair in range(n_enc // 2):
        values = head_part[:, pair * 128 : (pair + 1) * 128]
        for odd in range(2):
            message = pack_pair(values, odd, half)
            msg[2 * pair + odd] = jnp.concatenate([message, extra], axis=0).astype(BF16)

    def head_copy(k, target):
        return pltpu.make_async_remote_copy(
            src_ref=msg.at[target],
            dst_ref=msg_in.at[k],
            send_sem=msg_send.at[k],
            recv_sem=msg_recv.at[k],
            device_id=(target, lat, lon),
            device_id_type=MESH,
        )

    def send_head(k, carry):
        head_copy(k, (enc + k) % n_enc).start()
        return carry

    lax.fori_loop(1, n_enc, send_head, 0)

    grad[:, :, : 3 * HD] = (
        (dot_ta(hid_ref[...], grad_rows) * factor)
        .astype(BF16)
        .reshape(group, size.chunk, 3 * HD)
    )
    grad[:, :, 3 * HD :] = (
        (dot_ta(cot_ref[...], heads_out) * factor).astype(BF16).reshape(group, size.chunk, HD)
    )

    def grad_copy(k, target):
        return pltpu.make_async_remote_copy(
            src_ref=grad.at[target],
            dst_ref=grad_in.at[k],
            send_sem=grad_send.at[k],
            recv_sem=grad_recv.at[k],
            device_id=(enc, target // n_lon, target % n_lon),
            device_id_type=MESH,
        )

    def send_grad(k, carry):
        grad_copy(k, (member + k) % group).start()
        return carry

    lax.fori_loop(1, group, send_grad, 0)

    columns = pl.ds(pl.multiple_of((enc // 2) * 128, 128), 128)
    odd = enc % 2 == 1

    def own_share(values):
        return jnp.where(odd, pack_pair(values, 1, half), pack_pair(values, 0, half))

    def side_by_side(column):
        left = lax.broadcasted_iota(jnp.int32, (half, 128), 1) < HD
        return jnp.where(left, column[:half], column[half:])

    normed_own = own_share(normed_ref[:, columns])
    cot_own = own_share(cot_ref[:, columns].astype(F32))
    inverse_own = side_by_side(inv_ref[...])

    def take_head(k, total):
        head_copy(k, enc).wait_recv()
        return total + msg_in[k].astype(F32)

    total = lax.fori_loop(1, n_enc, take_head, msg[enc].astype(F32))
    token = lax.broadcasted_iota(jnp.int32, (tokens, 1), 0)
    place = lax.broadcasted_iota(jnp.int32, (tokens, 128), 1)
    line = jnp.right_shift(token, 7)
    pick = jnp.where(token - line * 128 == place, 1.0, 0.0)
    means = lax.dot_general(
        pick,
        total[half:packed],
        (((1,), (1,)), ((), ())),
        precision=lax.Precision.HIGHEST,
        preferred_element_type=F32,
    ) * (1.0 / size.width)
    which = lax.broadcasted_iota(jnp.int32, (tokens, 8), 1)
    mean_grad = jnp.sum(jnp.where(which == line, means, 0.0), axis=-1, keepdims=True)
    mean_cross = jnp.sum(jnp.where(which == line + 4, means, 0.0), axis=-1, keepdims=True)
    latent_out[...] = (
        cot_own
        + inverse_own
        * (total[:half] - side_by_side(mean_grad) - normed_own * side_by_side(mean_cross))
    ).astype(BF16)

    def take_grad(k, total):
        grad_copy(k, member).wait_recv()
        return total + grad_in[k].astype(F32)

    weight_out[...] = lax.fori_loop(1, group, take_grad, grad[member].astype(F32))

    @pl.when(away)
    def _():
        multicast(0, slot).wait_send()

    def sent_block(k, carry):
        multicast(k, slot).wait_send()
        return carry

    lax.fori_loop(1, n_enc, sent_block, 0)
    for copy in halo_copies + back_copies:
        copy.wait_send()

    def sent_head(k, carry):
        head_copy(k, (enc + k) % n_enc).wait_send()
        return carry

    lax.fori_loop(1, n_enc, sent_head, 0)

    def sent_grad(k, carry):
        grad_copy(k, (member + k) % group).wait_send()
        return carry

    lax.fori_loop(1, group, sent_grad, 0)


def layer(size, lat_shift, lon_shift, block, wqkv, proj, cot):
    tokens, packed = size.tokens, size.packed
    vmem = pl.BlockSpec(memory_space=pltpu.VMEM)
    smem = pl.BlockSpec(memory_space=pltpu.SMEM)
    factor = (tokens * size.group) ** (-0.5)
    wide = 4 * HD
    dma = pltpu.SemaphoreType.DMA
    return pl.pallas_call(
        functools.partial(layer_kernel, size, factor),
        out_shape=(
            jax.ShapeDtypeStruct((size.half, 128), BF16),
            jax.ShapeDtypeStruct((size.chunk, wide), F32),
        ),
        in_specs=[smem, smem] + [vmem] * 5,
        out_specs=(vmem, vmem),
        scratch_shapes=[
            pltpu.VMEM((size.slots, size.block_rows, size.width), BF16),
            pltpu.VMEM((tokens, size.width), F32),
            pltpu.VMEM((tokens, 128), F32),
            pltpu.VMEM((tokens, size.width), BF16),
            pltpu.VMEM((tokens, wide), F32),
            pltpu.VMEM((tokens, wide), BF16),
            pltpu.VMEM((tokens, wide), BF16),
            pltpu.VMEM((packed, wide), BF16),
            pltpu.VMEM((packed, wide), BF16),
            pltpu.VMEM((tokens, wide), F32),
            pltpu.VMEM((tokens, wide), BF16),
            pltpu.VMEM((tokens, wide), BF16),
            pltpu.VMEM((packed, wide), BF16),
            pltpu.VMEM((packed, wide), BF16),
            pltpu.VMEM((size.enc, packed, 128), BF16),
            pltpu.VMEM((size.enc, packed, 128), BF16),
            pltpu.VMEM((size.group, size.chunk, wide), BF16),
            pltpu.VMEM((size.group, size.chunk, wide), BF16),
            dma((size.enc,)),
            dma((size.slots,)),
            dma((3,)),
            dma((3,)),
            dma((3,)),
            dma((3,)),
            dma((size.enc,)),
            dma((size.enc,)),
            dma((size.group,)),
            dma((size.group,)),
        ],
        compiler_params=pltpu.CompilerParams(
            collective_id=0, has_side_effects=True, vmem_limit_bytes=56 * 1024 * 1024
        ),
    )(lat_shift, lon_shift, block, jnp.asarray(block_order(size), BF16), wqkv, proj, cot)


def layer_part(size, latent_band, lat_shift, lon_shift, qkv_weight, proj_weight, cotangent):
    block = latent_band.reshape(size.block_tokens, size.width)
    block = jnp.pad(block, ((0, size.block_rows - size.block_tokens), (0, 0)))
    cot = cotangent.transpose(1, 0, 2, 3).reshape(size.tokens, size.width)
    packed_latent, weights = layer(
        size, lat_shift, lon_shift, block, qkv_weight, proj_weight, cot
    )
    latent = packed_latent.reshape(size.half, 2, HD).transpose(1, 0, 2)
    latent = latent.reshape(size.rows, LEVELS, size.cols, HD).transpose(1, 0, 2, 3)
    return latent, weights[:, : 3 * HD], weights[:, 3 * HD :].T


def local(
    atmos,
    land_sea,
    level_count,
    atm_weight,
    land_weight,
    level_embed,
    latent_query,
    key_weight,
    value_weight,
    merge_weight,
    lat_shift,
    lon_shift,
    qkv_weight,
    proj_weight,
    cotangent,
):
    fine_band = encode(
        atmos,
        land_sea,
        level_count,
        atm_weight,
        land_weight,
        level_embed,
        latent_query,
        key_weight,
        value_weight,
    )
    latent_band = merge_patches(fine_band, merge_weight)
    unused, band, block, width = latent_band.shape
    size = Sizes(
        lax.axis_size("enc"), lax.axis_size("lat"), lax.axis_size("lon"), band, block, width
    )
    return layer_part(
        size, latent_band, lat_shift, lon_shift, qkv_weight, proj_weight, cotangent
    )


def solution(mesh):
    return jax.shard_map(
        local,
        mesh=mesh,
        in_specs=(
            P("enc", ("lon", "lat"), None, None),
            P("enc", ("lon", "lat"), None),
            P("enc", ("lon", "lat")),
            P(),
            P(),
            P(),
            P(),
            P(),
            P(),
            P(),
            P(),
            P(),
            P(None, "enc"),
            P("enc", None),
            P(None, "lat", "lon", None),
        ),
        out_specs=(
            P(None, "lat", "lon", "enc"),
            P(("lat", "lon"), "enc"),
            P("enc", ("lat", "lon")),
        ),
        check_vma=False,
    )
```

```python
import functools

import jax
import jax.numpy as jnp
import numpy as np
from jax import lax
from jax.experimental import pallas as pl
from jax.experimental.pallas import tpu as pltpu
from jax.sharding import PartitionSpec as P

PHEADS = 16
WIN_LAT = 6
WIN_LON = 12
HD = 64
LEVELS = 3
MESH = pl.DeviceIdType.MESH

epsilon = 1e-05
F32 = jnp.float32
BF16 = jnp.bfloat16


def layer_norm(values):
    centre = jnp.mean(values, axis=-1, keepdims=True)
    centred = values - centre
    variance = jnp.mean(centred * centred, axis=-1, keepdims=True)
    inverse = lax.rsqrt(variance + epsilon)
    return (centred * inverse, inverse)


def encode(
    atmos,
    land_sea,
    level_count,
    atm_weight,
    land_weight,
    level_embed,
    latent_query,
    key_weight,
    value_weight,
):
    row_count, col_count, levels, pixels = atmos.shape
    patches = row_count * col_count
    embedded = jnp.dot(
        atmos.reshape(patches * levels, pixels), atm_weight, preferred_element_type=jnp.float32
    )
    embedded = embedded.reshape(patches, levels, -1)
    static = jnp.dot(
        land_sea.reshape(patches, -1).astype(jnp.bfloat16),
        land_weight,
        preferred_element_type=jnp.float32,
    )
    embedded = embedded + level_embed[None, :, :] + static[:, None, :]
    normed, unused_scale = layer_norm(embedded)
    tokens = normed.astype(jnp.bfloat16).reshape(patches * levels, -1)
    key_rows = jnp.dot(tokens, key_weight, preferred_element_type=jnp.float32).astype(jnp.bfloat16)
    value_rows = jnp.dot(tokens, value_weight, preferred_element_type=jnp.float32).astype(
        jnp.bfloat16
    )
    key_rows = key_rows.reshape(patches, levels, PHEADS, -1)
    value_rows = value_rows.reshape(patches, levels, PHEADS, -1)
    queries = latent_query.reshape(latent_query.shape[0], PHEADS, -1)
    score_scale = key_rows.shape[-1] ** (-0.5)
    scores = (
        jnp.einsum("mhc,plhc->phml", queries, key_rows, preferred_element_type=jnp.float32)
        * score_scale
    )
    present = jnp.arange(levels, dtype=jnp.int32)[None, :] < level_count.reshape(patches, 1)
    weights = jnp.where(present[:, None, None, :], jnp.exp(scores), 0.0)
    level_probs = (weights / jnp.sum(weights, axis=-1, keepdims=True)).astype(jnp.bfloat16)
    attended = jnp.einsum(
        "phml,plhc->pmhc", level_probs, value_rows, preferred_element_type=jnp.float32
    )
    attended = attended.astype(jnp.bfloat16).reshape(row_count, col_count, queries.shape[0], -1)
    return attended.transpose(2, 0, 1, 3)


def merge_patches(fine, merge_weight):
    levels, row_count, col_count, width = fine.shape
    grouped = fine.reshape(levels, row_count // 2, 2, col_count // 2, 2, width).transpose(
        0, 1, 3, 4, 2, 5
    )
    grouped = grouped.reshape(levels, row_count // 2, col_count // 2, 4 * width)
    merge_in = layer_norm(grouped.astype(jnp.float32))[0].astype(jnp.bfloat16)
    merged = jnp.dot(
        merge_in.reshape(-1, 4 * width), merge_weight, preferred_element_type=jnp.float32
    ).astype(jnp.bfloat16)
    return merged.reshape(levels, row_count // 2, col_count // 2, -1)


class Sizes:
    def __init__(self, enc, lat, lon, band, block, width):
        self.enc, self.lat, self.lon = enc, lat, lon
        self.band, self.block, self.width = band, block, width
        self.share = enc // lat
        self.rows, self.cols = self.share * band, lat * block
        self.slots = self.share * lat
        self.block_tokens = LEVELS * band * block
        self.block_rows = -(-self.block_tokens // 16) * 16
        self.row_tokens = LEVELS * self.cols
        self.tokens = self.rows * self.row_tokens
        self.half = self.tokens // 2
        self.packed = -(-self.half // 16) * 16
        self.group = lat * lon
        self.chunk = width // self.group
        self.total_rows = self.rows * lat


def block_order(size):
    matrix = np.zeros((size.tokens, size.slots * size.block_rows), np.float32)
    for a in range(size.rows):
        for level in range(LEVELS):
            for b in range(size.cols):
                slot = (a // size.band) * size.lat + b // size.block
                inner = (level * size.band + a % size.band) * size.block + b % size.block
                token = a * size.row_tokens + level * size.cols + b
                matrix[token, slot * size.block_rows + inner] = 1.0
    return matrix


def token_place(size, token):
    row = ((token.astype(F32) + 0.5) * (1.0 / size.row_tokens)).astype(jnp.int32)
    rest = token - row * size.row_tokens
    level = ((rest.astype(F32) + 0.5) * (1.0 / size.cols)).astype(jnp.int32)
    return row, level, rest - level * size.cols


def dot(a, b):
    return jnp.dot(a, b, preferred_element_type=F32)


def dot_tb(a, b):
    return lax.dot_general(a, b, (((1,), (1,)), ((), ())), preferred_element_type=F32)


def dot_ta(a, b):
    return lax.dot_general(a, b, (((0,), (0,)), ((), ())), preferred_element_type=F32)


def pack_pair(values, odd, half):
    top, bottom = values[:half], values[half:]
    left = lax.broadcasted_iota(jnp.int32, top.shape, 1) < HD
    if odd:
        return jnp.where(left, pltpu.roll(top, HD, 1), bottom)
    return jnp.where(left, top, pltpu.roll(bottom, HD, 1))


def layer_kernel(
    size,
    factor,
    lat_shift,
    lon_shift,
    x_ref,
    order_ref,
    wqkv_ref,
    proj_ref,
    cot_ref,
    latent_out,
    qkv_out,
    proj_out,
    lat_buf,
    normed_ref,
    inv_ref,
    hid_ref,
    halo_f,
    halo,
    halo_left,
    halo_up,
    halo_diag,
    halo_right,
    back_f,
    back,
    back_right,
    back_down,
    back_diag,
    back_left,
    msg,
    msg_in,
    part_out,
    part_in,
    grad,
    grad_in,
    mid,
    mid_in,
    total_out,
    total_in,
    own_send,
    far_send,
    multi_recv,
    halo_send,
    halo_recv,
    back_send,
    back_recv,
    msg_send,
    msg_recv,
    part_send,
    part_recv,
    grad_send,
    grad_recv,
    total_send,
    total_recv,
):
    enc, lat, lon = lax.axis_index("enc"), lax.axis_index("lat"), lax.axis_index("lon")
    n_enc, n_lat, n_lon, group = size.enc, size.lat, size.lon, size.group
    home = enc // size.share
    tokens, half, packed = size.tokens, size.half, size.packed
    away = home != lat

    barrier = pltpu.get_barrier_semaphore()

    def greet(*device):
        pl.semaphore_signal(barrier, inc=1, device_id=device, device_id_type=MESH)

    def greet_heads(k, carry):
        greet((enc + k) % n_enc, lat, lon)
        return carry

    lax.fori_loop(1, n_enc, greet_heads, 0)
    member = lat * n_lon + lon

    def greet_tiles(k, carry):
        other = (member + k) % group
        greet(enc, other // n_lon, other % n_lon)
        return carry

    lax.fori_loop(1, group, greet_tiles, 0)

    def greet_targets(k, carry):
        greet(k, home, lon)
        return carry

    @pl.when(away)
    def _():
        lax.fori_loop(0, n_enc, greet_targets, 0)

    def greet_sources(k, carry):
        source = lat * size.share + k // (n_lat - 1)
        greet(source, (lat + 1 + k % (n_lat - 1)) % n_lat, lon)
        return carry

    lax.fori_loop(0, size.share * (n_lat - 1), greet_sources, 0)
    expected = n_enc - 1 + group - 1 + size.share * (n_lat - 1)
    pl.semaphore_wait(barrier, jnp.where(away, expected + n_enc, expected))

    share = size.share
    place = enc % share
    slot = place * n_lat + lat
    order = (0, 1, 3, 2) if share == 4 else tuple(range(share))
    sides = (1, n_lat - 1) if n_lat > 2 else (1,)
    relay = jnp.logical_not(away)
    if n_lat == 4:
        passes_on = home == (lat + jnp.where(lat % 2 == 0, n_lat - 1, 1)) % n_lat
    else:
        passes_on = None
    opposite = (lat + 2) % n_lat

    def block_copy(source, k, send, target):
        return pltpu.make_async_remote_copy(
            src_ref=source,
            dst_ref=lat_buf.at[k],
            send_sem=send,
            recv_sem=multi_recv.at[k],
            device_id=target,
            device_id_type=MESH,
        )

    own_block = pltpu.make_async_copy(x_ref, lat_buf.at[slot], multi_recv.at[slot])

    def first_copy(step):
        target = (home * share + (place + step) % share, home, lon)
        return block_copy(x_ref, slot, own_send.at[step], target)

    def pass_copy(k, index, group):
        return block_copy(lat_buf.at[k], k, far_send.at[index], (group * share + place, lat, lon))

    @pl.when(relay)
    def _():
        own_block.start()

    @pl.when(away)
    def _():
        first_copy(0).start()

    for step in order[1:]:
        first_copy(step).start()

    halo_f[:, 3 * HD :] = dot_tb(cot_ref[...], proj_ref[...])
    row_shift, col_shift = lat_shift[0], lon_shift[0]
    win = size.half
    win_pad = size.packed

    def number(rows, start=0):
        return start + lax.broadcasted_iota(jnp.int32, (rows, 1), 0)

    def column_of(rows, start=0):
        return token_place(size, number(rows, start))[2]

    def one_hot(index, columns):
        lane = lax.broadcasted_iota(jnp.int32, (index.shape[0], columns), 1)
        return jnp.where(index == lane, 1.0, 0.0).astype(BF16)

    low_rows = -(-(WIN_LAT - 1) * size.row_tokens // 16) * 16
    high_start = (size.rows - WIN_LAT + 1) * size.row_tokens // 16 * 16
    high_rows = tokens - high_start
    mid_start = size.row_tokens // 16 * 16
    mid_rows = -(-(size.rows - 1) * size.row_tokens // 16) * 16 - mid_start

    def rolled_index(start):
        row, level, col = token_place(size, number(win, start))
        row, col = row - row_shift, col - col_shift
        col = jnp.where(col < 0, col + size.cols, col)
        return row, row * size.row_tokens + level * size.cols + col

    first_row, first_index = rolled_index(0)
    take_first = one_hot(
        jnp.where(first_row < 0, first_index + tokens - high_start + low_rows, first_index),
        low_rows + high_rows,
    )
    take_second = one_hot(rolled_index(win)[1] - mid_start, mid_rows)

    row, level, col = token_place(size, number(tokens))
    row, col = row + row_shift, col + col_shift
    col = jnp.where(col >= size.cols, col - size.cols, col)
    inner = level * size.cols + col
    give_index = jnp.where(
        row < WIN_LAT,
        row * size.row_tokens + inner,
        jnp.where(
            row < 2 * WIN_LAT,
            (row - WIN_LAT) * size.row_tokens + inner + win_pad,
            (row - 2 * WIN_LAT) * size.row_tokens + inner + 2 * win_pad,
        ),
    )
    give = one_hot(give_index, 2 * win_pad + low_rows)

    def arrive(step):
        def body(k, carry):
            index = ((place + step) % share) * n_lat + k
            local_slot = jnp.logical_and(index == slot, relay)

            @pl.when(local_slot)
            def _():
                own_block.wait()

            @pl.when(jnp.logical_not(local_slot))
            def _():
                block_copy(x_ref, index, own_send.at[0], (enc, lat, lon)).wait_recv()

            @pl.when(relay)
            def _():
                for at, side in enumerate(sides):
                    pass_copy(index, at * size.slots + index, (lat + side) % n_lat).start()

            if passes_on is not None:

                @pl.when(passes_on)
                def _():
                    pass_copy(index, index, opposite).start()

            return carry

        return body

    for step in order:
        lax.fori_loop(0, n_lat, arrive(step), 0)

    step_rows = tokens // 3
    blocks = lat_buf[...].reshape(size.slots * size.block_rows, size.width)

    def normalise(k, carry):
        rows = pl.ds(pl.multiple_of(k * step_rows, 16), step_rows)
        values = dot(order_ref[rows, :], blocks)
        normed, inverse = layer_norm(values)
        normed_ref[rows, :] = normed
        inv_ref[rows, :] = jnp.broadcast_to(inverse, (step_rows, 128))
        hidden = normed.astype(BF16)
        hid_ref[rows, :] = hidden
        halo_f[rows, : 3 * HD] = dot(hidden, wqkv_ref[...])
        return carry

    lax.fori_loop(0, 3, normalise, 0)
    halo[...] = halo_f[...].astype(BF16)

    next_lat, last_lat = (lat + 1) % n_lat, (lat + n_lat - 1) % n_lat
    next_lon, last_lon = (lon + 1) % n_lon, (lon + n_lon - 1) % n_lon
    def exchange(source, target, send, recv, k, *place):
        return pltpu.make_async_remote_copy(
            src_ref=source,
            dst_ref=target,
            send_sem=send.at[k],
            recv_sem=recv.at[k],
            device_id=(enc, *place),
            device_id_type=MESH,
        )

    low_part = halo.at[pl.ds(0, low_rows)]
    high_part = halo.at[pl.ds(high_start, high_rows)]
    mid_part = halo.at[pl.ds(mid_start, mid_rows)]
    halo_copies = [
        exchange(low_part, halo_left, halo_send, halo_recv, 0, lat, next_lon),
        exchange(high_part, halo_diag, halo_send, halo_recv, 1, next_lat, next_lon),
        exchange(high_part, halo_up, halo_send, halo_recv, 2, next_lat, lon),
        exchange(mid_part, halo_right, halo_send, halo_recv, 3, lat, last_lon),
    ]
    for copy in halo_copies:
        copy.start()
    for copy in halo_copies:
        copy.wait_recv()

    split = size.cols - col_shift

    def choose(condition, one, other):
        return jnp.where(condition, one.astype(F32), other.astype(F32))

    low = choose(column_of(low_rows) < split, halo[:low_rows, :], halo_left[...])
    high = choose(column_of(high_rows, high_start) < split, halo_up[...], halo_diag[...])
    middle = choose(
        column_of(mid_rows, mid_start) < split,
        halo_right[...],
        halo[mid_start : mid_start + mid_rows, :],
    )
    windows = (
        dot(take_first, jnp.concatenate([low, high], axis=0).astype(BF16)),
        dot(take_second, middle.astype(BF16)),
    )

    score_scale = HD ** (-0.5)
    for w in range(2):
        part = windows[w].astype(BF16)
        queries, keys = part[:, :HD], part[:, HD : 2 * HD]
        values, grads = part[:, 2 * HD : 3 * HD], part[:, 3 * HD :]
        first = lat * size.rows + w * WIN_LAT
        row_a = token_place(size, lax.broadcasted_iota(jnp.int32, (win, 1), 0))[0]
        row_b = token_place(size, lax.broadcasted_iota(jnp.int32, (1, win), 1))[0]
        side_a = jnp.where(row_a + first < row_shift, 1, 0)
        side_b = jnp.where(row_b + first < row_shift, 1, 0)
        scores = dot_tb(queries, keys) * score_scale
        weights = jnp.where(side_a == side_b, jnp.exp(scores), 0.0)
        probs = weights / jnp.sum(weights, axis=-1, keepdims=True)
        low = probs.astype(BF16)
        grad_probs = dot_tb(grads, values)
        grad_scores = probs * (
            grad_probs - jnp.sum(grad_probs * probs, axis=-1, keepdims=True)
        )
        grad_low = grad_scores.astype(BF16)
        there = pl.ds(w * win_pad, win)
        back_f[there, :HD] = dot(grad_low, keys) * score_scale
        back_f[there, HD : 2 * HD] = dot_ta(grad_low, queries) * score_scale
        back_f[there, 2 * HD : 3 * HD] = dot_ta(low, grads)
        back_f[there, 3 * HD :] = dot(low, values)
        back_f[pl.ds(w * win_pad + win, win_pad - win), :] = jnp.zeros((win_pad - win, 4 * HD), F32)
    back[...] = back_f[...].astype(BF16)

    far_start = size.row_tokens // 16 * 16
    far_rows = win_pad - far_start
    early_part = back.at[pl.ds(0, low_rows)]
    late_part = back.at[pl.ds(far_start, far_rows)]
    second_part = back.at[pl.ds(win_pad, win_pad)]
    back_copies = [
        exchange(late_part, back_right, back_send, back_recv, 0, lat, last_lon),
        exchange(early_part, back_diag, back_send, back_recv, 1, last_lat, last_lon),
        exchange(early_part, back_down, back_send, back_recv, 2, last_lat, lon),
        exchange(second_part, back_left, back_send, back_recv, 3, lat, next_lon),
    ]
    for copy in back_copies:
        copy.start()
    for copy in back_copies:
        copy.wait_recv()

    here = back[...].astype(F32)
    cover = jnp.concatenate(
        [
            here[:far_start],
            choose(column_of(far_rows, far_start) >= col_shift, here[far_start:win_pad], back_right[...]),
            choose(column_of(win_pad) >= col_shift, back_left[...], here[win_pad:]),
            choose(column_of(low_rows) >= col_shift, back_down[...], back_diag[...]),
        ],
        axis=0,
    )
    own = dot(give, cover.astype(BF16)).astype(BF16)
    grad_rows, heads_out = own[:, : 3 * HD], own[:, 3 * HD :]

    head_part = dot_tb(grad_rows, wqkv_ref[...])
    ones = jnp.ones((8, size.width), BF16)
    sums = dot_tb(ones, head_part.astype(BF16))
    cross = dot_tb(ones, (head_part * normed_ref[...]).astype(BF16))
    lanes = 4 * 128
    pad = jnp.zeros((8, lanes - tokens), F32)
    sums = jnp.concatenate([sums, pad], axis=1)
    cross = jnp.concatenate([cross, pad], axis=1)
    index = lax.broadcasted_iota(jnp.int32, (8, 128), 0)
    extra = jnp.zeros((8, 128), F32)
    for k in range(4):
        columns = slice(k * 128, (k + 1) * 128)
        extra = jnp.where(index == k, sums[:, columns], extra)
        extra = jnp.where(index == k + 4, cross[:, columns], extra)
    for pair in range(n_enc // 2):
        values = head_part[:, pair * 128 : (pair + 1) * 128]
        for odd in range(2):
            message = pack_pair(values, odd, half)
            msg[2 * pair + odd] = jnp.concatenate([message, extra], axis=0).astype(BF16)

    later = tuple((place + step) % share for step in ((2, 1, 3, 0) if share == 4 else (1, 0)))

    def group_copy(k, step):
        target = (home + step) % n_lat
        return pltpu.make_async_remote_copy(
            src_ref=msg.at[target * share + later[k]],
            dst_ref=msg_in.at[k, step],
            send_sem=msg_send.at[k, step],
            recv_sem=msg_recv.at[k, step],
            device_id=(target * share + place, lat, lon),
            device_id_type=MESH,
        )

    group_copies = [
        group_copy(k, step) for k in range(share) for step in ((2, 1, 3) if n_lat == 4 else (1,))
    ]
    for copy in group_copies:
        copy.start()

    grad[:, :, :, : 3 * HD] = (
        (dot_ta(hid_ref[...], grad_rows) * factor)
        .astype(BF16)
        .reshape(n_lat, n_lon, size.chunk, 3 * HD)
    )
    grad[:, :, :, 3 * HD :] = (
        (dot_ta(cot_ref[...], heads_out) * factor)
        .astype(BF16)
        .reshape(n_lat, n_lon, size.chunk, HD)
    )

    pairs = n_lat // 2
    pair, core = lat // 2, lat % 2

    def core_copy(k):
        return pltpu.make_async_remote_copy(
            src_ref=grad.at[((pair + k) % pairs) * 2 + 1 - core],
            dst_ref=grad_in.at[k],
            send_sem=grad_send.at[k],
            recv_sem=grad_recv.at[k],
            device_id=(enc, pair * 2 + 1 - core, lon),
            device_id_type=MESH,
        )

    def pair_copy():
        return pltpu.make_async_remote_copy(
            src_ref=mid,
            dst_ref=mid_in,
            send_sem=grad_send.at[pairs],
            recv_sem=grad_recv.at[pairs],
            device_id=(enc, ((pair + 1) % pairs) * 2 + core, lon),
            device_id_type=MESH,
        )

    def line_copy(step):
        target = (lon + step) % n_lon
        return pltpu.make_async_remote_copy(
            src_ref=total_out.at[target],
            dst_ref=total_in.at[step],
            send_sem=total_send.at[step],
            recv_sem=total_recv.at[step],
            device_id=(enc, lat, target),
            device_id_type=MESH,
        )

    for k in reversed(range(pairs)):
        core_copy(k).start()
    if pairs == 2:
        core_copy(1).wait_recv()
        mid[...] = (grad[(1 - pair) * 2 + core].astype(F32) + grad_in[1].astype(F32)).astype(BF16)
        pair_copy().start()

    columns = pl.ds(pl.multiple_of((enc // 2) * 128, 128), 128)
    odd = enc % 2 == 1

    def own_share(values):
        return jnp.where(odd, pack_pair(values, 1, half), pack_pair(values, 0, half))

    def side_by_side(column):
        left = lax.broadcasted_iota(jnp.int32, (half, 128), 1) < HD
        return jnp.where(left, column[:half], column[half:])

    normed_own = own_share(normed_ref[:, columns])
    cot_own = own_share(cot_ref[:, columns].astype(F32))
    inverse_own = side_by_side(inv_ref[...])

    def part_copy(k):
        return pltpu.make_async_remote_copy(
            src_ref=part_out.at[k],
            dst_ref=part_in.at[k],
            send_sem=part_send.at[k],
            recv_sem=part_recv.at[k],
            device_id=(home * share + later[k], lat, lon),
            device_id_type=MESH,
        )

    def group_sum(k):
        values = msg[home * share + later[k]].astype(F32)
        for step in range(1, n_lat):
            group_copy(k, step).wait_recv()
            values = values + msg_in[k, step].astype(F32)
        return values

    def send_part(k):
        part_out[k] = group_sum(k).astype(BF16)
        part_copy(k).start()

    send_part(0)
    core_copy(0).wait_recv()
    weight_sum = grad[lat].astype(F32) + grad_in[0].astype(F32)
    if pairs == 2:
        pair_copy().wait_recv()
        weight_sum = weight_sum + mid_in[...].astype(F32)
    total_out[...] = weight_sum.astype(BF16)
    far_first = sorted(range(1, n_lon), key=lambda step: -min(step, n_lon - step))
    for step in far_first:
        line_copy(step).start()
    for k in range(1, share - 1):
        send_part(k)
    total = group_sum(share - 1)
    for k in range(share - 1):
        part_copy(k).wait_recv()
        total = total + part_in[k].astype(F32)

    token = lax.broadcasted_iota(jnp.int32, (tokens, 1), 0)
    lane = lax.broadcasted_iota(jnp.int32, (tokens, 128), 1)
    line = jnp.right_shift(token, 7)
    pick = jnp.where(token - line * 128 == lane, 1.0, 0.0)
    means = lax.dot_general(
        pick,
        total[half:packed],
        (((1,), (1,)), ((), ())),
        precision=lax.Precision.HIGHEST,
        preferred_element_type=F32,
    ) * (1.0 / size.width)
    which = lax.broadcasted_iota(jnp.int32, (tokens, 8), 1)
    mean_grad = jnp.sum(jnp.where(which == line, means, 0.0), axis=-1, keepdims=True)
    mean_cross = jnp.sum(jnp.where(which == line + 4, means, 0.0), axis=-1, keepdims=True)
    latent = cot_own + inverse_own * (
        total[:half] - side_by_side(mean_grad) - normed_own * side_by_side(mean_cross)
    )
    other = pltpu.roll(latent, HD, 1)
    lines = size.rows * LEVELS // 2
    for k in range(2 * lines):
        start = (k % lines) * size.cols
        values = (latent, other)[k // lines][start : start + size.cols, :HD]
        latent_out[k % LEVELS, k // LEVELS] = values.astype(BF16)

    weights = total_out[lon].astype(F32)
    for step in reversed(far_first):
        line_copy(step).wait_recv()
        weights = weights + total_in[step].astype(F32)
    qkv_out[...] = weights[:, : 3 * HD]
    proj_out[...] = weights[:, 3 * HD :].T

    @pl.when(away)
    def _():
        first_copy(0).wait_send()

    for step in order[1:]:
        first_copy(step).wait_send()

    def passed(k, carry):
        @pl.when(relay)
        def _():
            for at, side in enumerate(sides):
                pass_copy(k, at * size.slots + k, (lat + side) % n_lat).wait_send()

        if passes_on is not None:

            @pl.when(passes_on)
            def _():
                pass_copy(k, k, opposite).wait_send()

        return carry

    lax.fori_loop(0, size.slots, passed, 0)
    for copy in halo_copies + back_copies + group_copies:
        copy.wait_send()
    for k in range(share - 1):
        part_copy(k).wait_send()
    for k in range(pairs):
        core_copy(k).wait_send()
    if pairs == 2:
        pair_copy().wait_send()
    for step in far_first:
        line_copy(step).wait_send()


def layer(size, lat_shift, lon_shift, block, wqkv, proj, cot):
    tokens, packed = size.tokens, size.packed
    vmem = pl.BlockSpec(memory_space=pltpu.VMEM)
    smem = pl.BlockSpec(memory_space=pltpu.SMEM)
    factor = (tokens * size.group) ** (-0.5)
    wide = 4 * HD
    dma = pltpu.SemaphoreType.DMA
    low = -(-(WIN_LAT - 1) * size.row_tokens // 16) * 16
    high = tokens - (size.rows - WIN_LAT + 1) * size.row_tokens // 16 * 16
    one_row = size.row_tokens // 16 * 16
    middle = -(-(size.rows - 1) * size.row_tokens // 16) * 16 - one_row
    return pl.pallas_call(
        functools.partial(layer_kernel, size, factor),
        out_shape=(
            jax.ShapeDtypeStruct((LEVELS, size.rows, size.cols, HD), BF16),
            jax.ShapeDtypeStruct((size.chunk, 3 * HD), F32),
            jax.ShapeDtypeStruct((HD, size.chunk), F32),
        ),
        in_specs=[smem, smem] + [vmem] * 5,
        out_specs=(vmem, vmem, vmem),
        scratch_shapes=[
            pltpu.VMEM((size.slots, size.block_rows, size.width), BF16),
            pltpu.VMEM((tokens, size.width), F32),
            pltpu.VMEM((tokens, 128), F32),
            pltpu.VMEM((tokens, size.width), BF16),
            pltpu.VMEM((tokens, wide), F32),
            pltpu.VMEM((tokens, wide), BF16),
            pltpu.VMEM((low, wide), BF16),
            pltpu.VMEM((high, wide), BF16),
            pltpu.VMEM((high, wide), BF16),
            pltpu.VMEM((middle, wide), BF16),
            pltpu.VMEM((2 * packed, wide), F32),
            pltpu.VMEM((2 * packed, wide), BF16),
            pltpu.VMEM((packed - one_row, wide), BF16),
            pltpu.VMEM((low, wide), BF16),
            pltpu.VMEM((low, wide), BF16),
            pltpu.VMEM((packed, wide), BF16),
            pltpu.VMEM((size.enc, packed, 128), BF16),
            pltpu.VMEM((size.share, size.lat, packed, 128), BF16),
            pltpu.VMEM((size.share, packed, 128), BF16),
            pltpu.VMEM((size.share, packed, 128), BF16),
            pltpu.VMEM((size.lat, size.lon, size.chunk, wide), BF16),
            pltpu.VMEM((size.lat // 2, size.lon, size.chunk, wide), BF16),
            pltpu.VMEM((size.lon, size.chunk, wide), BF16),
            pltpu.VMEM((size.lon, size.chunk, wide), BF16),
            pltpu.VMEM((size.lon, size.chunk, wide), BF16),
            pltpu.VMEM((size.lon, size.chunk, wide), BF16),
            dma((size.share,)),
            dma((2 * size.slots,)),
            dma((size.slots,)),
            dma((4,)),
            dma((4,)),
            dma((4,)),
            dma((4,)),
            dma((size.share, size.lat)),
            dma((size.share, size.lat)),
            dma((size.share,)),
            dma((size.share,)),
            dma((size.lat,)),
            dma((size.lat,)),
            dma((size.lon,)),
            dma((size.lon,)),
        ],
        compiler_params=pltpu.CompilerParams(
            collective_id=0, has_side_effects=True, vmem_limit_bytes=56 * 1024 * 1024
        ),
    )(lat_shift, lon_shift, block, jnp.asarray(block_order(size), BF16), wqkv, proj, cot)


def layer_part(size, latent_band, lat_shift, lon_shift, qkv_weight, proj_weight, cotangent):
    block = latent_band.reshape(size.block_tokens, size.width)
    block = jnp.pad(block, ((0, size.block_rows - size.block_tokens), (0, 0)))
    cot = cotangent.transpose(1, 0, 2, 3).reshape(size.tokens, size.width)
    return layer(size, lat_shift, lon_shift, block, qkv_weight, proj_weight, cot)


def local(
    atmos,
    land_sea,
    level_count,
    atm_weight,
    land_weight,
    level_embed,
    latent_query,
    key_weight,
    value_weight,
    merge_weight,
    lat_shift,
    lon_shift,
    qkv_weight,
    proj_weight,
    cotangent,
):
    fine_band = encode(
        atmos,
        land_sea,
        level_count,
        atm_weight,
        land_weight,
        level_embed,
        latent_query,
        key_weight,
        value_weight,
    )
    latent_band = merge_patches(fine_band, merge_weight)
    unused, band, block, width = latent_band.shape
    size = Sizes(
        lax.axis_size("enc"), lax.axis_size("lat"), lax.axis_size("lon"), band, block, width
    )
    return layer_part(
        size, latent_band, lat_shift, lon_shift, qkv_weight, proj_weight, cotangent
    )


def solution(mesh):
    return jax.shard_map(
        local,
        mesh=mesh,
        in_specs=(
            P("enc", ("lon", "lat"), None, None),
            P("enc", ("lon", "lat"), None),
            P("enc", ("lon", "lat")),
            P(),
            P(),
            P(),
            P(),
            P(),
            P(),
            P(),
            P(),
            P(),
            P(None, "enc"),
            P("enc", None),
            P(None, "lat", "lon", None),
        ),
        out_specs=(
            P(None, "lat", "lon", "enc"),
            P(("lat", "lon"), "enc"),
            P("enc", ("lat", "lon")),
        ),
        check_vma=False,
    )
```

```python
import functools

import jax
import jax.numpy as jnp
import numpy as np
from jax import lax
from jax.experimental import pallas as pl
from jax.experimental.pallas import tpu as pltpu
from jax.sharding import PartitionSpec as P

PHEADS = 16
WIN_LAT = 6
WIN_LON = 12
HD = 64
LEVELS = 3
LINES = 16
MESH = pl.DeviceIdType.MESH

epsilon = 1e-05
F32 = jnp.float32
BF16 = jnp.bfloat16


def layer_norm(values):
    centre = jnp.mean(values, axis=-1, keepdims=True)
    centred = values - centre
    variance = jnp.mean(centred * centred, axis=-1, keepdims=True)
    inverse = lax.rsqrt(variance + epsilon)
    return (centred * inverse, inverse)


class Sizes:
    def __init__(self, enc, lat, lon, fine_rows, fine_cols, width):
        self.enc, self.lat, self.lon = enc, lat, lon
        band, block = fine_rows // 2, fine_cols // 2
        self.fine_rows, self.fine_cols = fine_rows, fine_cols
        self.patches = fine_rows * fine_cols
        self.patch_rows = -(-self.patches // 8) * 8
        self.fine_total = -(-LEVELS * self.patch_rows // 16) * 16
        self.band, self.block, self.width = band, block, width
        self.share = enc // lat
        self.rows, self.cols = self.share * band, lat * block
        self.slots = self.share * lat
        self.block_tokens = LEVELS * band * block
        self.block_rows = -(-self.block_tokens // 16) * 16
        self.row_tokens = LEVELS * self.cols
        self.tokens = self.rows * self.row_tokens
        self.half = self.tokens // 2
        self.packed = -(-self.half // 16) * 16
        self.group = lat * lon
        self.chunk = width // self.group
        self.total_rows = self.rows * lat


def block_order(size):
    matrix = np.zeros((size.tokens, size.slots * size.block_rows), np.float32)
    for a in range(size.rows):
        for level in range(LEVELS):
            for b in range(size.cols):
                slot = (a // size.band) * size.lat + b // size.block
                inner = (level * size.band + a % size.band) * size.block + b % size.block
                token = a * size.row_tokens + level * size.cols + b
                matrix[token, slot * size.block_rows + inner] = 1.0
    return matrix


def merge_order(size):
    matrix = np.zeros((4 * size.block_rows, size.fine_total), np.float32)
    for quadrant in range(4):
        for level in range(LEVELS):
            for i in range(size.band):
                for j in range(size.block):
                    patch = (2 * i + quadrant % 2) * size.fine_cols + 2 * j + quadrant // 2
                    token = (level * size.band + i) * size.block + j
                    matrix[quadrant * size.block_rows + token, level * size.patch_rows + patch] = 1.0
    return matrix


def token_place(size, token):
    row = ((token.astype(F32) + 0.5) * (1.0 / size.row_tokens)).astype(jnp.int32)
    rest = token - row * size.row_tokens
    level = ((rest.astype(F32) + 0.5) * (1.0 / size.cols)).astype(jnp.int32)
    return row, level, rest - level * size.cols


def dot(a, b):
    return jnp.dot(a, b, preferred_element_type=F32)


def dot_tb(a, b):
    return lax.dot_general(a, b, (((1,), (1,)), ((), ())), preferred_element_type=F32)


def dot_ta(a, b):
    return lax.dot_general(a, b, (((0,), (0,)), ((), ())), preferred_element_type=F32)


def encode_block(
    size,
    atmos_ref,
    land_ref,
    count_ref,
    atm_weight_ref,
    land_weight_ref,
    level_ref,
    query_ref,
    key_ref,
    value_ref,
    select_ref,
    merge_ref,
    merge_ready,
    atm_rows,
    land_rows,
    level_rows,
    fine_rows,
    block_ref,
):
    patches = size.patches
    count, cols = patches * LINES, size.fine_cols
    width = key_ref.shape[0]
    atm_rows[...] = jnp.zeros_like(atm_rows)
    land_rows[...] = jnp.zeros_like(land_rows)
    level_rows[...] = jnp.zeros_like(level_rows)
    fine_rows[...] = jnp.zeros_like(fine_rows)
    for i in range(size.fine_rows):
        land_rows[i * cols : (i + 1) * cols, :] = land_ref[i].astype(F32)
        for j in range(cols):
            atm_rows[i * cols + j, : atmos_ref.shape[2], :] = atmos_ref[i, j]
    level_rows[: level_ref.shape[0], :] = level_ref[...]

    token = lax.broadcasted_iota(jnp.int32, (count, 1), 0)
    patch = jnp.right_shift(token, 4)
    height = token - jnp.left_shift(patch, 4)
    row = ((patch.astype(F32) + 0.5) * (1.0 / cols)).astype(jnp.int32)
    col = patch - row * cols
    spread = jnp.where(
        patch == lax.broadcasted_iota(jnp.int32, (count, size.patch_rows), 1), 1.0, 0.0
    ).astype(BF16)
    in_row = jnp.where(
        row == lax.broadcasted_iota(jnp.int32, (count, size.fine_rows), 1), 1.0, 0.0
    ).astype(BF16)
    counts = dot(in_row, count_ref[...].astype(F32).astype(BF16))
    in_col = col == lax.broadcasted_iota(jnp.int32, (count, cols), 1)
    limit = jnp.sum(jnp.where(in_col, counts, 0.0), axis=-1, keepdims=True)
    present = height.astype(F32) < limit

    land = dot(spread, land_rows[...].astype(BF16)).astype(BF16)
    embedded = dot(atm_rows[...].reshape(count, atm_rows.shape[2]), atm_weight_ref[...])
    embedded = embedded + dot(land, land_weight_ref[...])
    embedded = embedded.reshape(patches, LINES, width) + level_rows[...][None]
    tokens = layer_norm(embedded.reshape(count, width))[0].astype(BF16)
    key_rows = dot(tokens, key_ref[...]).astype(BF16)
    value_rows = dot(tokens, value_ref[...]).astype(BF16).astype(F32)

    head_width = width // PHEADS
    shape = (PHEADS, width)
    lane = lax.broadcasted_iota(jnp.int32, shape, 1)
    first = lax.broadcasted_iota(jnp.int32, shape, 0) * head_width
    in_head = jnp.logical_and(lane >= first, lane < first + head_width)
    queries = query_ref[...].astype(F32)
    queries = jnp.concatenate(
        [
            jnp.where(in_head, jnp.broadcast_to(queries[m : m + 1], shape), 0.0)
            for m in range(LEVELS)
        ],
        axis=0,
    ).astype(BF16)
    scores = dot_tb(key_rows, queries) * head_width ** (-0.5)
    weights = jnp.where(present, jnp.exp(scores), 0.0).reshape(patches, LINES, LEVELS * PHEADS)
    probs = weights / jnp.sum(weights, axis=1, keepdims=True)
    probs = probs.reshape(count, LEVELS * PHEADS).astype(BF16)
    shape = (LEVELS * PHEADS, LEVELS * width)
    lane = lax.broadcasted_iota(jnp.int32, shape, 1)
    first = lax.broadcasted_iota(jnp.int32, shape, 0) * head_width
    widen = jnp.where(
        jnp.logical_and(lane >= first, lane < first + head_width), 1.0, 0.0
    ).astype(BF16)
    for m in range(LEVELS):
        wide = dot(probs, widen[:, m * width : (m + 1) * width])
        attended = jnp.sum((wide * value_rows).reshape(patches, LINES, width), axis=1)
        fine_rows[m * size.patch_rows : m * size.patch_rows + patches, :] = attended

    merged = dot(select_ref[...], fine_rows[...].astype(BF16))
    parts = [merged[q * size.block_rows : (q + 1) * size.block_rows] for q in range(4)]
    centre = sum(jnp.sum(part, axis=-1, keepdims=True) for part in parts) * (0.25 / width)
    parts = [part - centre for part in parts]
    square = sum(jnp.sum(part * part, axis=-1, keepdims=True) for part in parts)
    inverse = lax.rsqrt(square * (0.25 / width) + epsilon)
    merge_ready()
    block = sum(
        dot((part * inverse).astype(BF16), merge_ref[q * width : (q + 1) * width, :])
        for q, part in enumerate(parts)
    )
    block_ref[...] = block.astype(BF16)


def pack_pair(values, odd, half):
    top, bottom = values[:half], values[half:]
    left = lax.broadcasted_iota(jnp.int32, top.shape, 1) < HD
    if odd:
        return jnp.where(left, pltpu.roll(top, HD, 1), bottom)
    return jnp.where(left, top, pltpu.roll(bottom, HD, 1))


def layer_kernel(
    size,
    factor,
    lat_shift,
    lon_shift,
    atmos_ref,
    land_ref,
    count_ref,
    atm_weight_ref,
    land_weight_ref,
    level_ref,
    query_ref,
    key_ref,
    value_ref,
    cot_in,
    select_hbm,
    merge_hbm,
    order_hbm,
    wqkv_hbm,
    proj_hbm,
    latent_out,
    weight_out,
    select_ref,
    merge_ref,
    order_ref,
    wqkv_ref,
    proj_ref,
    cot_ref,
    atm_rows,
    land_rows,
    level_rows,
    fine_rows,
    x_ref,
    lat_buf,
    normed_ref,
    inv_ref,
    hid_ref,
    halo_f,
    halo,
    halo_left,
    halo_up,
    halo_diag,
    halo_right,
    back_f,
    back,
    back_right,
    back_down,
    back_diag,
    back_left,
    msg,
    msg_in,
    part_out,
    part_in,
    grad,
    grad_in,
    mid,
    mid_in,
    total_out,
    total_in,
    load_sem,
    own_send,
    far_send,
    multi_recv,
    halo_send,
    halo_recv,
    back_send,
    back_recv,
    msg_send,
    msg_recv,
    part_send,
    part_recv,
    grad_send,
    grad_recv,
    total_send,
    total_recv,
):
    enc, lat, lon = lax.axis_index("enc"), lax.axis_index("lat"), lax.axis_index("lon")
    n_enc, n_lat, n_lon, group = size.enc, size.lat, size.lon, size.group
    home = enc // size.share
    tokens, half, packed = size.tokens, size.half, size.packed
    away = home != lat

    loads = [
        pltpu.make_async_copy(source, target, load_sem.at[k])
        for k, (source, target) in enumerate(
            (
                (select_hbm, select_ref),
                (merge_hbm, merge_ref),
                (proj_hbm, proj_ref),
                (order_hbm, order_ref),
                (wqkv_hbm, wqkv_ref),
            )
        )
    ]
    for load in loads:
        load.start()
    barrier = pltpu.get_barrier_semaphore()

    def greet(*device):
        pl.semaphore_signal(barrier, inc=1, device_id=device, device_id_type=MESH)

    def greet_heads(k, carry):
        greet((enc + k) % n_enc, lat, lon)
        return carry

    lax.fori_loop(1, n_enc, greet_heads, 0)
    member = lat * n_lon + lon

    def greet_tiles(k, carry):
        other = (member + k) % group
        greet(enc, other // n_lon, other % n_lon)
        return carry

    lax.fori_loop(1, group, greet_tiles, 0)

    def greet_targets(k, carry):
        greet(k, home, lon)
        return carry

    @pl.when(away)
    def _():
        lax.fori_loop(0, n_enc, greet_targets, 0)

    def greet_sources(k, carry):
        source = lat * size.share + k // (n_lat - 1)
        greet(source, (lat + 1 + k % (n_lat - 1)) % n_lat, lon)
        return carry

    lax.fori_loop(0, size.share * (n_lat - 1), greet_sources, 0)

    loads[0].wait()
    encode_block(
        size,
        atmos_ref,
        land_ref,
        count_ref,
        atm_weight_ref,
        land_weight_ref,
        level_ref,
        query_ref,
        key_ref,
        value_ref,
        select_ref,
        merge_ref,
        loads[1].wait,
        atm_rows,
        land_rows,
        level_rows,
        fine_rows,
        x_ref,
    )
    expected = n_enc - 1 + group - 1 + size.share * (n_lat - 1)
    pl.semaphore_wait(barrier, jnp.where(away, expected + n_enc, expected))

    share = size.share
    place = enc % share
    slot = place * n_lat + lat
    order = (0, 1, 3, 2) if share == 4 else tuple(range(share))
    sides = (1, n_lat - 1) if n_lat > 2 else (1,)
    relay = jnp.logical_not(away)
    if n_lat == 4:
        passes_on = home == (lat + jnp.where(lat % 2 == 0, n_lat - 1, 1)) % n_lat
    else:
        passes_on = None
    opposite = (lat + 2) % n_lat

    def block_copy(source, k, send, target):
        return pltpu.make_async_remote_copy(
            src_ref=source,
            dst_ref=lat_buf.at[k],
            send_sem=send,
            recv_sem=multi_recv.at[k],
            device_id=target,
            device_id_type=MESH,
        )

    own_block = pltpu.make_async_copy(x_ref, lat_buf.at[slot], multi_recv.at[slot])

    def first_copy(step):
        target = (home * share + (place + step) % share, home, lon)
        return block_copy(x_ref, slot, own_send.at[step], target)

    def pass_copy(k, index, group):
        return block_copy(lat_buf.at[k], k, far_send.at[index], (group * share + place, lat, lon))

    @pl.when(relay)
    def _():
        own_block.start()

    @pl.when(away)
    def _():
        first_copy(0).start()

    for step in order[1:]:
        first_copy(step).start()

    for load in loads[2:]:
        load.wait()
    for k in range(size.rows * LEVELS):
        rows = pl.ds(k * size.cols, size.cols)
        normed_ref[rows, :] = cot_in[k % LEVELS, k // LEVELS].astype(F32)
    cot_ref[...] = normed_ref[...].astype(BF16)
    halo_f[:, 3 * HD :] = dot_tb(cot_ref[...], proj_ref[...])
    row_shift, col_shift = lat_shift[0], lon_shift[0]
    win = size.half
    win_pad = size.packed

    def number(rows, start=0):
        return start + lax.broadcasted_iota(jnp.int32, (rows, 1), 0)

    def column_of(rows, start=0):
        return token_place(size, number(rows, start))[2]

    def one_hot(index, columns):
        lane = lax.broadcasted_iota(jnp.int32, (index.shape[0], columns), 1)
        return jnp.where(index == lane, 1.0, 0.0).astype(BF16)

    low_rows = -(-(WIN_LAT - 1) * size.row_tokens // 16) * 16
    high_start = (size.rows - WIN_LAT + 1) * size.row_tokens // 16 * 16
    high_rows = tokens - high_start
    mid_start = size.row_tokens // 16 * 16
    mid_rows = -(-(size.rows - 1) * size.row_tokens // 16) * 16 - mid_start

    def rolled_index(start):
        row, level, col = token_place(size, number(win, start))
        row, col = row - row_shift, col - col_shift
        col = jnp.where(col < 0, col + size.cols, col)
        return row, row * size.row_tokens + level * size.cols + col

    first_row, first_index = rolled_index(0)
    take_first = one_hot(
        jnp.where(first_row < 0, first_index + tokens - high_start + low_rows, first_index),
        low_rows + high_rows,
    )
    take_second = one_hot(rolled_index(win)[1] - mid_start, mid_rows)

    row, level, col = token_place(size, number(tokens))
    row, col = row + row_shift, col + col_shift
    col = jnp.where(col >= size.cols, col - size.cols, col)
    inner = level * size.cols + col
    give_index = jnp.where(
        row < WIN_LAT,
        row * size.row_tokens + inner,
        jnp.where(
            row < 2 * WIN_LAT,
            (row - WIN_LAT) * size.row_tokens + inner + win_pad,
            (row - 2 * WIN_LAT) * size.row_tokens + inner + 2 * win_pad,
        ),
    )
    give = one_hot(give_index, 2 * win_pad + low_rows)

    def arrive(step):
        def body(k, carry):
            index = ((place + step) % share) * n_lat + k
            local_slot = jnp.logical_and(index == slot, relay)

            @pl.when(local_slot)
            def _():
                own_block.wait()

            @pl.when(jnp.logical_not(local_slot))
            def _():
                block_copy(x_ref, index, own_send.at[0], (enc, lat, lon)).wait_recv()

            @pl.when(relay)
            def _():
                for at, side in enumerate(sides):
                    pass_copy(index, at * size.slots + index, (lat + side) % n_lat).start()

            if passes_on is not None:

                @pl.when(passes_on)
                def _():
                    pass_copy(index, index, opposite).start()

            return carry

        return body

    for step in order:
        lax.fori_loop(0, n_lat, arrive(step), 0)

    step_rows = tokens // 3
    blocks = lat_buf[...].reshape(size.slots * size.block_rows, size.width)

    def normalise(k, carry):
        rows = pl.ds(pl.multiple_of(k * step_rows, 16), step_rows)
        values = dot(order_ref[rows, :], blocks)
        normed, inverse = layer_norm(values)
        normed_ref[rows, :] = normed
        inv_ref[rows, :] = jnp.broadcast_to(inverse, (step_rows, 128))
        hidden = normed.astype(BF16)
        hid_ref[rows, :] = hidden
        halo_f[rows, : 3 * HD] = dot_tb(hidden, wqkv_ref[...])
        return carry

    lax.fori_loop(0, 3, normalise, 0)
    halo[...] = halo_f[...].astype(BF16)

    next_lat, last_lat = (lat + 1) % n_lat, (lat + n_lat - 1) % n_lat
    next_lon, last_lon = (lon + 1) % n_lon, (lon + n_lon - 1) % n_lon
    def exchange(source, target, send, recv, k, *place):
        return pltpu.make_async_remote_copy(
            src_ref=source,
            dst_ref=target,
            send_sem=send.at[k],
            recv_sem=recv.at[k],
            device_id=(enc, *place),
            device_id_type=MESH,
        )

    low_part = halo.at[pl.ds(0, low_rows)]
    high_part = halo.at[pl.ds(high_start, high_rows)]
    mid_part = halo.at[pl.ds(mid_start, mid_rows)]
    halo_copies = [
        exchange(low_part, halo_left, halo_send, halo_recv, 0, lat, next_lon),
        exchange(high_part, halo_diag, halo_send, halo_recv, 1, next_lat, next_lon),
        exchange(high_part, halo_up, halo_send, halo_recv, 2, next_lat, lon),
        exchange(mid_part, halo_right, halo_send, halo_recv, 3, lat, last_lon),
    ]
    for copy in halo_copies:
        copy.start()
    for copy in halo_copies:
        copy.wait_recv()

    split = size.cols - col_shift

    def choose(condition, one, other):
        return jnp.where(condition, one.astype(F32), other.astype(F32))

    low = choose(column_of(low_rows) < split, halo[:low_rows, :], halo_left[...])
    high = choose(column_of(high_rows, high_start) < split, halo_up[...], halo_diag[...])
    middle = choose(
        column_of(mid_rows, mid_start) < split,
        halo_right[...],
        halo[mid_start : mid_start + mid_rows, :],
    )
    windows = (
        dot(take_first, jnp.concatenate([low, high], axis=0).astype(BF16)),
        dot(take_second, middle.astype(BF16)),
    )

    score_scale = HD ** (-0.5)
    for w in range(2):
        part = windows[w].astype(BF16)
        queries, keys = part[:, :HD], part[:, HD : 2 * HD]
        values, grads = part[:, 2 * HD : 3 * HD], part[:, 3 * HD :]
        first = lat * size.rows + w * WIN_LAT
        row_a = token_place(size, lax.broadcasted_iota(jnp.int32, (win, 1), 0))[0]
        row_b = token_place(size, lax.broadcasted_iota(jnp.int32, (1, win), 1))[0]
        side_a = jnp.where(row_a + first < row_shift, 1, 0)
        side_b = jnp.where(row_b + first < row_shift, 1, 0)
        scores = dot_tb(queries, keys) * score_scale
        weights = jnp.where(side_a == side_b, jnp.exp(scores), 0.0)
        probs = weights / jnp.sum(weights, axis=-1, keepdims=True)
        low = probs.astype(BF16)
        grad_probs = dot_tb(grads, values)
        grad_scores = probs * (
            grad_probs - jnp.sum(grad_probs * probs, axis=-1, keepdims=True)
        )
        grad_low = grad_scores.astype(BF16)
        there = pl.ds(w * win_pad, win)
        back_f[there, :HD] = dot(grad_low, keys) * score_scale
        back_f[there, HD : 2 * HD] = dot_ta(grad_low, queries) * score_scale
        back_f[there, 2 * HD : 3 * HD] = dot_ta(low, grads)
        back_f[there, 3 * HD :] = dot(low, values)
        back_f[pl.ds(w * win_pad + win, win_pad - win), :] = jnp.zeros((win_pad - win, 4 * HD), F32)
    back[...] = back_f[...].astype(BF16)

    far_start = size.row_tokens // 16 * 16
    far_rows = win_pad - far_start
    early_part = back.at[pl.ds(0, low_rows)]
    late_part = back.at[pl.ds(far_start, far_rows)]
    second_part = back.at[pl.ds(win_pad, win_pad)]
    back_copies = [
        exchange(late_part, back_right, back_send, back_recv, 0, lat, last_lon),
        exchange(early_part, back_diag, back_send, back_recv, 1, last_lat, last_lon),
        exchange(early_part, back_down, back_send, back_recv, 2, last_lat, lon),
        exchange(second_part, back_left, back_send, back_recv, 3, lat, next_lon),
    ]
    for copy in back_copies:
        copy.start()
    for copy in back_copies:
        copy.wait_recv()

    here = back[...].astype(F32)
    cover = jnp.concatenate(
        [
            here[:far_start],
            choose(column_of(far_rows, far_start) >= col_shift, here[far_start:win_pad], back_right[...]),
            choose(column_of(win_pad) >= col_shift, back_left[...], here[win_pad:]),
            choose(column_of(low_rows) >= col_shift, back_down[...], back_diag[...]),
        ],
        axis=0,
    )
    own = dot(give, cover.astype(BF16)).astype(BF16)
    grad_rows, heads_out = own[:, : 3 * HD], own[:, 3 * HD :]

    head_part = dot(grad_rows, wqkv_ref[...])
    ones = jnp.ones((8, size.width), BF16)
    sums = dot_tb(ones, head_part.astype(BF16))
    cross = dot_tb(ones, (head_part * normed_ref[...]).astype(BF16))
    lanes = 4 * 128
    pad = jnp.zeros((8, lanes - tokens), F32)
    sums = jnp.concatenate([sums, pad], axis=1)
    cross = jnp.concatenate([cross, pad], axis=1)
    index = lax.broadcasted_iota(jnp.int32, (8, 128), 0)
    extra = jnp.zeros((8, 128), F32)
    for k in range(4):
        columns = slice(k * 128, (k + 1) * 128)
        extra = jnp.where(index == k, sums[:, columns], extra)
        extra = jnp.where(index == k + 4, cross[:, columns], extra)
    for pair in range(n_enc // 2):
        values = head_part[:, pair * 128 : (pair + 1) * 128]
        for odd in range(2):
            message = pack_pair(values, odd, half)
            msg[2 * pair + odd] = jnp.concatenate([message, extra], axis=0).astype(BF16)

    later = tuple((place + step) % share for step in ((2, 1, 3, 0) if share == 4 else (1, 0)))

    def group_copy(k, step):
        target = (home + step) % n_lat
        return pltpu.make_async_remote_copy(
            src_ref=msg.at[target * share + later[k]],
            dst_ref=msg_in.at[k, step],
            send_sem=msg_send.at[k, step],
            recv_sem=msg_recv.at[k, step],
            device_id=(target * share + place, lat, lon),
            device_id_type=MESH,
        )

    group_copies = [
        group_copy(k, step) for k in range(share) for step in ((2, 1, 3) if n_lat == 4 else (1,))
    ]
    for copy in group_copies:
        copy.start()

    grad[:, :, :, : 3 * HD] = (
        (dot_ta(hid_ref[...], grad_rows) * factor)
        .astype(BF16)
        .reshape(n_lat, n_lon, size.chunk, 3 * HD)
    )
    grad[:, :, :, 3 * HD :] = (
        (dot_ta(cot_ref[...], heads_out) * factor)
        .astype(BF16)
        .reshape(n_lat, n_lon, size.chunk, HD)
    )

    pairs = n_lat // 2
    pair, core = lat // 2, lat % 2

    def core_copy(k):
        return pltpu.make_async_remote_copy(
            src_ref=grad.at[((pair + k) % pairs) * 2 + 1 - core],
            dst_ref=grad_in.at[k],
            send_sem=grad_send.at[k],
            recv_sem=grad_recv.at[k],
            device_id=(enc, pair * 2 + 1 - core, lon),
            device_id_type=MESH,
        )

    def pair_copy():
        return pltpu.make_async_remote_copy(
            src_ref=mid,
            dst_ref=mid_in,
            send_sem=grad_send.at[pairs],
            recv_sem=grad_recv.at[pairs],
            device_id=(enc, ((pair + 1) % pairs) * 2 + core, lon),
            device_id_type=MESH,
        )

    def line_copy(step):
        target = (lon + step) % n_lon
        return pltpu.make_async_remote_copy(
            src_ref=total_out.at[target],
            dst_ref=total_in.at[step],
            send_sem=total_send.at[step],
            recv_sem=total_recv.at[step],
            device_id=(enc, lat, target),
            device_id_type=MESH,
        )

    for k in reversed(range(pairs)):
        core_copy(k).start()
    if pairs == 2:
        core_copy(1).wait_recv()
        mid[...] = (grad[(1 - pair) * 2 + core].astype(F32) + grad_in[1].astype(F32)).astype(BF16)
        pair_copy().start()

    columns = pl.ds(pl.multiple_of((enc // 2) * 128, 128), 128)
    odd = enc % 2 == 1

    def own_share(values):
        return jnp.where(odd, pack_pair(values, 1, half), pack_pair(values, 0, half))

    def side_by_side(column):
        left = lax.broadcasted_iota(jnp.int32, (half, 128), 1) < HD
        return jnp.where(left, column[:half], column[half:])

    normed_own = own_share(normed_ref[:, columns])
    cot_own = own_share(cot_ref[:, columns].astype(F32))
    inverse_own = side_by_side(inv_ref[...])

    def part_copy(k):
        return pltpu.make_async_remote_copy(
            src_ref=part_out.at[k],
            dst_ref=part_in.at[k],
            send_sem=part_send.at[k],
            recv_sem=part_recv.at[k],
            device_id=(home * share + later[k], lat, lon),
            device_id_type=MESH,
        )

    def group_sum(k):
        values = msg[home * share + later[k]].astype(F32)
        for step in range(1, n_lat):
            group_copy(k, step).wait_recv()
            values = values + msg_in[k, step].astype(F32)
        return values

    def send_part(k):
        part_out[k] = group_sum(k).astype(BF16)
        part_copy(k).start()

    send_part(0)
    core_copy(0).wait_recv()
    weight_sum = grad[lat].astype(F32) + grad_in[0].astype(F32)
    if pairs == 2:
        pair_copy().wait_recv()
        weight_sum = weight_sum + mid_in[...].astype(F32)
    total_out[...] = weight_sum.astype(BF16)
    far_first = sorted(range(1, n_lon), key=lambda step: -min(step, n_lon - step))
    for step in far_first:
        line_copy(step).start()
    for k in range(1, share - 1):
        send_part(k)
    total = group_sum(share - 1)
    for k in range(share - 1):
        part_copy(k).wait_recv()
        total = total + part_in[k].astype(F32)

    token = lax.broadcasted_iota(jnp.int32, (tokens, 1), 0)
    lane = lax.broadcasted_iota(jnp.int32, (tokens, 128), 1)
    line = jnp.right_shift(token, 7)
    pick = jnp.where(token - line * 128 == lane, 1.0, 0.0)
    means = lax.dot_general(
        pick,
        total[half:packed],
        (((1,), (1,)), ((), ())),
        precision=lax.Precision.HIGHEST,
        preferred_element_type=F32,
    ) * (1.0 / size.width)
    which = lax.broadcasted_iota(jnp.int32, (tokens, 8), 1)
    mean_grad = jnp.sum(jnp.where(which == line, means, 0.0), axis=-1, keepdims=True)
    mean_cross = jnp.sum(jnp.where(which == line + 4, means, 0.0), axis=-1, keepdims=True)
    latent_out[...] = cot_own + inverse_own * (
        total[:half] - side_by_side(mean_grad) - normed_own * side_by_side(mean_cross)
    )

    weights = total_out[lon].astype(F32)
    for step in reversed(far_first):
        line_copy(step).wait_recv()
        weights = weights + total_in[step].astype(F32)
    weight_out[...] = weights

    @pl.when(away)
    def _():
        first_copy(0).wait_send()

    for step in order[1:]:
        first_copy(step).wait_send()

    def passed(k, carry):
        @pl.when(relay)
        def _():
            for at, side in enumerate(sides):
                pass_copy(k, at * size.slots + k, (lat + side) % n_lat).wait_send()

        if passes_on is not None:

            @pl.when(passes_on)
            def _():
                pass_copy(k, k, opposite).wait_send()

        return carry

    lax.fori_loop(0, size.slots, passed, 0)
    for copy in halo_copies + back_copies + group_copies:
        copy.wait_send()
    for k in range(share - 1):
        part_copy(k).wait_send()
    for k in range(pairs):
        core_copy(k).wait_send()
    if pairs == 2:
        pair_copy().wait_send()
    for step in far_first:
        line_copy(step).wait_send()


def finish_kernel(size, packed_ref, weight_ref, latent_out, qkv_out, proj_out):
    latent = packed_ref[...]
    other = pltpu.roll(latent, HD, 1)
    lines = size.rows * LEVELS // 2
    for k in range(2 * lines):
        start = (k % lines) * size.cols
        values = (latent, other)[k // lines][start : start + size.cols, :HD]
        latent_out[k % LEVELS, k // LEVELS] = values.astype(BF16)
    qkv_out[...] = weight_ref[:, : 3 * HD]
    proj_out[...] = weight_ref[:, 3 * HD :]


def finish(size, packed, weights):
    vmem = pl.BlockSpec(memory_space=pltpu.VMEM)
    return pl.pallas_call(
        functools.partial(finish_kernel, size),
        out_shape=(
            jax.ShapeDtypeStruct((LEVELS, size.rows, size.cols, HD), BF16),
            jax.ShapeDtypeStruct((size.chunk, 3 * HD), F32),
            jax.ShapeDtypeStruct((size.chunk, HD), F32),
        ),
        in_specs=[vmem, vmem],
        out_specs=(vmem, vmem, vmem),
    )(packed, weights)


def layer(size, lat_shift, lon_shift, arrays, merge, wqkv, proj):
    tokens, packed = size.tokens, size.packed
    atmos, land, key = arrays[0], arrays[1], arrays[7]
    vmem = pl.BlockSpec(memory_space=pltpu.VMEM)
    smem = pl.BlockSpec(memory_space=pltpu.SMEM)
    factor = (tokens * size.group) ** (-0.5)
    wide = 4 * HD
    dma = pltpu.SemaphoreType.DMA
    low = -(-(WIN_LAT - 1) * size.row_tokens // 16) * 16
    high = tokens - (size.rows - WIN_LAT + 1) * size.row_tokens // 16 * 16
    one_row = size.row_tokens // 16 * 16
    middle = -(-(size.rows - 1) * size.row_tokens // 16) * 16 - one_row
    return pl.pallas_call(
        functools.partial(layer_kernel, size, factor),
        out_shape=(
            jax.ShapeDtypeStruct((size.half, 128), F32),
            jax.ShapeDtypeStruct((size.chunk, wide), F32),
        ),
        in_specs=[smem, smem] + [vmem] * len(arrays) + [pl.BlockSpec(memory_space=pl.ANY)] * 5,
        out_specs=(vmem, vmem),
        scratch_shapes=[
            pltpu.VMEM((4 * size.block_rows, size.fine_total), BF16),
            pltpu.VMEM(merge.shape, BF16),
            pltpu.VMEM((tokens, size.slots * size.block_rows), BF16),
            pltpu.VMEM(wqkv.shape, BF16),
            pltpu.VMEM(proj.shape, BF16),
            pltpu.VMEM((tokens, size.width), BF16),
            pltpu.VMEM((size.patches, LINES, atmos.shape[3]), BF16),
            pltpu.VMEM((size.patch_rows, land.shape[2]), F32),
            pltpu.VMEM((LINES, key.shape[0]), F32),
            pltpu.VMEM((size.fine_total, key.shape[0]), F32),
            pltpu.VMEM((size.block_rows, size.width), BF16),
            pltpu.VMEM((size.slots, size.block_rows, size.width), BF16),
            pltpu.VMEM((tokens, size.width), F32),
            pltpu.VMEM((tokens, 128), F32),
            pltpu.VMEM((tokens, size.width), BF16),
            pltpu.VMEM((tokens, wide), F32),
            pltpu.VMEM((tokens, wide), BF16),
            pltpu.VMEM((low, wide), BF16),
            pltpu.VMEM((high, wide), BF16),
            pltpu.VMEM((high, wide), BF16),
            pltpu.VMEM((middle, wide), BF16),
            pltpu.VMEM((2 * packed, wide), F32),
            pltpu.VMEM((2 * packed, wide), BF16),
            pltpu.VMEM((packed - one_row, wide), BF16),
            pltpu.VMEM((low, wide), BF16),
            pltpu.VMEM((low, wide), BF16),
            pltpu.VMEM((packed, wide), BF16),
            pltpu.VMEM((size.enc, packed, 128), BF16),
            pltpu.VMEM((size.share, size.lat, packed, 128), BF16),
            pltpu.VMEM((size.share, packed, 128), BF16),
            pltpu.VMEM((size.share, packed, 128), BF16),
            pltpu.VMEM((size.lat, size.lon, size.chunk, wide), BF16),
            pltpu.VMEM((size.lat // 2, size.lon, size.chunk, wide), BF16),
            pltpu.VMEM((size.lon, size.chunk, wide), BF16),
            pltpu.VMEM((size.lon, size.chunk, wide), BF16),
            pltpu.VMEM((size.lon, size.chunk, wide), BF16),
            pltpu.VMEM((size.lon, size.chunk, wide), BF16),
            dma((5,)),
            dma((size.share,)),
            dma((2 * size.slots,)),
            dma((size.slots,)),
            dma((4,)),
            dma((4,)),
            dma((4,)),
            dma((4,)),
            dma((size.share, size.lat)),
            dma((size.share, size.lat)),
            dma((size.share,)),
            dma((size.share,)),
            dma((size.lat,)),
            dma((size.lat,)),
            dma((size.lon,)),
            dma((size.lon,)),
        ],
        compiler_params=pltpu.CompilerParams(
            collective_id=0, has_side_effects=True, vmem_limit_bytes=56 * 1024 * 1024
        ),
    )(
        lat_shift,
        lon_shift,
        *arrays,
        jnp.asarray(merge_order(size), BF16),
        merge,
        jnp.asarray(block_order(size), BF16),
        wqkv,
        proj,
    )


def local(
    atmos,
    land_sea,
    level_count,
    atm_weight,
    land_weight,
    level_embed,
    latent_query,
    key_weight,
    value_weight,
    merge_weight,
    lat_shift,
    lon_shift,
    qkv_weight,
    proj_weight,
    cotangent,
):
    size = Sizes(
        lax.axis_size("enc"),
        lax.axis_size("lat"),
        lax.axis_size("lon"),
        atmos.shape[0],
        atmos.shape[1],
        merge_weight.shape[1],
    )
    arrays = (
        atmos,
        land_sea,
        level_count,
        atm_weight,
        land_weight,
        level_embed,
        latent_query,
        key_weight,
        value_weight,
        cotangent,
    )
    packed, weights = layer(
        size, lat_shift, lon_shift, arrays, merge_weight, qkv_weight.T, proj_weight
    )
    latent, grad_qkv, grad_proj = finish(size, packed, weights)
    return latent, grad_qkv, grad_proj.T


def solution(mesh):
    return jax.shard_map(
        local,
        mesh=mesh,
        in_specs=(
            P("enc", ("lon", "lat"), None, None),
            P("enc", ("lon", "lat"), None),
            P("enc", ("lon", "lat")),
            P(),
            P(),
            P(),
            P(),
            P(),
            P(),
            P(),
            P(),
            P(),
            P(None, "enc"),
            P("enc", None),
            P(None, "lat", "lon", None),
        ),
        out_specs=(
            P(None, "lat", "lon", "enc"),
            P(("lat", "lon"), "enc"),
            P("enc", ("lat", "lon")),
        ),
        check_vma=False,
    )
```

```python
import functools

import jax
import jax.numpy as jnp
import numpy as np
from jax import lax
from jax.experimental import pallas as pl
from jax.experimental.pallas import tpu as pltpu
from jax.sharding import PartitionSpec as P

PHEADS = 16
WIN_LAT = 6
WIN_LON = 12
HD = 64
LEVELS = 3
LINES = 16
MESH = pl.DeviceIdType.MESH

epsilon = 1e-05
F32 = jnp.float32
BF16 = jnp.bfloat16


def layer_norm(values):
    centre = jnp.mean(values, axis=-1, keepdims=True)
    centred = values - centre
    variance = jnp.mean(centred * centred, axis=-1, keepdims=True)
    inverse = lax.rsqrt(variance + epsilon)
    return (centred * inverse, inverse)


class Sizes:
    def __init__(self, enc, lat, lon, fine_rows, fine_cols, width):
        self.enc, self.lat, self.lon = enc, lat, lon
        band, block = fine_rows // 2, fine_cols // 2
        self.fine_rows, self.fine_cols = fine_rows, fine_cols
        self.patches = fine_rows * fine_cols
        self.patch_rows = -(-self.patches // 8) * 8
        self.fine_total = -(-LEVELS * self.patch_rows // 16) * 16
        self.band, self.block, self.width = band, block, width
        self.share = enc // lat
        self.rows, self.cols = self.share * band, lat * block
        self.slots = self.share * lat
        self.block_tokens = LEVELS * band * block
        self.block_rows = -(-self.block_tokens // 16) * 16
        self.row_tokens = LEVELS * self.cols
        self.tokens = self.rows * self.row_tokens
        self.half = self.tokens // 2
        self.packed = -(-self.half // 16) * 16
        self.group = lat * lon
        self.chunk = width // self.group
        self.total_rows = self.rows * lat


def block_order(size):
    matrix = np.zeros((size.tokens, size.slots * size.block_rows), np.float32)
    for a in range(size.rows):
        for level in range(LEVELS):
            for b in range(size.cols):
                slot = (a // size.band) * size.lat + b // size.block
                inner = (level * size.band + a % size.band) * size.block + b % size.block
                token = a * size.row_tokens + level * size.cols + b
                matrix[token, slot * size.block_rows + inner] = 1.0
    return matrix


def merge_order(size):
    matrix = np.zeros((4 * size.block_rows, size.fine_total), np.float32)
    for quadrant in range(4):
        for level in range(LEVELS):
            for i in range(size.band):
                for j in range(size.block):
                    patch = (2 * i + quadrant % 2) * size.fine_cols + 2 * j + quadrant // 2
                    token = (level * size.band + i) * size.block + j
                    matrix[quadrant * size.block_rows + token, level * size.patch_rows + patch] = 1.0
    return matrix


def token_place(size, token):
    row = ((token.astype(F32) + 0.5) * (1.0 / size.row_tokens)).astype(jnp.int32)
    rest = token - row * size.row_tokens
    level = ((rest.astype(F32) + 0.5) * (1.0 / size.cols)).astype(jnp.int32)
    return row, level, rest - level * size.cols


def dot(a, b):
    return jnp.dot(a, b, preferred_element_type=F32)


def dot_tb(a, b):
    return lax.dot_general(a, b, (((1,), (1,)), ((), ())), preferred_element_type=F32)


def dot_ta(a, b):
    return lax.dot_general(a, b, (((0,), (0,)), ((), ())), preferred_element_type=F32)


def encode_block(
    size,
    atmos_ref,
    land_ref,
    count_ref,
    atm_weight_ref,
    land_weight_ref,
    level_ref,
    query_ref,
    key_ref,
    value_ref,
    select_ref,
    merge_ref,
    loads,
    atm_rows,
    land_rows,
    level_rows,
    fine_rows,
    block_ref,
):
    patches = size.patches
    count, cols = patches * LINES, size.fine_cols
    width = key_ref.shape[0]
    atm_rows[...] = jnp.zeros_like(atm_rows)
    land_rows[...] = jnp.zeros_like(land_rows)
    level_rows[...] = jnp.zeros_like(level_rows)
    fine_rows[...] = jnp.zeros_like(fine_rows)
    for i in range(size.fine_rows):
        land_rows[i * cols : (i + 1) * cols, :] = land_ref[i].astype(F32)
        for j in range(cols):
            atm_rows[i * cols + j, : atmos_ref.shape[2], :] = atmos_ref[i, j]
    level_rows[: level_ref.shape[0], :] = level_ref[...]

    token = lax.broadcasted_iota(jnp.int32, (count, 1), 0)
    patch = jnp.right_shift(token, 4)
    height = token - jnp.left_shift(patch, 4)
    row = ((patch.astype(F32) + 0.5) * (1.0 / cols)).astype(jnp.int32)
    col = patch - row * cols
    spread = jnp.where(
        patch == lax.broadcasted_iota(jnp.int32, (count, size.patch_rows), 1), 1.0, 0.0
    ).astype(BF16)
    in_row = jnp.where(
        row == lax.broadcasted_iota(jnp.int32, (count, size.fine_rows), 1), 1.0, 0.0
    ).astype(BF16)
    counts = dot(in_row, count_ref[...].astype(F32).astype(BF16))
    in_col = col == lax.broadcasted_iota(jnp.int32, (count, cols), 1)
    limit = jnp.sum(jnp.where(in_col, counts, 0.0), axis=-1, keepdims=True)
    present = height.astype(F32) < limit

    land = dot(spread, land_rows[...].astype(BF16)).astype(BF16)
    embedded = dot(atm_rows[...].reshape(count, atm_rows.shape[2]), atm_weight_ref[...])
    embedded = embedded + dot(land, land_weight_ref[...])
    embedded = embedded.reshape(patches, LINES, width) + level_rows[...][None]
    tokens = layer_norm(embedded.reshape(count, width))[0].astype(BF16)
    loads[0].wait()
    loads[1].wait()
    key_rows = dot(tokens, key_ref[...]).astype(BF16)
    value_rows = dot(tokens, value_ref[...]).astype(BF16).astype(F32)

    head_width = width // PHEADS
    shape = (PHEADS, width)
    lane = lax.broadcasted_iota(jnp.int32, shape, 1)
    first = lax.broadcasted_iota(jnp.int32, shape, 0) * head_width
    in_head = jnp.logical_and(lane >= first, lane < first + head_width)
    queries = query_ref[...].astype(F32)
    queries = jnp.concatenate(
        [
            jnp.where(in_head, jnp.broadcast_to(queries[m : m + 1], shape), 0.0)
            for m in range(LEVELS)
        ],
        axis=0,
    ).astype(BF16)
    scores = dot_tb(key_rows, queries) * head_width ** (-0.5)
    weights = jnp.where(present, jnp.exp(scores), 0.0).reshape(patches, LINES, LEVELS * PHEADS)
    probs = weights / jnp.sum(weights, axis=1, keepdims=True)
    probs = probs.reshape(count, LEVELS * PHEADS).astype(BF16)
    shape = (LEVELS * PHEADS, LEVELS * width)
    lane = lax.broadcasted_iota(jnp.int32, shape, 1)
    first = lax.broadcasted_iota(jnp.int32, shape, 0) * head_width
    widen = jnp.where(
        jnp.logical_and(lane >= first, lane < first + head_width), 1.0, 0.0
    ).astype(BF16)
    for m in range(LEVELS):
        wide = dot(probs, widen[:, m * width : (m + 1) * width])
        attended = jnp.sum((wide * value_rows).reshape(patches, LINES, width), axis=1)
        fine_rows[m * size.patch_rows : m * size.patch_rows + patches, :] = attended

    loads[2].wait()
    merged = dot(select_ref[...], fine_rows[...].astype(BF16))
    parts = [merged[q * size.block_rows : (q + 1) * size.block_rows] for q in range(4)]
    centre = sum(jnp.sum(part, axis=-1, keepdims=True) for part in parts) * (0.25 / width)
    parts = [part - centre for part in parts]
    square = sum(jnp.sum(part * part, axis=-1, keepdims=True) for part in parts)
    inverse = lax.rsqrt(square * (0.25 / width) + epsilon)
    loads[3].wait()
    block = sum(
        dot((part * inverse).astype(BF16), merge_ref[q * width : (q + 1) * width, :])
        for q, part in enumerate(parts)
    )
    block_ref[...] = block.astype(BF16)


def pack_pair(values, odd, half):
    top, bottom = values[:half], values[half:]
    left = lax.broadcasted_iota(jnp.int32, top.shape, 1) < HD
    if odd:
        return jnp.where(left, pltpu.roll(top, HD, 1), bottom)
    return jnp.where(left, top, pltpu.roll(bottom, HD, 1))


def layer_kernel(
    size,
    factor,
    lat_shift,
    lon_shift,
    atmos_ref,
    land_ref,
    count_ref,
    atm_weight_ref,
    land_weight_ref,
    level_ref,
    query_ref,
    cot_in,
    select_hbm,
    key_hbm,
    value_hbm,
    merge_hbm,
    order_hbm,
    wqkv_hbm,
    proj_hbm,
    latent_out,
    weight_out,
    select_ref,
    key_ref,
    value_ref,
    merge_ref,
    order_ref,
    wqkv_ref,
    proj_ref,
    cot_ref,
    atm_rows,
    land_rows,
    level_rows,
    fine_rows,
    x_ref,
    lat_buf,
    normed_ref,
    inv_ref,
    hid_ref,
    blocks_qkv,
    products,
    halo_f,
    halo,
    halo_left,
    halo_up,
    halo_diag,
    halo_right,
    back_f,
    back,
    back_right,
    back_down,
    back_diag,
    back_left,
    msg,
    msg_in,
    part_out,
    part_in,
    grad,
    grad_in,
    mid,
    mid_in,
    total_out,
    total_in,
    load_sem,
    own_send,
    far_send,
    multi_recv,
    halo_send,
    halo_recv,
    back_send,
    back_recv,
    msg_send,
    msg_recv,
    part_send,
    part_recv,
    grad_send,
    grad_recv,
    total_send,
    total_recv,
):
    enc, lat, lon = lax.axis_index("enc"), lax.axis_index("lat"), lax.axis_index("lon")
    n_enc, n_lat, n_lon, group = size.enc, size.lat, size.lon, size.group
    home = enc // size.share
    tokens, half, packed = size.tokens, size.half, size.packed
    away = home != lat

    loads = [
        pltpu.make_async_copy(source, target, load_sem.at[k])
        for k, (source, target) in enumerate(
            (
                (key_hbm, key_ref),
                (value_hbm, value_ref),
                (select_hbm, select_ref),
                (merge_hbm, merge_ref),
                (proj_hbm, proj_ref),
                (order_hbm, order_ref),
                (wqkv_hbm, wqkv_ref),
            )
        )
    ]
    for load in loads:
        load.start()
    barrier = pltpu.get_barrier_semaphore()

    def greet(*device):
        pl.semaphore_signal(barrier, inc=1, device_id=device, device_id_type=MESH)

    def greet_heads(k, carry):
        greet((enc + k) % n_enc, lat, lon)
        return carry

    lax.fori_loop(1, n_enc, greet_heads, 0)
    member = lat * n_lon + lon

    def greet_tiles(k, carry):
        other = (member + k) % group
        greet(enc, other // n_lon, other % n_lon)
        return carry

    lax.fori_loop(1, group, greet_tiles, 0)

    def greet_targets(k, carry):
        greet(k, home, lon)
        return carry

    @pl.when(away)
    def _():
        lax.fori_loop(0, n_enc, greet_targets, 0)

    def greet_sources(k, carry):
        source = lat * size.share + k // (n_lat - 1)
        greet(source, (lat + 1 + k % (n_lat - 1)) % n_lat, lon)
        return carry

    lax.fori_loop(0, size.share * (n_lat - 1), greet_sources, 0)

    encode_block(
        size,
        atmos_ref,
        land_ref,
        count_ref,
        atm_weight_ref,
        land_weight_ref,
        level_ref,
        query_ref,
        key_ref,
        value_ref,
        select_ref,
        merge_ref,
        loads,
        atm_rows,
        land_rows,
        level_rows,
        fine_rows,
        x_ref,
    )
    expected = n_enc - 1 + group - 1 + size.share * (n_lat - 1)
    pl.semaphore_wait(barrier, jnp.where(away, expected + n_enc, expected))

    share = size.share
    place = enc % share
    slot = place * n_lat + lat
    order = (0, 1, 3, 2) if share == 4 else tuple(range(share))
    sides = (1, n_lat - 1) if n_lat > 2 else (1,)
    relay = jnp.logical_not(away)
    if n_lat == 4:
        passes_on = home == (lat + jnp.where(lat % 2 == 0, n_lat - 1, 1)) % n_lat
    else:
        passes_on = None
    opposite = (lat + 2) % n_lat

    def block_copy(source, k, send, target):
        return pltpu.make_async_remote_copy(
            src_ref=source,
            dst_ref=lat_buf.at[k],
            send_sem=send,
            recv_sem=multi_recv.at[k],
            device_id=target,
            device_id_type=MESH,
        )

    own_block = pltpu.make_async_copy(x_ref, lat_buf.at[slot], multi_recv.at[slot])

    def first_copy(step):
        target = (home * share + (place + step) % share, home, lon)
        return block_copy(x_ref, slot, own_send.at[step], target)

    def pass_copy(k, index, group):
        return block_copy(lat_buf.at[k], k, far_send.at[index], (group * share + place, lat, lon))

    @pl.when(relay)
    def _():
        own_block.start()

    @pl.when(away)
    def _():
        first_copy(0).start()

    for step in order[1:]:
        first_copy(step).start()

    for load in loads[4:]:
        load.wait()
    for k in range(size.rows * LEVELS):
        rows = pl.ds(k * size.cols, size.cols)
        normed_ref[rows, :] = cot_in[k % LEVELS, k // LEVELS].astype(F32)
    cot_ref[...] = normed_ref[...].astype(BF16)
    halo_f[:, 3 * HD :] = dot_tb(cot_ref[...], proj_ref[...])
    row_shift, col_shift = lat_shift[0], lon_shift[0]
    win = size.half
    win_pad = size.packed

    def number(rows, start=0):
        return start + lax.broadcasted_iota(jnp.int32, (rows, 1), 0)

    def column_of(rows, start=0):
        return token_place(size, number(rows, start))[2]

    def one_hot(index, columns):
        lane = lax.broadcasted_iota(jnp.int32, (index.shape[0], columns), 1)
        return jnp.where(index == lane, 1.0, 0.0).astype(BF16)

    low_rows = -(-(WIN_LAT - 1) * size.row_tokens // 16) * 16
    high_start = (size.rows - WIN_LAT + 1) * size.row_tokens // 16 * 16
    high_rows = tokens - high_start
    mid_start = size.row_tokens // 16 * 16
    mid_rows = -(-(size.rows - 1) * size.row_tokens // 16) * 16 - mid_start

    def rolled_index(start):
        row, level, col = token_place(size, number(win, start))
        row, col = row - row_shift, col - col_shift
        col = jnp.where(col < 0, col + size.cols, col)
        return row, row * size.row_tokens + level * size.cols + col

    first_row, first_index = rolled_index(0)
    take_first = one_hot(
        jnp.where(first_row < 0, first_index + tokens - high_start + low_rows, first_index),
        low_rows + high_rows,
    )
    take_second = one_hot(rolled_index(win)[1] - mid_start, mid_rows)

    row, level, col = token_place(size, number(tokens))
    row, col = row + row_shift, col + col_shift
    col = jnp.where(col >= size.cols, col - size.cols, col)
    inner = level * size.cols + col
    give_index = jnp.where(
        row < WIN_LAT,
        row * size.row_tokens + inner,
        jnp.where(
            row < 2 * WIN_LAT,
            (row - WIN_LAT) * size.row_tokens + inner + win_pad,
            (row - 2 * WIN_LAT) * size.row_tokens + inner + 2 * win_pad,
        ),
    )
    give = one_hot(give_index, 2 * win_pad + low_rows)

    def arrive(step):
        def body(k, carry):
            index = ((place + step) % share) * n_lat + k
            local_slot = jnp.logical_and(index == slot, relay)

            @pl.when(local_slot)
            def _():
                own_block.wait()

            @pl.when(jnp.logical_not(local_slot))
            def _():
                block_copy(x_ref, index, own_send.at[0], (enc, lat, lon)).wait_recv()

            @pl.when(relay)
            def _():
                for at, side in enumerate(sides):
                    pass_copy(index, at * size.slots + index, (lat + side) % n_lat).start()

            if passes_on is not None:

                @pl.when(passes_on)
                def _():
                    pass_copy(index, index, opposite).start()

            return carry

        return body

    band_rows = n_lat * size.block_rows
    for step in order:
        lax.fori_loop(0, n_lat, arrive(step), 0)
        band = (place + step) % share
        values = lat_buf[pl.ds(band * n_lat, n_lat)].reshape(band_rows, size.width)
        hidden = layer_norm(values.astype(F32))[0].astype(BF16)
        rows = pl.ds(pl.multiple_of(band * band_rows, 16), band_rows)
        blocks_qkv[rows, :] = dot_tb(hidden, wqkv_ref[...]).astype(BF16)
    halo_f[:, : 3 * HD] = dot(order_ref[...], blocks_qkv[...])
    halo[...] = halo_f[...].astype(BF16)


    next_lat, last_lat = (lat + 1) % n_lat, (lat + n_lat - 1) % n_lat
    next_lon, last_lon = (lon + 1) % n_lon, (lon + n_lon - 1) % n_lon
    def exchange(source, target, send, recv, k, *place):
        return pltpu.make_async_remote_copy(
            src_ref=source,
            dst_ref=target,
            send_sem=send.at[k],
            recv_sem=recv.at[k],
            device_id=(enc, *place),
            device_id_type=MESH,
        )

    low_part = halo.at[pl.ds(0, low_rows)]
    high_part = halo.at[pl.ds(high_start, high_rows)]
    mid_part = halo.at[pl.ds(mid_start, mid_rows)]
    halo_copies = [
        exchange(low_part, halo_left, halo_send, halo_recv, 0, lat, next_lon),
        exchange(high_part, halo_diag, halo_send, halo_recv, 1, next_lat, next_lon),
        exchange(high_part, halo_up, halo_send, halo_recv, 2, next_lat, lon),
        exchange(mid_part, halo_right, halo_send, halo_recv, 3, lat, last_lon),
    ]
    for copy in halo_copies:
        copy.start()

    step_rows = tokens // 3
    blocks = lat_buf[...].reshape(size.slots * size.block_rows, size.width)

    def normalise(k, carry):
        rows = pl.ds(pl.multiple_of(k * step_rows, 16), step_rows)
        normed, inverse = layer_norm(dot(order_ref[rows, :], blocks))
        normed_ref[rows, :] = normed
        inv_ref[rows, :] = jnp.broadcast_to(inverse, (step_rows, 128))
        hidden = normed.astype(BF16)
        hid_ref[rows, :] = hidden
        products[rows, :] = dot_tb(hidden, wqkv_ref[...])
        return carry

    lax.fori_loop(0, 3, normalise, 0)
    ones = jnp.ones((8, size.width), BF16)
    weight_sums = dot_tb(ones, wqkv_ref[...])
    coarse = weight_sums.astype(BF16)
    finer = (weight_sums - coarse.astype(F32)).astype(BF16)
    index = lax.broadcasted_iota(jnp.int32, weight_sums.shape, 0)
    weight_sums = jnp.where(
        index == 0, coarse.astype(F32), jnp.where(index == 1, finer.astype(F32), 0.0)
    ).astype(BF16)

    for copy in halo_copies:
        copy.wait_recv()

    split = size.cols - col_shift

    def choose(condition, one, other):
        return jnp.where(condition, one.astype(F32), other.astype(F32))

    low = choose(column_of(low_rows) < split, halo[:low_rows, :], halo_left[...])
    high = choose(column_of(high_rows, high_start) < split, halo_up[...], halo_diag[...])
    middle = choose(
        column_of(mid_rows, mid_start) < split,
        halo_right[...],
        halo[mid_start : mid_start + mid_rows, :],
    )
    score_scale = HD ** (-0.5)

    def window(w, tokens_in, take):
        part = dot(take, tokens_in.astype(BF16)).astype(BF16)
        queries, keys = part[:, :HD], part[:, HD : 2 * HD]
        values, grads = part[:, 2 * HD : 3 * HD], part[:, 3 * HD :]
        first = lat * size.rows + w * WIN_LAT
        row_a = token_place(size, lax.broadcasted_iota(jnp.int32, (win, 1), 0))[0]
        row_b = token_place(size, lax.broadcasted_iota(jnp.int32, (1, win), 1))[0]
        side_a = jnp.where(row_a + first < row_shift, 1, 0)
        side_b = jnp.where(row_b + first < row_shift, 1, 0)
        scores = dot_tb(queries, keys) * score_scale
        weights = jnp.where(side_a == side_b, jnp.exp(scores), 0.0)
        probs = weights / jnp.sum(weights, axis=-1, keepdims=True)
        low = probs.astype(BF16)
        grad_probs = dot_tb(grads, values)
        grad_scores = probs * (
            grad_probs - jnp.sum(grad_probs * probs, axis=-1, keepdims=True)
        )
        grad_low = grad_scores.astype(BF16)
        there = pl.ds(w * win_pad, win)
        back_f[there, :HD] = dot(grad_low, keys) * score_scale
        back_f[there, HD : 2 * HD] = dot_ta(grad_low, queries) * score_scale
        back_f[there, 2 * HD : 3 * HD] = dot_ta(low, grads)
        back_f[there, 3 * HD :] = dot(low, values)
        back_f[pl.ds(w * win_pad + win, win_pad - win), :] = jnp.zeros((win_pad - win, 4 * HD), F32)
        whole = pl.ds(w * win_pad, win_pad)
        back[whole, :] = back_f[whole, :].astype(BF16)

    far_start = size.row_tokens // 16 * 16
    far_rows = win_pad - far_start
    early_part = back.at[pl.ds(0, low_rows)]
    late_part = back.at[pl.ds(far_start, far_rows)]
    second_part = back.at[pl.ds(win_pad, win_pad)]
    back_copies = [
        exchange(late_part, back_right, back_send, back_recv, 0, lat, last_lon),
        exchange(early_part, back_diag, back_send, back_recv, 1, last_lat, last_lon),
        exchange(early_part, back_down, back_send, back_recv, 2, last_lat, lon),
        exchange(second_part, back_left, back_send, back_recv, 3, lat, next_lon),
    ]
    window(0, jnp.concatenate([low, high], axis=0), take_first)
    for copy in back_copies[:3]:
        copy.start()
    window(1, middle, take_second)
    back_copies[3].start()
    for copy in back_copies:
        copy.wait_recv()

    here = back[...].astype(F32)
    cover = jnp.concatenate(
        [
            here[:far_start],
            choose(column_of(far_rows, far_start) >= col_shift, here[far_start:win_pad], back_right[...]),
            choose(column_of(win_pad) >= col_shift, back_left[...], here[win_pad:]),
            choose(column_of(low_rows) >= col_shift, back_down[...], back_diag[...]),
        ],
        axis=0,
    )
    own = dot(give, cover.astype(BF16)).astype(BF16)
    grad_rows, heads_out = own[:, : 3 * HD], own[:, 3 * HD :]

    sums = dot_tb(weight_sums, grad_rows)
    sums = sums + pltpu.roll(sums, 7, 0)
    cross = dot_tb(
        jnp.ones((8, 3 * HD), BF16), (grad_rows.astype(F32) * products[...]).astype(BF16)
    )
    lanes = 4 * 128
    pad = jnp.zeros((8, lanes - tokens), F32)
    sums = jnp.concatenate([sums, pad], axis=1)
    cross = jnp.concatenate([cross, pad], axis=1)
    index = lax.broadcasted_iota(jnp.int32, (8, 128), 0)
    extra = jnp.zeros((8, 128), F32)
    for k in range(4):
        columns = slice(k * 128, (k + 1) * 128)
        extra = jnp.where(index == k, jnp.broadcast_to(sums[:1, columns], (8, 128)), extra)
        extra = jnp.where(index == k + 4, cross[:, columns], extra)
    later = tuple((place + step) % share for step in ((2, 1, 3, 0) if share == 4 else (1, 0)))

    def group_copy(k, step):
        target = (home + step) % n_lat
        return pltpu.make_async_remote_copy(
            src_ref=msg.at[target * share + later[k]],
            dst_ref=msg_in.at[k, step],
            send_sem=msg_send.at[k, step],
            recv_sem=msg_recv.at[k, step],
            device_id=(target * share + place, lat, lon),
            device_id_type=MESH,
        )

    group_copies = []
    group_width = share * HD
    for step in (2, 1, 3, 0) if n_lat == 4 else (1, 0):
        target = (home + step) % n_lat
        columns = pl.ds(pl.multiple_of(target * group_width, 128), group_width)
        head_part = dot(grad_rows, wqkv_ref[:, columns])
        for k in range(share):
            values = head_part[:, k // 2 * 128 : (k // 2 + 1) * 128]
            message = pack_pair(values, k % 2, half)
            msg[target * share + k] = jnp.concatenate([message, extra], axis=0).astype(BF16)
        if step > 0:
            for k in range(share):
                group_copies.append(group_copy(k, step))
                group_copies[-1].start()

    grad[:, :, :, : 3 * HD] = (
        (dot_ta(hid_ref[...], grad_rows) * factor)
        .astype(BF16)
        .reshape(n_lat, n_lon, size.chunk, 3 * HD)
    )
    grad[:, :, :, 3 * HD :] = (
        (dot_ta(cot_ref[...], heads_out) * factor)
        .astype(BF16)
        .reshape(n_lat, n_lon, size.chunk, HD)
    )

    pairs = n_lat // 2
    pair, core = lat // 2, lat % 2

    def core_copy(k):
        return pltpu.make_async_remote_copy(
            src_ref=grad.at[((pair + k) % pairs) * 2 + 1 - core],
            dst_ref=grad_in.at[k],
            send_sem=grad_send.at[k],
            recv_sem=grad_recv.at[k],
            device_id=(enc, pair * 2 + 1 - core, lon),
            device_id_type=MESH,
        )

    def pair_copy():
        return pltpu.make_async_remote_copy(
            src_ref=mid,
            dst_ref=mid_in,
            send_sem=grad_send.at[pairs],
            recv_sem=grad_recv.at[pairs],
            device_id=(enc, ((pair + 1) % pairs) * 2 + core, lon),
            device_id_type=MESH,
        )

    def line_copy(step):
        target = (lon + step) % n_lon
        return pltpu.make_async_remote_copy(
            src_ref=total_out.at[target],
            dst_ref=total_in.at[step],
            send_sem=total_send.at[step],
            recv_sem=total_recv.at[step],
            device_id=(enc, lat, target),
            device_id_type=MESH,
        )

    for k in reversed(range(pairs)):
        core_copy(k).start()
    if pairs == 2:
        core_copy(1).wait_recv()
        mid[...] = (grad[(1 - pair) * 2 + core].astype(F32) + grad_in[1].astype(F32)).astype(BF16)
        pair_copy().start()

    columns = pl.ds(pl.multiple_of((enc // 2) * 128, 128), 128)
    odd = enc % 2 == 1

    def own_share(values):
        return jnp.where(odd, pack_pair(values, 1, half), pack_pair(values, 0, half))

    def side_by_side(column):
        left = lax.broadcasted_iota(jnp.int32, (half, 128), 1) < HD
        return jnp.where(left, column[:half], column[half:])

    normed_own = own_share(normed_ref[:, columns])
    cot_own = own_share(cot_ref[:, columns].astype(F32))
    inverse_own = side_by_side(inv_ref[...])

    def part_copy(k):
        return pltpu.make_async_remote_copy(
            src_ref=part_out.at[k],
            dst_ref=part_in.at[k],
            send_sem=part_send.at[k],
            recv_sem=part_recv.at[k],
            device_id=(home * share + later[k], lat, lon),
            device_id_type=MESH,
        )

    def group_sum(k):
        values = msg[home * share + later[k]].astype(F32)
        for step in range(1, n_lat):
            group_copy(k, step).wait_recv()
            values = values + msg_in[k, step].astype(F32)
        return values

    def send_part(k):
        part_out[k] = group_sum(k).astype(BF16)
        part_copy(k).start()

    send_part(0)
    core_copy(0).wait_recv()
    weight_sum = grad[lat].astype(F32) + grad_in[0].astype(F32)
    if pairs == 2:
        pair_copy().wait_recv()
        weight_sum = weight_sum + mid_in[...].astype(F32)
    total_out[...] = weight_sum.astype(BF16)
    far_first = sorted(range(1, n_lon), key=lambda step: -min(step, n_lon - step))
    for step in far_first:
        line_copy(step).start()
    for k in range(1, share - 1):
        send_part(k)
    total = group_sum(share - 1)
    for k in range(share - 1):
        part_copy(k).wait_recv()
        total = total + part_in[k].astype(F32)

    token = lax.broadcasted_iota(jnp.int32, (tokens, 1), 0)
    lane = lax.broadcasted_iota(jnp.int32, (tokens, 128), 1)
    line = jnp.right_shift(token, 7)
    pick = jnp.where(token - line * 128 == lane, 1.0, 0.0)
    means = lax.dot_general(
        pick,
        total[half:packed],
        (((1,), (1,)), ((), ())),
        precision=lax.Precision.HIGHEST,
        preferred_element_type=F32,
    ) * (1.0 / size.width)
    which = lax.broadcasted_iota(jnp.int32, (tokens, 8), 1)
    mean_grad = jnp.sum(jnp.where(which == line, means, 0.0), axis=-1, keepdims=True)
    mean_cross = jnp.sum(jnp.where(which == line + 4, means, 0.0), axis=-1, keepdims=True)
    latent_out[...] = cot_own + inverse_own * (
        total[:half] - side_by_side(mean_grad) - normed_own * side_by_side(mean_cross)
    )

    weights = total_out[lon].astype(F32)
    for step in reversed(far_first):
        line_copy(step).wait_recv()
        weights = weights + total_in[step].astype(F32)
    weight_out[...] = weights

    @pl.when(away)
    def _():
        first_copy(0).wait_send()

    for step in order[1:]:
        first_copy(step).wait_send()

    def passed(k, carry):
        @pl.when(relay)
        def _():
            for at, side in enumerate(sides):
                pass_copy(k, at * size.slots + k, (lat + side) % n_lat).wait_send()

        if passes_on is not None:

            @pl.when(passes_on)
            def _():
                pass_copy(k, k, opposite).wait_send()

        return carry

    lax.fori_loop(0, size.slots, passed, 0)
    for copy in halo_copies + back_copies + group_copies:
        copy.wait_send()
    for k in range(share - 1):
        part_copy(k).wait_send()
    for k in range(pairs):
        core_copy(k).wait_send()
    if pairs == 2:
        pair_copy().wait_send()
    for step in far_first:
        line_copy(step).wait_send()


def finish_kernel(size, packed_ref, weight_ref, latent_out, qkv_out, proj_out):
    latent = packed_ref[...]
    other = pltpu.roll(latent, HD, 1)
    lines = size.rows * LEVELS // 2
    for k in range(2 * lines):
        start = (k % lines) * size.cols
        values = (latent, other)[k // lines][start : start + size.cols, :HD]
        latent_out[k % LEVELS, k // LEVELS] = values.astype(BF16)
    qkv_out[...] = weight_ref[:, : 3 * HD]
    proj_out[...] = weight_ref[:, 3 * HD :]


def finish(size, packed, weights):
    vmem = pl.BlockSpec(memory_space=pltpu.VMEM)
    return pl.pallas_call(
        functools.partial(finish_kernel, size),
        out_shape=(
            jax.ShapeDtypeStruct((LEVELS, size.rows, size.cols, HD), BF16),
            jax.ShapeDtypeStruct((size.chunk, 3 * HD), F32),
            jax.ShapeDtypeStruct((size.chunk, HD), F32),
        ),
        in_specs=[vmem, vmem],
        out_specs=(vmem, vmem, vmem),
    )(packed, weights)


def layer(size, lat_shift, lon_shift, arrays, key, value, merge, wqkv, proj):
    tokens, packed = size.tokens, size.packed
    atmos, land = arrays[0], arrays[1]
    vmem = pl.BlockSpec(memory_space=pltpu.VMEM)
    smem = pl.BlockSpec(memory_space=pltpu.SMEM)
    factor = (tokens * size.group) ** (-0.5)
    wide = 4 * HD
    dma = pltpu.SemaphoreType.DMA
    low = -(-(WIN_LAT - 1) * size.row_tokens // 16) * 16
    high = tokens - (size.rows - WIN_LAT + 1) * size.row_tokens // 16 * 16
    one_row = size.row_tokens // 16 * 16
    middle = -(-(size.rows - 1) * size.row_tokens // 16) * 16 - one_row
    return pl.pallas_call(
        functools.partial(layer_kernel, size, factor),
        out_shape=(
            jax.ShapeDtypeStruct((size.half, 128), F32),
            jax.ShapeDtypeStruct((size.chunk, wide), F32),
        ),
        in_specs=[smem, smem] + [vmem] * len(arrays) + [pl.BlockSpec(memory_space=pl.ANY)] * 7,
        out_specs=(vmem, vmem),
        scratch_shapes=[
            pltpu.VMEM((4 * size.block_rows, size.fine_total), BF16),
            pltpu.VMEM(key.shape, BF16),
            pltpu.VMEM(key.shape, BF16),
            pltpu.VMEM(merge.shape, BF16),
            pltpu.VMEM((tokens, size.slots * size.block_rows), BF16),
            pltpu.VMEM(wqkv.shape, BF16),
            pltpu.VMEM(proj.shape, BF16),
            pltpu.VMEM((tokens, size.width), BF16),
            pltpu.VMEM((size.patches, LINES, atmos.shape[3]), BF16),
            pltpu.VMEM((size.patch_rows, land.shape[2]), F32),
            pltpu.VMEM((LINES, key.shape[0]), F32),
            pltpu.VMEM((size.fine_total, key.shape[0]), F32),
            pltpu.VMEM((size.block_rows, size.width), BF16),
            pltpu.VMEM((size.slots, size.block_rows, size.width), BF16),
            pltpu.VMEM((tokens, size.width), F32),
            pltpu.VMEM((tokens, 128), F32),
            pltpu.VMEM((tokens, size.width), BF16),
            pltpu.VMEM((size.slots * size.block_rows, 3 * HD), BF16),
            pltpu.VMEM((tokens, 3 * HD), F32),
            pltpu.VMEM((tokens, wide), F32),
            pltpu.VMEM((tokens, wide), BF16),
            pltpu.VMEM((low, wide), BF16),
            pltpu.VMEM((high, wide), BF16),
            pltpu.VMEM((high, wide), BF16),
            pltpu.VMEM((middle, wide), BF16),
            pltpu.VMEM((2 * packed, wide), F32),
            pltpu.VMEM((2 * packed, wide), BF16),
            pltpu.VMEM((packed - one_row, wide), BF16),
            pltpu.VMEM((low, wide), BF16),
            pltpu.VMEM((low, wide), BF16),
            pltpu.VMEM((packed, wide), BF16),
            pltpu.VMEM((size.enc, packed, 128), BF16),
            pltpu.VMEM((size.share, size.lat, packed, 128), BF16),
            pltpu.VMEM((size.share, packed, 128), BF16),
            pltpu.VMEM((size.share, packed, 128), BF16),
            pltpu.VMEM((size.lat, size.lon, size.chunk, wide), BF16),
            pltpu.VMEM((size.lat // 2, size.lon, size.chunk, wide), BF16),
            pltpu.VMEM((size.lon, size.chunk, wide), BF16),
            pltpu.VMEM((size.lon, size.chunk, wide), BF16),
            pltpu.VMEM((size.lon, size.chunk, wide), BF16),
            pltpu.VMEM((size.lon, size.chunk, wide), BF16),
            dma((7,)),
            dma((size.share,)),
            dma((2 * size.slots,)),
            dma((size.slots,)),
            dma((4,)),
            dma((4,)),
            dma((4,)),
            dma((4,)),
            dma((size.share, size.lat)),
            dma((size.share, size.lat)),
            dma((size.share,)),
            dma((size.share,)),
            dma((size.lat,)),
            dma((size.lat,)),
            dma((size.lon,)),
            dma((size.lon,)),
        ],
        compiler_params=pltpu.CompilerParams(
            collective_id=0, has_side_effects=True, vmem_limit_bytes=56 * 1024 * 1024
        ),
    )(
        lat_shift,
        lon_shift,
        *arrays,
        jnp.asarray(merge_order(size), BF16),
        key,
        value,
        merge,
        jnp.asarray(block_order(size), BF16),
        wqkv,
        proj,
    )


def local(
    atmos,
    land_sea,
    level_count,
    atm_weight,
    land_weight,
    level_embed,
    latent_query,
    key_weight,
    value_weight,
    merge_weight,
    lat_shift,
    lon_shift,
    qkv_weight,
    proj_weight,
    cotangent,
):
    size = Sizes(
        lax.axis_size("enc"),
        lax.axis_size("lat"),
        lax.axis_size("lon"),
        atmos.shape[0],
        atmos.shape[1],
        merge_weight.shape[1],
    )
    arrays = (
        atmos,
        land_sea,
        level_count,
        atm_weight,
        land_weight,
        level_embed,
        latent_query,
        cotangent,
    )
    packed, weights = layer(
        size,
        lat_shift,
        lon_shift,
        arrays,
        key_weight,
        value_weight,
        merge_weight,
        qkv_weight.T,
        proj_weight,
    )
    latent, grad_qkv, grad_proj = finish(size, packed, weights)
    return latent, grad_qkv, grad_proj.T


def solution(mesh):
    return jax.shard_map(
        local,
        mesh=mesh,
        in_specs=(
            P("enc", ("lon", "lat"), None, None),
            P("enc", ("lon", "lat"), None),
            P("enc", ("lon", "lat")),
            P(),
            P(),
            P(),
            P(),
            P(),
            P(),
            P(),
            P(),
            P(),
            P(None, "enc"),
            P("enc", None),
            P(None, "lat", "lon", None),
        ),
        out_specs=(
            P(None, "lat", "lon", "enc"),
            P(("lat", "lon"), "enc"),
            P("enc", ("lat", "lon")),
        ),
        check_vma=False,
    )
```

```python
import functools

import jax
import jax.numpy as jnp
import numpy as np
from jax import lax
from jax.experimental import pallas as pl
from jax.experimental.pallas import tpu as pltpu
from jax.sharding import PartitionSpec as P

PHEADS = 16
WIN_LAT = 6
WIN_LON = 12
HD = 64
LEVELS = 3
LINES = 16
MESH = pl.DeviceIdType.MESH

epsilon = 1e-05
F32 = jnp.float32
BF16 = jnp.bfloat16


def layer_norm(values):
    centre = jnp.mean(values, axis=-1, keepdims=True)
    centred = values - centre
    variance = jnp.mean(centred * centred, axis=-1, keepdims=True)
    inverse = lax.rsqrt(variance + epsilon)
    return (centred * inverse, inverse)


class Sizes:
    def __init__(self, enc, lat, lon, fine_rows, fine_cols, width):
        self.enc, self.lat, self.lon = enc, lat, lon
        band, block = fine_rows // 2, fine_cols // 2
        self.fine_rows, self.fine_cols = fine_rows, fine_cols
        self.patches = fine_rows * fine_cols
        self.patch_rows = -(-self.patches // 8) * 8
        self.fine_total = -(-LEVELS * self.patch_rows // 16) * 16
        self.band, self.block, self.width = band, block, width
        self.share = enc // lat
        self.rows, self.cols = self.share * band, lat * block
        self.slots = self.share * lat
        self.block_tokens = LEVELS * band * block
        self.block_rows = -(-self.block_tokens // 16) * 16
        self.row_tokens = LEVELS * self.cols
        self.tokens = self.rows * self.row_tokens
        self.half = self.tokens // 2
        self.packed = -(-self.half // 16) * 16
        self.group = lat * lon
        self.chunk = width // self.group
        self.total_rows = self.rows * lat


def block_order(size):
    matrix = np.zeros((size.tokens, size.slots * size.block_rows), np.float32)
    for a in range(size.rows):
        for level in range(LEVELS):
            for b in range(size.cols):
                slot = (a // size.band) * size.lat + b // size.block
                inner = (level * size.band + a % size.band) * size.block + b % size.block
                token = a * size.row_tokens + level * size.cols + b
                matrix[token, slot * size.block_rows + inner] = 1.0
    return matrix


def merge_order(size):
    matrix = np.zeros((4 * size.block_rows, size.fine_total), np.float32)
    for quadrant in range(4):
        for level in range(LEVELS):
            for i in range(size.band):
                for j in range(size.block):
                    patch = (2 * i + quadrant % 2) * size.fine_cols + 2 * j + quadrant // 2
                    token = (level * size.band + i) * size.block + j
                    matrix[quadrant * size.block_rows + token, level * size.patch_rows + patch] = 1.0
    return matrix


def token_place(size, token):
    row = ((token.astype(F32) + 0.5) * (1.0 / size.row_tokens)).astype(jnp.int32)
    rest = token - row * size.row_tokens
    level = ((rest.astype(F32) + 0.5) * (1.0 / size.cols)).astype(jnp.int32)
    return row, level, rest - level * size.cols


def dot(a, b):
    return jnp.dot(a, b, preferred_element_type=F32)


def dot_tb(a, b):
    return lax.dot_general(a, b, (((1,), (1,)), ((), ())), preferred_element_type=F32)


def dot_ta(a, b):
    return lax.dot_general(a, b, (((0,), (0,)), ((), ())), preferred_element_type=F32)


def encode_block(
    size,
    atmos_ref,
    land_ref,
    count_ref,
    atm_weight_ref,
    land_weight_ref,
    level_ref,
    query_ref,
    key_ref,
    value_ref,
    select_ref,
    merge_ref,
    loads,
    atm_rows,
    land_rows,
    level_rows,
    fine_rows,
    block_ref,
):
    patches = size.patches
    count, cols = patches * LINES, size.fine_cols
    width = key_ref.shape[0]
    atm_rows[...] = jnp.zeros_like(atm_rows)
    land_rows[...] = jnp.zeros_like(land_rows)
    level_rows[...] = jnp.zeros_like(level_rows)
    fine_rows[...] = jnp.zeros_like(fine_rows)
    for i in range(size.fine_rows):
        land_rows[i * cols : (i + 1) * cols, :] = land_ref[i].astype(F32)
        for j in range(cols):
            atm_rows[i * cols + j, : atmos_ref.shape[2], :] = atmos_ref[i, j]
    level_rows[: level_ref.shape[0], :] = level_ref[...]

    token = lax.broadcasted_iota(jnp.int32, (count, 1), 0)
    patch = jnp.right_shift(token, 4)
    height = token - jnp.left_shift(patch, 4)
    row = ((patch.astype(F32) + 0.5) * (1.0 / cols)).astype(jnp.int32)
    col = patch - row * cols
    spread = jnp.where(
        patch == lax.broadcasted_iota(jnp.int32, (count, size.patch_rows), 1), 1.0, 0.0
    ).astype(BF16)
    in_row = jnp.where(
        row == lax.broadcasted_iota(jnp.int32, (count, size.fine_rows), 1), 1.0, 0.0
    ).astype(BF16)
    counts = dot(in_row, count_ref[...].astype(F32).astype(BF16))
    in_col = col == lax.broadcasted_iota(jnp.int32, (count, cols), 1)
    limit = jnp.sum(jnp.where(in_col, counts, 0.0), axis=-1, keepdims=True)
    present = height.astype(F32) < limit

    land = dot(spread, land_rows[...].astype(BF16)).astype(BF16)
    embedded = dot(atm_rows[...].reshape(count, atm_rows.shape[2]), atm_weight_ref[...])
    embedded = embedded + dot(land, land_weight_ref[...])
    embedded = embedded.reshape(patches, LINES, width) + level_rows[...][None]
    tokens = layer_norm(embedded.reshape(count, width))[0].astype(BF16)
    loads[0].wait()
    loads[1].wait()
    key_rows = dot(tokens, key_ref[...]).astype(BF16)
    value_rows = dot(tokens, value_ref[...]).astype(BF16).astype(F32)

    head_width = width // PHEADS
    shape = (PHEADS, width)
    lane = lax.broadcasted_iota(jnp.int32, shape, 1)
    first = lax.broadcasted_iota(jnp.int32, shape, 0) * head_width
    in_head = jnp.logical_and(lane >= first, lane < first + head_width)
    queries = query_ref[...].astype(F32)
    queries = jnp.concatenate(
        [
            jnp.where(in_head, jnp.broadcast_to(queries[m : m + 1], shape), 0.0)
            for m in range(LEVELS)
        ],
        axis=0,
    ).astype(BF16)
    scores = dot_tb(key_rows, queries) * head_width ** (-0.5)
    weights = jnp.where(present, jnp.exp(scores), 0.0).reshape(patches, LINES, LEVELS * PHEADS)
    probs = weights / jnp.sum(weights, axis=1, keepdims=True)
    probs = probs.reshape(count, LEVELS * PHEADS).astype(BF16)
    shape = (LEVELS * PHEADS, LEVELS * width)
    lane = lax.broadcasted_iota(jnp.int32, shape, 1)
    first = lax.broadcasted_iota(jnp.int32, shape, 0) * head_width
    widen = jnp.where(
        jnp.logical_and(lane >= first, lane < first + head_width), 1.0, 0.0
    ).astype(BF16)
    for m in range(LEVELS):
        wide = dot(probs, widen[:, m * width : (m + 1) * width])
        attended = jnp.sum((wide * value_rows).reshape(patches, LINES, width), axis=1)
        fine_rows[m * size.patch_rows : m * size.patch_rows + patches, :] = attended

    loads[2].wait()
    merged = dot(select_ref[...], fine_rows[...].astype(BF16))
    parts = [merged[q * size.block_rows : (q + 1) * size.block_rows] for q in range(4)]
    centre = sum(jnp.sum(part, axis=-1, keepdims=True) for part in parts) * (0.25 / width)
    parts = [part - centre for part in parts]
    square = sum(jnp.sum(part * part, axis=-1, keepdims=True) for part in parts)
    inverse = lax.rsqrt(square * (0.25 / width) + epsilon)
    loads[3].wait()
    block = sum(
        dot((part * inverse).astype(BF16), merge_ref[q * width : (q + 1) * width, :])
        for q, part in enumerate(parts)
    )
    block_ref[...] = block.astype(BF16)


def pack_pair(values, odd, half):
    top, bottom = values[:half], values[half:]
    left = lax.broadcasted_iota(jnp.int32, top.shape, 1) < HD
    if odd:
        return jnp.where(left, pltpu.roll(top, HD, 1), bottom)
    return jnp.where(left, top, pltpu.roll(bottom, HD, 1))


def layer_kernel(
    size,
    factor,
    lat_shift,
    lon_shift,
    atmos_ref,
    land_ref,
    count_ref,
    atm_weight_ref,
    land_weight_ref,
    level_ref,
    query_ref,
    cot_in,
    select_hbm,
    key_hbm,
    value_hbm,
    merge_hbm,
    order_hbm,
    wqkv_hbm,
    proj_hbm,
    latent_out,
    weight_out,
    select_ref,
    key_ref,
    value_ref,
    merge_ref,
    order_ref,
    wqkv_ref,
    proj_ref,
    cot_ref,
    atm_rows,
    land_rows,
    level_rows,
    fine_rows,
    x_ref,
    lat_buf,
    normed_ref,
    inv_ref,
    hid_ref,
    blocks_qkv,
    products,
    halo_f,
    halo,
    halo_left,
    halo_up,
    halo_diag,
    halo_right,
    back_f,
    back,
    back_right,
    back_down,
    back_diag,
    back_left,
    msg,
    msg_in,
    part_out,
    part_in,
    grad,
    grad_in,
    mid,
    mid_in,
    total_out,
    total_in,
    load_sem,
    own_send,
    far_send,
    multi_recv,
    halo_send,
    halo_recv,
    back_send,
    back_recv,
    msg_send,
    msg_recv,
    part_send,
    part_recv,
    grad_send,
    grad_recv,
    total_send,
    total_recv,
    sums_out,
    sums_in,
    sums_send,
    sums_recv,
    rest_in,
    rest_out,
    rest_part,
    rest_send,
    rest_recv,
):
    enc, lat, lon = lax.axis_index("enc"), lax.axis_index("lat"), lax.axis_index("lon")
    n_enc, n_lat, n_lon, group = size.enc, size.lat, size.lon, size.group
    home = enc // size.share
    tokens, half, packed = size.tokens, size.half, size.packed
    away = home != lat

    loads = [
        pltpu.make_async_copy(source, target, load_sem.at[k])
        for k, (source, target) in enumerate(
            (
                (key_hbm, key_ref),
                (value_hbm, value_ref),
                (select_hbm, select_ref),
                (merge_hbm, merge_ref),
                (proj_hbm, proj_ref),
                (order_hbm, order_ref),
                (wqkv_hbm, wqkv_ref),
            )
        )
    ]
    for load in loads:
        load.start()
    barrier = pltpu.get_barrier_semaphore()

    def greet(*device):
        pl.semaphore_signal(barrier, inc=1, device_id=device, device_id_type=MESH)

    share = size.share
    place = enc % share
    next_lat, last_lat = (lat + 1) % n_lat, (lat + n_lat - 1) % n_lat
    next_lon, last_lon = (lon + 1) % n_lon, (lon + n_lon - 1) % n_lon
    for step in range(1, n_lat):
        greet(((home + step) % n_lat) * share + place, lat, lon)
        greet(enc, (lat + step) % n_lat, lon)
    for step in range(1, share):
        greet(home * share + (place + step) % share, lat, lon)
    for step in range(1, n_lon):
        greet(enc, lat, (lon + step) % n_lon)
    greet(enc, next_lat, next_lon)
    greet(enc, last_lat, last_lon)

    def greet_targets(k, carry):
        greet(home * share + k, home, lon)
        return carry

    def greet_sources(k, carry):
        for step in range(1, n_lat):
            greet(home * share + k, (lat + step) % n_lat, lon)
        return carry

    @pl.when(away)
    def _():
        lax.fori_loop(0, share, greet_targets, 0)

    @pl.when(jnp.logical_not(away))
    def _():
        lax.fori_loop(0, share, greet_sources, 0)

    encode_block(
        size,
        atmos_ref,
        land_ref,
        count_ref,
        atm_weight_ref,
        land_weight_ref,
        level_ref,
        query_ref,
        key_ref,
        value_ref,
        select_ref,
        merge_ref,
        loads,
        atm_rows,
        land_rows,
        level_rows,
        fine_rows,
        x_ref,
    )
    expected = 2 * (n_lat - 1) + share - 1 + n_lon - 1 + 2
    pl.semaphore_wait(
        barrier, expected + jnp.where(away, share, share * (n_lat - 1)).astype(jnp.int32)
    )

    slot = place * n_lat + lat
    order = (0, 1, 3, 2) if share == 4 else tuple(range(share))
    sides = (1, n_lat - 1) if n_lat > 2 else (1,)
    relay = jnp.logical_not(away)
    if n_lat == 4:
        passes_on = home == (lat + jnp.where(lat % 2 == 0, n_lat - 1, 1)) % n_lat
    else:
        passes_on = None
    opposite = (lat + 2) % n_lat

    def block_copy(source, k, send, target):
        return pltpu.make_async_remote_copy(
            src_ref=source,
            dst_ref=lat_buf.at[k],
            send_sem=send,
            recv_sem=multi_recv.at[k],
            device_id=target,
            device_id_type=MESH,
        )

    own_block = pltpu.make_async_copy(x_ref, lat_buf.at[slot], multi_recv.at[slot])

    def first_copy(step):
        target = (home * share + (place + step) % share, home, lon)
        return block_copy(x_ref, slot, own_send.at[step], target)

    def pass_copy(k, index, group):
        return block_copy(lat_buf.at[k], k, far_send.at[index], (group * share + place, lat, lon))

    @pl.when(relay)
    def _():
        own_block.start()

    @pl.when(away)
    def _():
        first_copy(0).start()

    for step in order[1:]:
        first_copy(step).start()

    for load in loads[4:]:
        load.wait()
    for k in range(size.rows * LEVELS):
        rows = pl.ds(k * size.cols, size.cols)
        normed_ref[rows, :] = cot_in[k % LEVELS, k // LEVELS].astype(F32)
    cot_ref[...] = normed_ref[...].astype(BF16)
    halo_f[:, 3 * HD :] = dot_tb(cot_ref[...], proj_ref[...])
    row_shift, col_shift = lat_shift[0], lon_shift[0]
    win = size.half
    win_pad = size.packed

    def number(rows, start=0):
        return start + lax.broadcasted_iota(jnp.int32, (rows, 1), 0)

    def column_of(rows, start=0):
        return token_place(size, number(rows, start))[2]

    def one_hot(index, columns):
        lane = lax.broadcasted_iota(jnp.int32, (index.shape[0], columns), 1)
        return jnp.where(index == lane, 1.0, 0.0).astype(BF16)

    low_rows = -(-(WIN_LAT - 1) * size.row_tokens // 16) * 16
    high_start = (size.rows - WIN_LAT + 1) * size.row_tokens // 16 * 16
    high_rows = tokens - high_start
    mid_start = size.row_tokens // 16 * 16
    mid_rows = -(-(size.rows - 1) * size.row_tokens // 16) * 16 - mid_start

    def rolled_index(start):
        row, level, col = token_place(size, number(win, start))
        row, col = row - row_shift, col - col_shift
        col = jnp.where(col < 0, col + size.cols, col)
        return row, row * size.row_tokens + level * size.cols + col

    first_row, first_index = rolled_index(0)
    take_first = one_hot(
        jnp.where(first_row < 0, first_index + tokens - high_start + low_rows, first_index),
        low_rows + high_rows,
    )
    take_second = one_hot(rolled_index(win)[1] - mid_start, mid_rows)

    row, level, col = token_place(size, number(tokens))
    row, col = row + row_shift, col + col_shift
    col = jnp.where(col >= size.cols, col - size.cols, col)
    inner = level * size.cols + col
    give_index = jnp.where(
        row < WIN_LAT,
        row * size.row_tokens + inner,
        jnp.where(
            row < 2 * WIN_LAT,
            (row - WIN_LAT) * size.row_tokens + inner + win_pad,
            (row - 2 * WIN_LAT) * size.row_tokens + inner + 2 * win_pad,
        ),
    )
    give = one_hot(give_index, 2 * win_pad + low_rows)

    def arrive(step):
        def body(k, carry):
            index = ((place + step) % share) * n_lat + k
            local_slot = jnp.logical_and(index == slot, relay)

            @pl.when(local_slot)
            def _():
                own_block.wait()

            @pl.when(jnp.logical_not(local_slot))
            def _():
                block_copy(x_ref, index, own_send.at[0], (enc, lat, lon)).wait_recv()

            @pl.when(relay)
            def _():
                for at, side in enumerate(sides):
                    pass_copy(index, at * size.slots + index, (lat + side) % n_lat).start()

            if passes_on is not None:

                @pl.when(passes_on)
                def _():
                    pass_copy(index, index, opposite).start()

            return carry

        return body

    band_rows = n_lat * size.block_rows
    for step in order:
        lax.fori_loop(0, n_lat, arrive(step), 0)
        band = (place + step) % share
        values = lat_buf[pl.ds(band * n_lat, n_lat)].reshape(band_rows, size.width)
        hidden = layer_norm(values.astype(F32))[0].astype(BF16)
        rows = pl.ds(pl.multiple_of(band * band_rows, 16), band_rows)
        blocks_qkv[rows, :] = dot_tb(hidden, wqkv_ref[...]).astype(BF16)
    halo_f[:, : 3 * HD] = dot(order_ref[...], blocks_qkv[...])
    halo[...] = halo_f[...].astype(BF16)


    def exchange(source, target, send, recv, k, *place):
        return pltpu.make_async_remote_copy(
            src_ref=source,
            dst_ref=target,
            send_sem=send.at[k],
            recv_sem=recv.at[k],
            device_id=(enc, *place),
            device_id_type=MESH,
        )

    low_part = halo.at[pl.ds(0, low_rows)]
    high_part = halo.at[pl.ds(high_start, high_rows)]
    mid_part = halo.at[pl.ds(mid_start, mid_rows)]
    halo_copies = [
        exchange(low_part, halo_left, halo_send, halo_recv, 0, lat, next_lon),
        exchange(high_part, halo_diag, halo_send, halo_recv, 1, next_lat, next_lon),
        exchange(high_part, halo_up, halo_send, halo_recv, 2, next_lat, lon),
        exchange(mid_part, halo_right, halo_send, halo_recv, 3, lat, last_lon),
    ]
    for copy in halo_copies:
        copy.start()

    step_rows = tokens // 3
    blocks = lat_buf[...].reshape(size.slots * size.block_rows, size.width)

    def normalise(k, carry):
        rows = pl.ds(pl.multiple_of(k * step_rows, 16), step_rows)
        normed, inverse = layer_norm(dot(order_ref[rows, :], blocks))
        normed_ref[rows, :] = normed
        inv_ref[rows, :] = jnp.broadcast_to(inverse, (step_rows, 128))
        hidden = normed.astype(BF16)
        hid_ref[rows, :] = hidden
        products[rows, :] = dot_tb(hidden, wqkv_ref[...])
        return carry

    lax.fori_loop(0, 3, normalise, 0)
    ones = jnp.ones((8, size.width), BF16)
    weight_sums = dot_tb(ones, wqkv_ref[...])
    coarse = weight_sums.astype(BF16)
    finer = (weight_sums - coarse.astype(F32)).astype(BF16)
    index = lax.broadcasted_iota(jnp.int32, weight_sums.shape, 0)
    weight_sums = jnp.where(
        index == 0, coarse.astype(F32), jnp.where(index == 1, finer.astype(F32), 0.0)
    ).astype(BF16)

    for copy in halo_copies:
        copy.wait_recv()

    split = size.cols - col_shift

    def choose(condition, one, other):
        return jnp.where(condition, one.astype(F32), other.astype(F32))

    low = choose(column_of(low_rows) < split, halo[:low_rows, :], halo_left[...])
    high = choose(column_of(high_rows, high_start) < split, halo_up[...], halo_diag[...])
    middle = choose(
        column_of(mid_rows, mid_start) < split,
        halo_right[...],
        halo[mid_start : mid_start + mid_rows, :],
    )
    score_scale = HD ** (-0.5)

    def window(w, tokens_in, take):
        part = dot(take, tokens_in.astype(BF16)).astype(BF16)
        queries, keys = part[:, :HD], part[:, HD : 2 * HD]
        values, grads = part[:, 2 * HD : 3 * HD], part[:, 3 * HD :]
        first = lat * size.rows + w * WIN_LAT
        row_a = token_place(size, lax.broadcasted_iota(jnp.int32, (win, 1), 0))[0]
        row_b = token_place(size, lax.broadcasted_iota(jnp.int32, (1, win), 1))[0]
        side_a = jnp.where(row_a + first < row_shift, 1, 0)
        side_b = jnp.where(row_b + first < row_shift, 1, 0)
        scores = dot_tb(queries, keys) * score_scale
        weights = jnp.where(side_a == side_b, jnp.exp(scores), 0.0)
        probs = weights * (1.0 / jnp.sum(weights, axis=-1, keepdims=True))
        low = probs.astype(BF16)
        grad_probs = dot_tb(grads, values)
        grad_scores = probs * (
            grad_probs - jnp.sum(grad_probs * probs, axis=-1, keepdims=True)
        )
        grad_low = grad_scores.astype(BF16)
        there = pl.ds(w * win_pad, win)
        back_f[there, :HD] = dot(grad_low, keys) * score_scale
        back_f[there, HD : 2 * HD] = dot_ta(grad_low, queries) * score_scale
        back_f[there, 2 * HD : 3 * HD] = dot_ta(low, grads)
        back_f[there, 3 * HD :] = dot(low, values)
        back_f[pl.ds(w * win_pad + win, win_pad - win), :] = jnp.zeros((win_pad - win, 4 * HD), F32)
        whole = pl.ds(w * win_pad, win_pad)
        back[whole, :] = back_f[whole, :].astype(BF16)

    far_start = size.row_tokens // 16 * 16
    far_rows = win_pad - far_start
    early_part = back.at[pl.ds(0, low_rows)]
    late_part = back.at[pl.ds(far_start, far_rows)]
    second_part = back.at[pl.ds(win_pad, win_pad)]
    back_copies = [
        exchange(late_part, back_right, back_send, back_recv, 0, lat, last_lon),
        exchange(early_part, back_diag, back_send, back_recv, 1, last_lat, last_lon),
        exchange(early_part, back_down, back_send, back_recv, 2, last_lat, lon),
        exchange(second_part, back_left, back_send, back_recv, 3, lat, next_lon),
    ]
    window(0, jnp.concatenate([low, high], axis=0), take_first)
    for copy in back_copies[:3]:
        copy.start()
    window(1, middle, take_second)
    back_copies[3].start()

    @pl.when(away)
    def _():
        first_copy(0).wait_send()

    for step in order[1:]:
        first_copy(step).wait_send()

    def passed(k, carry):
        @pl.when(relay)
        def _():
            for at, side in enumerate(sides):
                pass_copy(k, at * size.slots + k, (lat + side) % n_lat).wait_send()

        if passes_on is not None:

            @pl.when(passes_on)
            def _():
                pass_copy(k, k, opposite).wait_send()

        return carry

    lax.fori_loop(0, size.slots, passed, 0)
    for copy in back_copies:
        copy.wait_recv()

    here = back[...].astype(F32)
    cover = jnp.concatenate(
        [
            here[:far_start],
            choose(column_of(far_rows, far_start) >= col_shift, here[far_start:win_pad], back_right[...]),
            choose(column_of(win_pad) >= col_shift, back_left[...], here[win_pad:]),
            choose(column_of(low_rows) >= col_shift, back_down[...], back_diag[...]),
        ],
        axis=0,
    )
    own = dot(give, cover.astype(BF16)).astype(BF16)
    grad_rows, heads_out = own[:, : 3 * HD], own[:, 3 * HD :]

    sums = dot_tb(weight_sums, grad_rows)
    sums = sums + pltpu.roll(sums, 7, 0)
    cross = dot_tb(
        jnp.ones((8, 3 * HD), BF16), (grad_rows.astype(F32) * products[...]).astype(BF16)
    )
    lanes = 4 * 128
    pad = jnp.zeros((8, lanes - tokens), F32)
    sums = jnp.concatenate([sums, pad], axis=1)
    cross = jnp.concatenate([cross, pad], axis=1)
    index = lax.broadcasted_iota(jnp.int32, (8, 128), 0)
    extra = jnp.zeros((8, 128), F32)
    for k in range(4):
        columns = slice(k * 128, (k + 1) * 128)
        extra = jnp.where(index == k, jnp.broadcast_to(sums[:1, columns], (8, 128)), extra)
        extra = jnp.where(index == k + 4, cross[:, columns], extra)
    def sums_copy(step):
        target = ((home + step) % n_lat) * share + place
        return pltpu.make_async_remote_copy(
            src_ref=sums_out.at[0],
            dst_ref=sums_in.at[step - 1],
            send_sem=sums_send.at[step - 1],
            recv_sem=sums_recv.at[step - 1],
            device_id=(target, lat, lon),
            device_id_type=MESH,
        )

    def sums_part_copy(step):
        target = home * share + (place + step) % share
        return pltpu.make_async_remote_copy(
            src_ref=sums_out.at[1],
            dst_ref=sums_in.at[n_lat - 2 + step],
            send_sem=sums_send.at[n_lat - 2 + step],
            recv_sem=sums_recv.at[n_lat - 2 + step],
            device_id=(target, lat, lon),
            device_id_type=MESH,
        )

    filler = jnp.zeros((8, 128), F32)
    sums_out[0] = jnp.concatenate([extra, filler], axis=0).astype(BF16)
    sums_copies = [sums_copy(step) for step in range(1, n_lat)]
    sums_copies += [sums_part_copy(step) for step in range(1, share)]
    for copy in sums_copies[: n_lat - 1]:
        copy.start()

    later = tuple((place + step) % share for step in ((2, 1, 3, 0) if share == 4 else (1, 0)))

    most = packed - 48
    rest = pl.ds(most, packed - most)
    all_steps = (2, 1, 3, 0) if n_lat == 4 else (1, 0)

    def rest_copy(step, near):
        target = (place + near) % share
        return pltpu.make_async_remote_copy(
            src_ref=msg.at[((home + step) % n_lat) * share + target, rest],
            dst_ref=rest_in.at[step, near],
            send_sem=rest_send.at[step, near],
            recv_sem=rest_recv.at[step, near],
            device_id=(home * share + target, lat, lon),
            device_id_type=MESH,
        )

    def rest_part_copy(step):
        return pltpu.make_async_remote_copy(
            src_ref=rest_out.at[step],
            dst_ref=rest_part.at[step],
            send_sem=rest_send.at[step, 0],
            recv_sem=rest_recv.at[step, 0],
            device_id=(((home + step) % n_lat) * share + place, lat, lon),
            device_id_type=MESH,
        )

    rest_copies = []

    def group_copy(k, step):
        target = (home + step) % n_lat
        return pltpu.make_async_remote_copy(
            src_ref=msg.at[target * share + later[k], pl.ds(0, most)],
            dst_ref=msg_in.at[k, step],
            send_sem=msg_send.at[k, step],
            recv_sem=msg_recv.at[k, step],
            device_id=(target * share + place, lat, lon),
            device_id_type=MESH,
        )

    group_copies = []
    group_width = share * HD
    for step in all_steps:
        target = (home + step) % n_lat
        columns = pl.ds(pl.multiple_of(target * group_width, 128), group_width)
        head_part = dot(grad_rows, wqkv_ref[:, columns])
        for k in range(share):
            values = head_part[:, k // 2 * 128 : (k // 2 + 1) * 128]
            message = pack_pair(values, k % 2, half)
            msg[target * share + k] = jnp.concatenate([message, filler], axis=0).astype(BF16)
        if step > 0:
            for k in range(share):
                group_copies.append(group_copy(k, step))
                group_copies[-1].start()
        for near in range(1, share):
            rest_copies.append(rest_copy(step, near))
            rest_copies[-1].start()

    grad[:, :, :, : 3 * HD] = (
        (dot_ta(hid_ref[...], grad_rows) * factor)
        .astype(BF16)
        .reshape(n_lat, n_lon, size.chunk, 3 * HD)
    )
    grad[:, :, :, 3 * HD :] = (
        (dot_ta(cot_ref[...], heads_out) * factor)
        .astype(BF16)
        .reshape(n_lat, n_lon, size.chunk, HD)
    )

    pairs = n_lat // 2
    pair, core = lat // 2, lat % 2

    def core_copy(k):
        return pltpu.make_async_remote_copy(
            src_ref=grad.at[((pair + k) % pairs) * 2 + 1 - core],
            dst_ref=grad_in.at[k],
            send_sem=grad_send.at[k],
            recv_sem=grad_recv.at[k],
            device_id=(enc, pair * 2 + 1 - core, lon),
            device_id_type=MESH,
        )

    def pair_copy():
        return pltpu.make_async_remote_copy(
            src_ref=mid,
            dst_ref=mid_in,
            send_sem=grad_send.at[pairs],
            recv_sem=grad_recv.at[pairs],
            device_id=(enc, ((pair + 1) % pairs) * 2 + core, lon),
            device_id_type=MESH,
        )

    def line_copy(step):
        target = (lon + step) % n_lon
        return pltpu.make_async_remote_copy(
            src_ref=total_out.at[target],
            dst_ref=total_in.at[step],
            send_sem=total_send.at[step],
            recv_sem=total_recv.at[step],
            device_id=(enc, lat, target),
            device_id_type=MESH,
        )

    for k in reversed(range(pairs)):
        core_copy(k).start()
    feature_sums = jnp.concatenate([extra, filler], axis=0)
    for k in range(n_lat - 1):
        sums_copies[k].wait_recv()
        feature_sums = feature_sums + sums_in[k].astype(F32)
    sums_out[1] = feature_sums.astype(BF16)
    for copy in sums_copies[n_lat - 1 :]:
        copy.start()
    if pairs == 2:
        core_copy(1).wait_recv()
        mid[...] = (grad[(1 - pair) * 2 + core].astype(F32) + grad_in[1].astype(F32)).astype(BF16)
        pair_copy().start()

    for copy in halo_copies + back_copies:
        copy.wait_send()

    columns = pl.ds(pl.multiple_of((enc // 2) * 128, 128), 128)
    odd = enc % 2 == 1

    def own_share(values):
        return jnp.where(odd, pack_pair(values, 1, half), pack_pair(values, 0, half))

    def side_by_side(column):
        left = lax.broadcasted_iota(jnp.int32, (half, 128), 1) < HD
        return jnp.where(left, column[:half], column[half:])

    normed_own = own_share(normed_ref[:, columns])
    cot_own = own_share(cot_ref[:, columns].astype(F32))
    inverse_own = side_by_side(inv_ref[...])

    def part_copy(k):
        return pltpu.make_async_remote_copy(
            src_ref=part_out.at[k],
            dst_ref=part_in.at[k],
            send_sem=part_send.at[k],
            recv_sem=part_recv.at[k],
            device_id=(home * share + later[k], lat, lon),
            device_id_type=MESH,
        )

    def group_sum(k):
        values = msg[home * share + later[k], :most].astype(F32)
        for step in range(1, n_lat):
            group_copy(k, step).wait_recv()
            values = values + msg_in[k, step].astype(F32)
        return values

    def send_part(k):
        part_out[k] = group_sum(k).astype(BF16)
        part_copy(k).start()

    for k in range(n_lat - 1, len(sums_copies)):
        sums_copies[k].wait_recv()
        feature_sums = feature_sums + sums_in[k].astype(F32)
    feature_sums = feature_sums[:8]
    token = lax.broadcasted_iota(jnp.int32, (tokens, 1), 0)
    lane = lax.broadcasted_iota(jnp.int32, (tokens, 128), 1)
    line = jnp.right_shift(token, 7)
    pick = jnp.where(token - line * 128 == lane, 1.0, 0.0)
    means = lax.dot_general(
        pick,
        feature_sums,
        (((1,), (1,)), ((), ())),
        precision=lax.Precision.HIGHEST,
        preferred_element_type=F32,
    ) * (1.0 / size.width)
    which = lax.broadcasted_iota(jnp.int32, (tokens, 8), 1)
    mean_grad = jnp.sum(jnp.where(which == line, means, 0.0), axis=-1, keepdims=True)
    mean_cross = jnp.sum(jnp.where(which == line + 4, means, 0.0), axis=-1, keepdims=True)
    mean_grad_own, mean_cross_own = side_by_side(mean_grad), side_by_side(mean_cross)
    fixed = cot_own - inverse_own * (mean_grad_own + normed_own * mean_cross_own)

    def rest_sum(step):
        values = msg[((home + step) % n_lat) * share + place, most:].astype(F32)
        for near in range(1, share):
            rest_copy(step, near).wait_recv()
            values = values + rest_in[step, near].astype(F32)
        return values

    send_part(0)
    for step in all_steps[:-1]:
        rest_out[step] = rest_sum(step).astype(BF16)
        rest_part_copy(step).start()
    core_copy(0).wait_recv()
    weight_sum = grad[lat].astype(F32) + grad_in[0].astype(F32)
    if pairs == 2:
        pair_copy().wait_recv()
        weight_sum = weight_sum + mid_in[...].astype(F32)
    total_out[...] = weight_sum.astype(BF16)
    far_first = sorted(range(1, n_lon), key=lambda step: -min(step, n_lon - step))
    for step in far_first:
        line_copy(step).start()
    for k in range(1, share - 1):
        send_part(k)
    total = group_sum(share - 1)
    for copy in group_copies + sums_copies + rest_copies:
        copy.wait_send()
    for k in range(pairs):
        core_copy(k).wait_send()
    if pairs == 2:
        pair_copy().wait_send()
    for k in range(share - 1):
        part_copy(k).wait_recv()
        total = total + part_in[k].astype(F32)
    rest_total = rest_sum(0)
    for step in all_steps[:-1]:
        rest_part_copy(step).wait_recv()
        rest_total = rest_total + rest_part[step].astype(F32)
    total = jnp.concatenate([total, rest_total], axis=0)

    latent_out[...] = fixed + inverse_own * total[:half]

    weights = total_out[lon].astype(F32)
    for step in reversed(far_first):
        line_copy(step).wait_recv()
        weights = weights + total_in[step].astype(F32)
    weight_out[...] = weights

    for k in range(share - 1):
        part_copy(k).wait_send()
    for step in all_steps[:-1]:
        rest_part_copy(step).wait_send()
    for step in far_first:
        line_copy(step).wait_send()


def finish_kernel(size, packed_ref, weight_ref, latent_out, qkv_out, proj_out):
    latent = packed_ref[...]
    other = pltpu.roll(latent, HD, 1)
    lines = size.rows * LEVELS // 2
    for k in range(2 * lines):
        start = (k % lines) * size.cols
        values = (latent, other)[k // lines][start : start + size.cols, :HD]
        latent_out[k % LEVELS, k // LEVELS] = values.astype(BF16)
    qkv_out[...] = weight_ref[:, : 3 * HD]
    proj_out[...] = weight_ref[:, 3 * HD :]


def finish(size, packed, weights):
    vmem = pl.BlockSpec(memory_space=pltpu.VMEM)
    return pl.pallas_call(
        functools.partial(finish_kernel, size),
        out_shape=(
            jax.ShapeDtypeStruct((LEVELS, size.rows, size.cols, HD), BF16),
            jax.ShapeDtypeStruct((size.chunk, 3 * HD), F32),
            jax.ShapeDtypeStruct((size.chunk, HD), F32),
        ),
        in_specs=[vmem, vmem],
        out_specs=(vmem, vmem, vmem),
    )(packed, weights)


def layer(size, lat_shift, lon_shift, arrays, key, value, merge, wqkv, proj):
    tokens, packed = size.tokens, size.packed
    atmos, land = arrays[0], arrays[1]
    vmem = pl.BlockSpec(memory_space=pltpu.VMEM)
    smem = pl.BlockSpec(memory_space=pltpu.SMEM)
    factor = (tokens * size.group) ** (-0.5)
    wide = 4 * HD
    dma = pltpu.SemaphoreType.DMA
    low = -(-(WIN_LAT - 1) * size.row_tokens // 16) * 16
    high = tokens - (size.rows - WIN_LAT + 1) * size.row_tokens // 16 * 16
    one_row = size.row_tokens // 16 * 16
    middle = -(-(size.rows - 1) * size.row_tokens // 16) * 16 - one_row
    return pl.pallas_call(
        functools.partial(layer_kernel, size, factor),
        out_shape=(
            jax.ShapeDtypeStruct((size.half, 128), F32),
            jax.ShapeDtypeStruct((size.chunk, wide), F32),
        ),
        in_specs=[smem, smem] + [vmem] * len(arrays) + [pl.BlockSpec(memory_space=pl.ANY)] * 7,
        out_specs=(vmem, vmem),
        scratch_shapes=[
            pltpu.VMEM((4 * size.block_rows, size.fine_total), BF16),
            pltpu.VMEM(key.shape, BF16),
            pltpu.VMEM(key.shape, BF16),
            pltpu.VMEM(merge.shape, BF16),
            pltpu.VMEM((tokens, size.slots * size.block_rows), BF16),
            pltpu.VMEM(wqkv.shape, BF16),
            pltpu.VMEM(proj.shape, BF16),
            pltpu.VMEM((tokens, size.width), BF16),
            pltpu.VMEM((size.patches, LINES, atmos.shape[3]), BF16),
            pltpu.VMEM((size.patch_rows, land.shape[2]), F32),
            pltpu.VMEM((LINES, key.shape[0]), F32),
            pltpu.VMEM((size.fine_total, key.shape[0]), F32),
            pltpu.VMEM((size.block_rows, size.width), BF16),
            pltpu.VMEM((size.slots, size.block_rows, size.width), BF16),
            pltpu.VMEM((tokens, size.width), F32),
            pltpu.VMEM((tokens, 128), F32),
            pltpu.VMEM((tokens, size.width), BF16),
            pltpu.VMEM((size.slots * size.block_rows, 3 * HD), BF16),
            pltpu.VMEM((tokens, 3 * HD), F32),
            pltpu.VMEM((tokens, wide), F32),
            pltpu.VMEM((tokens, wide), BF16),
            pltpu.VMEM((low, wide), BF16),
            pltpu.VMEM((high, wide), BF16),
            pltpu.VMEM((high, wide), BF16),
            pltpu.VMEM((middle, wide), BF16),
            pltpu.VMEM((2 * packed, wide), F32),
            pltpu.VMEM((2 * packed, wide), BF16),
            pltpu.VMEM((packed - one_row, wide), BF16),
            pltpu.VMEM((low, wide), BF16),
            pltpu.VMEM((low, wide), BF16),
            pltpu.VMEM((packed, wide), BF16),
            pltpu.VMEM((size.enc, packed, 128), BF16),
            pltpu.VMEM((size.share, size.lat, packed - 48, 128), BF16),
            pltpu.VMEM((size.share, packed - 48, 128), BF16),
            pltpu.VMEM((size.share, packed - 48, 128), BF16),
            pltpu.VMEM((size.lat, size.lon, size.chunk, wide), BF16),
            pltpu.VMEM((size.lat // 2, size.lon, size.chunk, wide), BF16),
            pltpu.VMEM((size.lon, size.chunk, wide), BF16),
            pltpu.VMEM((size.lon, size.chunk, wide), BF16),
            pltpu.VMEM((size.lon, size.chunk, wide), BF16),
            pltpu.VMEM((size.lon, size.chunk, wide), BF16),
            dma((7,)),
            dma((size.share,)),
            dma((2 * size.slots,)),
            dma((size.slots,)),
            dma((4,)),
            dma((4,)),
            dma((4,)),
            dma((4,)),
            dma((size.share, size.lat)),
            dma((size.share, size.lat)),
            dma((size.share,)),
            dma((size.share,)),
            dma((size.lat,)),
            dma((size.lat,)),
            dma((size.lon,)),
            dma((size.lon,)),
            pltpu.VMEM((2, 16, 128), BF16),
            pltpu.VMEM((size.lat + size.share - 2, 16, 128), BF16),
            dma((size.lat + size.share - 2,)),
            dma((size.lat + size.share - 2,)),
            pltpu.VMEM((size.lat, size.share, 48, 128), BF16),
            pltpu.VMEM((size.lat, 48, 128), BF16),
            pltpu.VMEM((size.lat, 48, 128), BF16),
            dma((size.lat, size.share)),
            dma((size.lat, size.share)),
        ],
        compiler_params=pltpu.CompilerParams(
            collective_id=0, has_side_effects=True, vmem_limit_bytes=56 * 1024 * 1024
        ),
    )(
        lat_shift,
        lon_shift,
        *arrays,
        jnp.asarray(merge_order(size), BF16),
        key,
        value,
        merge,
        jnp.asarray(block_order(size), BF16),
        wqkv,
        proj,
    )


def local(
    atmos,
    land_sea,
    level_count,
    atm_weight,
    land_weight,
    level_embed,
    latent_query,
    key_weight,
    value_weight,
    merge_weight,
    lat_shift,
    lon_shift,
    qkv_weight,
    proj_weight,
    cotangent,
):
    size = Sizes(
        lax.axis_size("enc"),
        lax.axis_size("lat"),
        lax.axis_size("lon"),
        atmos.shape[0],
        atmos.shape[1],
        merge_weight.shape[1],
    )
    arrays = (
        atmos,
        land_sea,
        level_count,
        atm_weight,
        land_weight,
        level_embed,
        latent_query,
        cotangent,
    )
    packed, weights = layer(
        size,
        lat_shift,
        lon_shift,
        arrays,
        key_weight,
        value_weight,
        merge_weight,
        qkv_weight.T,
        proj_weight,
    )
    latent, grad_qkv, grad_proj = finish(size, packed, weights)
    return latent, grad_qkv, grad_proj.T


def solution(mesh):
    return jax.shard_map(
        local,
        mesh=mesh,
        in_specs=(
            P("enc", ("lon", "lat"), None, None),
            P("enc", ("lon", "lat"), None),
            P("enc", ("lon", "lat")),
            P(),
            P(),
            P(),
            P(),
            P(),
            P(),
            P(),
            P(),
            P(),
            P(None, "enc"),
            P("enc", None),
            P(None, "lat", "lon", None),
        ),
        out_specs=(
            P(None, "lat", "lon", "enc"),
            P(("lat", "lon"), "enc"),
            P("enc", ("lat", "lon")),
        ),
        check_vma=False,
    )
```

```python
import functools

import jax
import jax.numpy as jnp
import numpy as np
from jax import lax
from jax.experimental import pallas as pl
from jax.experimental.pallas import tpu as pltpu
from jax.sharding import PartitionSpec as P

PHEADS = 16
WIN_LAT = 6
WIN_LON = 12
HD = 64
LEVELS = 3
LINES = 16
MESH = pl.DeviceIdType.MESH

epsilon = 1e-05
F32 = jnp.float32
BF16 = jnp.bfloat16


def layer_norm(values):
    centre = jnp.mean(values, axis=-1, keepdims=True)
    centred = values - centre
    variance = jnp.mean(centred * centred, axis=-1, keepdims=True)
    inverse = lax.rsqrt(variance + epsilon)
    return (centred * inverse, inverse)


class Sizes:
    def __init__(self, enc, lat, lon, fine_rows, fine_cols, width):
        self.enc, self.lat, self.lon = enc, lat, lon
        band, block = fine_rows // 2, fine_cols // 2
        self.fine_rows, self.fine_cols = fine_rows, fine_cols
        self.patches = fine_rows * fine_cols
        self.patch_rows = -(-self.patches // 8) * 8
        self.fine_total = -(-LEVELS * self.patch_rows // 16) * 16
        self.band, self.block, self.width = band, block, width
        self.share = enc // lat
        self.rows, self.cols = self.share * band, lat * block
        self.slots = self.share * lat
        self.block_tokens = LEVELS * band * block
        self.block_rows = -(-self.block_tokens // 16) * 16
        self.row_tokens = LEVELS * self.cols
        self.tokens = self.rows * self.row_tokens
        self.half = self.tokens // 2
        self.packed = -(-self.half // 16) * 16
        self.group = lat * lon
        self.chunk = width // self.group
        self.total_rows = self.rows * lat


def block_order(size):
    matrix = np.zeros((size.tokens, size.slots * size.block_rows), np.float32)
    for a in range(size.rows):
        for level in range(LEVELS):
            for b in range(size.cols):
                slot = (a // size.band) * size.lat + b // size.block
                inner = (level * size.band + a % size.band) * size.block + b % size.block
                token = a * size.row_tokens + level * size.cols + b
                matrix[token, slot * size.block_rows + inner] = 1.0
    return matrix


def merge_order(size):
    matrix = np.zeros((4 * size.block_rows, size.fine_total), np.float32)
    for quadrant in range(4):
        for level in range(LEVELS):
            for i in range(size.band):
                for j in range(size.block):
                    patch = (2 * i + quadrant % 2) * size.fine_cols + 2 * j + quadrant // 2
                    token = (level * size.band + i) * size.block + j
                    matrix[quadrant * size.block_rows + token, level * size.patch_rows + patch] = 1.0
    return matrix


def token_place(size, token):
    row = ((token.astype(F32) + 0.5) * (1.0 / size.row_tokens)).astype(jnp.int32)
    rest = token - row * size.row_tokens
    level = ((rest.astype(F32) + 0.5) * (1.0 / size.cols)).astype(jnp.int32)
    return row, level, rest - level * size.cols


def dot(a, b):
    return jnp.dot(a, b, preferred_element_type=F32)


def dot_tb(a, b):
    return lax.dot_general(a, b, (((1,), (1,)), ((), ())), preferred_element_type=F32)


def dot_ta(a, b):
    return lax.dot_general(a, b, (((0,), (0,)), ((), ())), preferred_element_type=F32)


def encode_block(
    size,
    atmos_ref,
    land_ref,
    count_ref,
    atm_weight_ref,
    land_weight_ref,
    level_ref,
    query_ref,
    key_ref,
    value_ref,
    select_ref,
    merge_ref,
    loads,
    atm_rows,
    land_rows,
    level_rows,
    fine_rows,
    block_ref,
):
    patches = size.patches
    count, cols = patches * LINES, size.fine_cols
    width = key_ref.shape[0]
    atm_rows[...] = jnp.zeros_like(atm_rows)
    land_rows[...] = jnp.zeros_like(land_rows)
    level_rows[...] = jnp.zeros_like(level_rows)
    fine_rows[...] = jnp.zeros_like(fine_rows)
    for i in range(size.fine_rows):
        land_rows[i * cols : (i + 1) * cols, :] = land_ref[i].astype(F32)
        for j in range(cols):
            atm_rows[i * cols + j, : atmos_ref.shape[2], :] = atmos_ref[i, j]
    level_rows[: level_ref.shape[0], :] = level_ref[...]

    token = lax.broadcasted_iota(jnp.int32, (count, 1), 0)
    patch = jnp.right_shift(token, 4)
    height = token - jnp.left_shift(patch, 4)
    row = ((patch.astype(F32) + 0.5) * (1.0 / cols)).astype(jnp.int32)
    col = patch - row * cols
    spread = jnp.where(
        patch == lax.broadcasted_iota(jnp.int32, (count, size.patch_rows), 1), 1.0, 0.0
    ).astype(BF16)
    in_row = jnp.where(
        row == lax.broadcasted_iota(jnp.int32, (count, size.fine_rows), 1), 1.0, 0.0
    ).astype(BF16)
    counts = dot(in_row, count_ref[...].astype(F32).astype(BF16))
    in_col = col == lax.broadcasted_iota(jnp.int32, (count, cols), 1)
    limit = jnp.sum(jnp.where(in_col, counts, 0.0), axis=-1, keepdims=True)
    present = height.astype(F32) < limit

    land = dot(spread, land_rows[...].astype(BF16)).astype(BF16)
    embedded = dot(atm_rows[...].reshape(count, atm_rows.shape[2]), atm_weight_ref[...])
    embedded = embedded + dot(land, land_weight_ref[...])
    embedded = embedded.reshape(patches, LINES, width) + level_rows[...][None]
    tokens = layer_norm(embedded.reshape(count, width))[0].astype(BF16)
    loads[0].wait()
    loads[1].wait()
    key_rows = dot(tokens, key_ref[...]).astype(BF16)
    value_rows = dot(tokens, value_ref[...]).astype(BF16).astype(F32)

    head_width = width // PHEADS
    shape = (PHEADS, width)
    lane = lax.broadcasted_iota(jnp.int32, shape, 1)
    first = lax.broadcasted_iota(jnp.int32, shape, 0) * head_width
    in_head = jnp.logical_and(lane >= first, lane < first + head_width)
    queries = query_ref[...].astype(F32)
    queries = jnp.concatenate(
        [
            jnp.where(in_head, jnp.broadcast_to(queries[m : m + 1], shape), 0.0)
            for m in range(LEVELS)
        ],
        axis=0,
    ).astype(BF16)
    scores = dot_tb(key_rows, queries) * head_width ** (-0.5)
    weights = jnp.where(present, jnp.exp(scores), 0.0).reshape(patches, LINES, LEVELS * PHEADS)
    probs = weights / jnp.sum(weights, axis=1, keepdims=True)
    probs = probs.reshape(count, LEVELS * PHEADS).astype(BF16)
    shape = (LEVELS * PHEADS, LEVELS * width)
    lane = lax.broadcasted_iota(jnp.int32, shape, 1)
    first = lax.broadcasted_iota(jnp.int32, shape, 0) * head_width
    widen = jnp.where(
        jnp.logical_and(lane >= first, lane < first + head_width), 1.0, 0.0
    ).astype(BF16)
    for m in range(LEVELS):
        wide = dot(probs, widen[:, m * width : (m + 1) * width])
        attended = jnp.sum((wide * value_rows).reshape(patches, LINES, width), axis=1)
        fine_rows[m * size.patch_rows : m * size.patch_rows + patches, :] = attended

    loads[2].wait()
    merged = dot(select_ref[...], fine_rows[...].astype(BF16))
    parts = [merged[q * size.block_rows : (q + 1) * size.block_rows] for q in range(4)]
    centre = sum(jnp.sum(part, axis=-1, keepdims=True) for part in parts) * (0.25 / width)
    parts = [part - centre for part in parts]
    square = sum(jnp.sum(part * part, axis=-1, keepdims=True) for part in parts)
    inverse = lax.rsqrt(square * (0.25 / width) + epsilon)
    loads[3].wait()
    block = sum(
        dot((part * inverse).astype(BF16), merge_ref[q * width : (q + 1) * width, :])
        for q, part in enumerate(parts)
    )
    block_ref[...] = block.astype(BF16)


def pack_pair(values, odd, half):
    top, bottom = values[:half], values[half:]
    left = lax.broadcasted_iota(jnp.int32, top.shape, 1) < HD
    if odd:
        return jnp.where(left, pltpu.roll(top, HD, 1), bottom)
    return jnp.where(left, top, pltpu.roll(bottom, HD, 1))


def layer_kernel(
    size,
    factor,
    lat_shift,
    lon_shift,
    atmos_ref,
    land_ref,
    count_ref,
    atm_weight_ref,
    land_weight_ref,
    level_ref,
    query_ref,
    cot_in,
    select_hbm,
    key_hbm,
    value_hbm,
    merge_hbm,
    order_hbm,
    wqkv_hbm,
    proj_hbm,
    latent_out,
    weight_out,
    select_ref,
    key_ref,
    value_ref,
    merge_ref,
    order_ref,
    wqkv_ref,
    proj_ref,
    cot_ref,
    atm_rows,
    land_rows,
    level_rows,
    fine_rows,
    x_ref,
    lat_buf,
    normed_ref,
    inv_ref,
    hid_ref,
    blocks_qkv,
    products,
    halo_f,
    halo,
    halo_left,
    halo_up,
    halo_diag,
    halo_right,
    back_f,
    back,
    back_right,
    back_down,
    back_diag,
    back_left,
    msg,
    msg_in,
    part_out,
    part_in,
    grad,
    grad_in,
    mid,
    mid_in,
    total_out,
    total_in,
    load_sem,
    own_send,
    far_send,
    multi_recv,
    halo_send,
    halo_recv,
    back_send,
    back_recv,
    msg_send,
    msg_recv,
    part_send,
    part_recv,
    grad_send,
    grad_recv,
    total_send,
    total_recv,
    sums_out,
    sums_in,
    sums_send,
    sums_recv,
    side_send,
    side_recv,
    rest_in,
    rest_out,
    rest_part,
    rest_send,
    rest_recv,
):
    enc, lat, lon = lax.axis_index("enc"), lax.axis_index("lat"), lax.axis_index("lon")
    n_enc, n_lat, n_lon, group = size.enc, size.lat, size.lon, size.group
    home = enc // size.share
    tokens, half, packed = size.tokens, size.half, size.packed
    away = home != lat

    loads = [
        pltpu.make_async_copy(source, target, load_sem.at[k])
        for k, (source, target) in enumerate(
            (
                (key_hbm, key_ref),
                (value_hbm, value_ref),
                (select_hbm, select_ref),
                (merge_hbm, merge_ref),
                (proj_hbm, proj_ref),
                (order_hbm, order_ref),
                (wqkv_hbm, wqkv_ref),
            )
        )
    ]
    for load in loads:
        load.start()
    barrier = pltpu.get_barrier_semaphore()

    def greet(*device):
        pl.semaphore_signal(barrier, inc=1, device_id=device, device_id_type=MESH)

    share = size.share
    place = enc % share
    next_lat, last_lat = (lat + 1) % n_lat, (lat + n_lat - 1) % n_lat
    next_lon, last_lon = (lon + 1) % n_lon, (lon + n_lon - 1) % n_lon
    for step in range(1, n_lat):
        greet(((home + step) % n_lat) * share + place, lat, lon)
        greet(enc, (lat + step) % n_lat, lon)
        greet(((home + step) % n_lat) * share + place, home, lon)
    for step in range(1, share):
        greet(home * share + (place + step) % share, lat, lon)
    for step in range(1, n_lon):
        greet(enc, lat, (lon + step) % n_lon)
    greet(enc, next_lat, next_lon)
    greet(enc, last_lat, last_lon)

    def greet_targets(k, carry):
        greet(home * share + k, home, lon)
        return carry

    def greet_sources(k, carry):
        for step in range(1, n_lat):
            greet(home * share + k, (lat + step) % n_lat, lon)
        return carry

    def greet_side(k, carry):
        greet(lat * share + place, k, lon)
        return carry

    @pl.when(away)
    def _():
        lax.fori_loop(0, share, greet_targets, 0)
        lax.fori_loop(0, n_lat, greet_side, 0)

    @pl.when(jnp.logical_not(away))
    def _():
        lax.fori_loop(0, share, greet_sources, 0)

    encode_block(
        size,
        atmos_ref,
        land_ref,
        count_ref,
        atm_weight_ref,
        land_weight_ref,
        level_ref,
        query_ref,
        key_ref,
        value_ref,
        select_ref,
        merge_ref,
        loads,
        atm_rows,
        land_rows,
        level_rows,
        fine_rows,
        x_ref,
    )
    expected = 3 * (n_lat - 1) + share - 1 + n_lon - 1 + 2
    pl.semaphore_wait(
        barrier, expected + jnp.where(away, share + n_lat, share * (n_lat - 1)).astype(jnp.int32)
    )

    slot = place * n_lat + lat
    order = (0, 1, 3, 2) if share == 4 else tuple(range(share))
    sides = (1, n_lat - 1) if n_lat > 2 else (1,)
    relay = jnp.logical_not(away)
    if n_lat == 4:
        passes_on = home == (lat + jnp.where(lat % 2 == 0, n_lat - 1, 1)) % n_lat
    else:
        passes_on = None
    opposite = (lat + 2) % n_lat

    main = pl.ds(0, size.width - 128)
    side_part = pl.ds(size.width - 128, 128)

    def block_copy(source, k, send, target):
        return pltpu.make_async_remote_copy(
            src_ref=source.at[:, main],
            dst_ref=lat_buf.at[k, :, main],
            send_sem=send,
            recv_sem=multi_recv.at[k],
            device_id=target,
            device_id_type=MESH,
        )

    own_block = pltpu.make_async_copy(
        x_ref.at[:, main], lat_buf.at[slot, :, main], multi_recv.at[slot]
    )
    own_side = pltpu.make_async_copy(
        x_ref.at[:, side_part], lat_buf.at[slot, :, side_part], side_recv.at[slot]
    )

    def side_copy(source, k, send, target):
        return pltpu.make_async_remote_copy(
            src_ref=source.at[:, side_part],
            dst_ref=lat_buf.at[k, :, side_part],
            send_sem=send,
            recv_sem=side_recv.at[k],
            device_id=target,
            device_id_type=MESH,
        )

    def side_first(step):
        target = (((home + step) % n_lat) * share + place, home, lon)
        return side_copy(x_ref, slot, side_send.at[step], target)

    def side_pass(k, near):
        index = place * n_lat + k
        target = (home * share + (place + near) % share, lat, lon)
        return side_copy(lat_buf.at[index], index, side_send.at[n_lat * near + k], target)

    def first_copy(step):
        target = (home * share + (place + step) % share, home, lon)
        return block_copy(x_ref, slot, own_send.at[step], target)

    def pass_copy(k, index, group):
        return block_copy(lat_buf.at[k], k, far_send.at[index], (group * share + place, lat, lon))

    @pl.when(relay)
    def _():
        own_block.start()
        own_side.start()

    @pl.when(away)
    def _():
        first_copy(0).start()
        side_first(0).start()

    for step in range(1, n_lat):
        side_first(step).start()

    for step in order[1:]:
        first_copy(step).start()

    for load in loads[4:]:
        load.wait()
    for k in range(size.rows * LEVELS):
        rows = pl.ds(k * size.cols, size.cols)
        normed_ref[rows, :] = cot_in[k % LEVELS, k // LEVELS].astype(F32)
    cot_ref[...] = normed_ref[...].astype(BF16)
    halo_f[:, 3 * HD :] = dot_tb(cot_ref[...], proj_ref[...])
    row_shift, col_shift = lat_shift[0], lon_shift[0]
    win = size.half
    win_pad = size.packed

    def number(rows, start=0):
        return start + lax.broadcasted_iota(jnp.int32, (rows, 1), 0)

    def column_of(rows, start=0):
        return token_place(size, number(rows, start))[2]

    def one_hot(index, columns):
        lane = lax.broadcasted_iota(jnp.int32, (index.shape[0], columns), 1)
        return jnp.where(index == lane, 1.0, 0.0).astype(BF16)

    low_rows = -(-(WIN_LAT - 1) * size.row_tokens // 16) * 16
    high_start = (size.rows - WIN_LAT + 1) * size.row_tokens // 16 * 16
    high_rows = tokens - high_start
    mid_start = size.row_tokens // 16 * 16
    mid_rows = -(-(size.rows - 1) * size.row_tokens // 16) * 16 - mid_start

    def rolled_index(start):
        row, level, col = token_place(size, number(win, start))
        row, col = row - row_shift, col - col_shift
        col = jnp.where(col < 0, col + size.cols, col)
        return row, row * size.row_tokens + level * size.cols + col

    first_row, first_index = rolled_index(0)
    take_first = one_hot(
        jnp.where(first_row < 0, first_index + tokens - high_start + low_rows, first_index),
        low_rows + high_rows,
    )
    take_second = one_hot(rolled_index(win)[1] - mid_start, mid_rows)

    row, level, col = token_place(size, number(tokens))
    row, col = row + row_shift, col + col_shift
    col = jnp.where(col >= size.cols, col - size.cols, col)
    inner = level * size.cols + col
    give_index = jnp.where(
        row < WIN_LAT,
        row * size.row_tokens + inner,
        jnp.where(
            row < 2 * WIN_LAT,
            (row - WIN_LAT) * size.row_tokens + inner + win_pad,
            (row - 2 * WIN_LAT) * size.row_tokens + inner + 2 * win_pad,
        ),
    )
    give = one_hot(give_index, 2 * win_pad + low_rows)

    def arrive(step):
        def body(k, carry):
            index = ((place + step) % share) * n_lat + k
            local_slot = jnp.logical_and(index == slot, relay)

            @pl.when(local_slot)
            def _():
                own_block.wait()

            @pl.when(jnp.logical_not(local_slot))
            def _():
                block_copy(x_ref, index, own_send.at[0], (enc, lat, lon)).wait_recv()

            @pl.when(local_slot)
            def _():
                own_side.wait()

            @pl.when(jnp.logical_not(local_slot))
            def _():
                side_copy(x_ref, index, side_send.at[0], (enc, lat, lon)).wait_recv()

            if step == 0:
                for near in range(1, share):
                    side_pass(k, near).start()

            @pl.when(relay)
            def _():
                for at, side in enumerate(sides):
                    pass_copy(index, at * size.slots + index, (lat + side) % n_lat).start()

            if passes_on is not None:

                @pl.when(passes_on)
                def _():
                    pass_copy(index, index, opposite).start()

            return carry

        return body

    band_rows = n_lat * size.block_rows
    for step in order:
        lax.fori_loop(0, n_lat, arrive(step), 0)
        band = (place + step) % share
        values = lat_buf[pl.ds(band * n_lat, n_lat)].reshape(band_rows, size.width)
        hidden = layer_norm(values.astype(F32))[0].astype(BF16)
        rows = pl.ds(pl.multiple_of(band * band_rows, 16), band_rows)
        blocks_qkv[rows, :] = dot_tb(hidden, wqkv_ref[...]).astype(BF16)
    halo_f[:, : 3 * HD] = dot(order_ref[...], blocks_qkv[...])
    halo[...] = halo_f[...].astype(BF16)


    def exchange(source, target, send, recv, k, *place):
        return pltpu.make_async_remote_copy(
            src_ref=source,
            dst_ref=target,
            send_sem=send.at[k],
            recv_sem=recv.at[k],
            device_id=(enc, *place),
            device_id_type=MESH,
        )

    low_part = halo.at[pl.ds(0, low_rows)]
    high_part = halo.at[pl.ds(high_start, high_rows)]
    mid_part = halo.at[pl.ds(mid_start, mid_rows)]
    halo_copies = [
        exchange(low_part, halo_left, halo_send, halo_recv, 0, lat, next_lon),
        exchange(high_part, halo_diag, halo_send, halo_recv, 1, next_lat, next_lon),
        exchange(high_part, halo_up, halo_send, halo_recv, 2, next_lat, lon),
        exchange(mid_part, halo_right, halo_send, halo_recv, 3, lat, last_lon),
    ]
    for copy in halo_copies:
        copy.start()

    step_rows = tokens // 3
    blocks = lat_buf[...].reshape(size.slots * size.block_rows, size.width)

    def normalise(k, carry):
        rows = pl.ds(pl.multiple_of(k * step_rows, 16), step_rows)
        normed, inverse = layer_norm(dot(order_ref[rows, :], blocks))
        normed_ref[rows, :] = normed
        inv_ref[rows, :] = jnp.broadcast_to(inverse, (step_rows, 128))
        hidden = normed.astype(BF16)
        hid_ref[rows, :] = hidden
        products[rows, :] = dot_tb(hidden, wqkv_ref[...])
        return carry

    lax.fori_loop(0, 3, normalise, 0)
    ones = jnp.ones((8, size.width), BF16)
    weight_sums = dot_tb(ones, wqkv_ref[...])
    coarse = weight_sums.astype(BF16)
    finer = (weight_sums - coarse.astype(F32)).astype(BF16)
    index = lax.broadcasted_iota(jnp.int32, weight_sums.shape, 0)
    weight_sums = jnp.where(
        index == 0, coarse.astype(F32), jnp.where(index == 1, finer.astype(F32), 0.0)
    ).astype(BF16)

    for copy in halo_copies:
        copy.wait_recv()

    split = size.cols - col_shift

    def choose(condition, one, other):
        return jnp.where(condition, one.astype(F32), other.astype(F32))

    low = choose(column_of(low_rows) < split, halo[:low_rows, :], halo_left[...])
    high = choose(column_of(high_rows, high_start) < split, halo_up[...], halo_diag[...])
    middle = choose(
        column_of(mid_rows, mid_start) < split,
        halo_right[...],
        halo[mid_start : mid_start + mid_rows, :],
    )
    score_scale = HD ** (-0.5)

    def window(w, tokens_in, take):
        part = dot(take, tokens_in.astype(BF16)).astype(BF16)
        queries, keys = part[:, :HD], part[:, HD : 2 * HD]
        values, grads = part[:, 2 * HD : 3 * HD], part[:, 3 * HD :]
        first = lat * size.rows + w * WIN_LAT
        row_a = token_place(size, lax.broadcasted_iota(jnp.int32, (win, 1), 0))[0]
        row_b = token_place(size, lax.broadcasted_iota(jnp.int32, (1, win), 1))[0]
        side_a = jnp.where(row_a + first < row_shift, 1, 0)
        side_b = jnp.where(row_b + first < row_shift, 1, 0)
        scores = dot_tb(queries, keys) * score_scale
        weights = jnp.where(side_a == side_b, jnp.exp(scores), 0.0)
        probs = weights * (1.0 / jnp.sum(weights, axis=-1, keepdims=True))
        low = probs.astype(BF16)
        grad_probs = dot_tb(grads, values)
        grad_scores = probs * (
            grad_probs - jnp.sum(grad_probs * probs, axis=-1, keepdims=True)
        )
        grad_low = grad_scores.astype(BF16)
        there = pl.ds(w * win_pad, win)
        back_f[there, :HD] = dot(grad_low, keys) * score_scale
        back_f[there, HD : 2 * HD] = dot_ta(grad_low, queries) * score_scale
        back_f[there, 2 * HD : 3 * HD] = dot_ta(low, grads)
        back_f[there, 3 * HD :] = dot(low, values)
        back_f[pl.ds(w * win_pad + win, win_pad - win), :] = jnp.zeros((win_pad - win, 4 * HD), F32)
        whole = pl.ds(w * win_pad, win_pad)
        back[whole, :] = back_f[whole, :].astype(BF16)

    far_start = size.row_tokens // 16 * 16
    far_rows = win_pad - far_start
    early_part = back.at[pl.ds(0, low_rows)]
    late_part = back.at[pl.ds(far_start, far_rows)]
    second_part = back.at[pl.ds(win_pad, win_pad)]
    back_copies = [
        exchange(late_part, back_right, back_send, back_recv, 0, lat, last_lon),
        exchange(early_part, back_diag, back_send, back_recv, 1, last_lat, last_lon),
        exchange(early_part, back_down, back_send, back_recv, 2, last_lat, lon),
        exchange(second_part, back_left, back_send, back_recv, 3, lat, next_lon),
    ]
    window(0, jnp.concatenate([low, high], axis=0), take_first)
    for copy in back_copies[:3]:
        copy.start()
    window(1, middle, take_second)
    back_copies[3].start()

    @pl.when(away)
    def _():
        first_copy(0).wait_send()
        side_first(0).wait_send()

    for step in range(1, n_lat):
        side_first(step).wait_send()
    for near in range(1, share):
        for k in range(n_lat):
            side_pass(k, near).wait_send()

    for step in order[1:]:
        first_copy(step).wait_send()

    def passed(k, carry):
        @pl.when(relay)
        def _():
            for at, side in enumerate(sides):
                pass_copy(k, at * size.slots + k, (lat + side) % n_lat).wait_send()

        if passes_on is not None:

            @pl.when(passes_on)
            def _():
                pass_copy(k, k, opposite).wait_send()

        return carry

    lax.fori_loop(0, size.slots, passed, 0)
    for copy in back_copies:
        copy.wait_recv()

    here = back[...].astype(F32)
    cover = jnp.concatenate(
        [
            here[:far_start],
            choose(column_of(far_rows, far_start) >= col_shift, here[far_start:win_pad], back_right[...]),
            choose(column_of(win_pad) >= col_shift, back_left[...], here[win_pad:]),
            choose(column_of(low_rows) >= col_shift, back_down[...], back_diag[...]),
        ],
        axis=0,
    )
    own = dot(give, cover.astype(BF16)).astype(BF16)
    grad_rows, heads_out = own[:, : 3 * HD], own[:, 3 * HD :]

    sums = dot_tb(weight_sums, grad_rows)
    sums = sums + pltpu.roll(sums, 7, 0)
    cross = dot_tb(
        jnp.ones((8, 3 * HD), BF16), (grad_rows.astype(F32) * products[...]).astype(BF16)
    )
    lanes = 4 * 128
    pad = jnp.zeros((8, lanes - tokens), F32)
    sums = jnp.concatenate([sums, pad], axis=1)
    cross = jnp.concatenate([cross, pad], axis=1)
    index = lax.broadcasted_iota(jnp.int32, (8, 128), 0)
    extra = jnp.zeros((8, 128), F32)
    for k in range(4):
        columns = slice(k * 128, (k + 1) * 128)
        extra = jnp.where(index == k, jnp.broadcast_to(sums[:1, columns], (8, 128)), extra)
        extra = jnp.where(index == k + 4, cross[:, columns], extra)
    def sums_copy(step):
        target = ((home + step) % n_lat) * share + place
        return pltpu.make_async_remote_copy(
            src_ref=sums_out.at[0],
            dst_ref=sums_in.at[step - 1],
            send_sem=sums_send.at[step - 1],
            recv_sem=sums_recv.at[step - 1],
            device_id=(target, lat, lon),
            device_id_type=MESH,
        )

    def sums_part_copy(step):
        target = home * share + (place + step) % share
        return pltpu.make_async_remote_copy(
            src_ref=sums_out.at[1],
            dst_ref=sums_in.at[n_lat - 2 + step],
            send_sem=sums_send.at[n_lat - 2 + step],
            recv_sem=sums_recv.at[n_lat - 2 + step],
            device_id=(target, lat, lon),
            device_id_type=MESH,
        )

    filler = jnp.zeros((8, 128), F32)
    sums_out[0] = jnp.concatenate([extra, filler], axis=0).astype(BF16)
    sums_copies = [sums_copy(step) for step in range(1, n_lat)]
    sums_copies += [sums_part_copy(step) for step in range(1, share)]
    for copy in sums_copies[: n_lat - 1]:
        copy.start()

    later = tuple((place + step) % share for step in ((2, 1, 3, 0) if share == 4 else (1, 0)))

    most = packed - 48
    rest = pl.ds(most, packed - most)
    all_steps = (2, 1, 3, 0) if n_lat == 4 else (1, 0)

    def rest_copy(step, near):
        target = (place + near) % share
        return pltpu.make_async_remote_copy(
            src_ref=msg.at[((home + step) % n_lat) * share + target, rest],
            dst_ref=rest_in.at[step, near],
            send_sem=rest_send.at[step, near],
            recv_sem=rest_recv.at[step, near],
            device_id=(home * share + target, lat, lon),
            device_id_type=MESH,
        )

    def rest_part_copy(step):
        return pltpu.make_async_remote_copy(
            src_ref=rest_out.at[step],
            dst_ref=rest_part.at[step],
            send_sem=rest_send.at[step, 0],
            recv_sem=rest_recv.at[step, 0],
            device_id=(((home + step) % n_lat) * share + place, lat, lon),
            device_id_type=MESH,
        )

    rest_copies = []

    def group_copy(k, step):
        target = (home + step) % n_lat
        return pltpu.make_async_remote_copy(
            src_ref=msg.at[target * share + later[k], pl.ds(0, most)],
            dst_ref=msg_in.at[k, step],
            send_sem=msg_send.at[k, step],
            recv_sem=msg_recv.at[k, step],
            device_id=(target * share + place, lat, lon),
            device_id_type=MESH,
        )

    group_copies = []
    group_width = share * HD
    for step in all_steps:
        target = (home + step) % n_lat
        columns = pl.ds(pl.multiple_of(target * group_width, 128), group_width)
        head_part = dot(grad_rows, wqkv_ref[:, columns])
        for k in range(share):
            values = head_part[:, k // 2 * 128 : (k // 2 + 1) * 128]
            message = pack_pair(values, k % 2, half)
            msg[target * share + k] = jnp.concatenate([message, filler], axis=0).astype(BF16)
        if step > 0:
            for k in range(share):
                group_copies.append(group_copy(k, step))
                group_copies[-1].start()
        for near in range(1, share):
            rest_copies.append(rest_copy(step, near))
            rest_copies[-1].start()

    grad[:, :, :, : 3 * HD] = (
        (dot_ta(hid_ref[...], grad_rows) * factor)
        .astype(BF16)
        .reshape(n_lat, n_lon, size.chunk, 3 * HD)
    )
    grad[:, :, :, 3 * HD :] = (
        (dot_ta(cot_ref[...], heads_out) * factor)
        .astype(BF16)
        .reshape(n_lat, n_lon, size.chunk, HD)
    )

    pairs = n_lat // 2
    pair, core = lat // 2, lat % 2

    def core_copy(k):
        return pltpu.make_async_remote_copy(
            src_ref=grad.at[((pair + k) % pairs) * 2 + 1 - core],
            dst_ref=grad_in.at[k],
            send_sem=grad_send.at[k],
            recv_sem=grad_recv.at[k],
            device_id=(enc, pair * 2 + 1 - core, lon),
            device_id_type=MESH,
        )

    def pair_copy():
        return pltpu.make_async_remote_copy(
            src_ref=mid,
            dst_ref=mid_in,
            send_sem=grad_send.at[pairs],
            recv_sem=grad_recv.at[pairs],
            device_id=(enc, ((pair + 1) % pairs) * 2 + core, lon),
            device_id_type=MESH,
        )

    def line_copy(step):
        target = (lon + step) % n_lon
        return pltpu.make_async_remote_copy(
            src_ref=total_out.at[target],
            dst_ref=total_in.at[step],
            send_sem=total_send.at[step],
            recv_sem=total_recv.at[step],
            device_id=(enc, lat, target),
            device_id_type=MESH,
        )

    for k in reversed(range(pairs)):
        core_copy(k).start()
    feature_sums = jnp.concatenate([extra, filler], axis=0)
    for k in range(n_lat - 1):
        sums_copies[k].wait_recv()
        feature_sums = feature_sums + sums_in[k].astype(F32)
    sums_out[1] = feature_sums.astype(BF16)
    for copy in sums_copies[n_lat - 1 :]:
        copy.start()
    if pairs == 2:
        core_copy(1).wait_recv()
        mid[...] = (grad[(1 - pair) * 2 + core].astype(F32) + grad_in[1].astype(F32)).astype(BF16)
        pair_copy().start()

    for copy in halo_copies + back_copies:
        copy.wait_send()

    columns = pl.ds(pl.multiple_of((enc // 2) * 128, 128), 128)
    odd = enc % 2 == 1

    def own_share(values):
        return jnp.where(odd, pack_pair(values, 1, half), pack_pair(values, 0, half))

    def side_by_side(column):
        left = lax.broadcasted_iota(jnp.int32, (half, 128), 1) < HD
        return jnp.where(left, column[:half], column[half:])

    normed_own = own_share(normed_ref[:, columns])
    cot_own = own_share(cot_ref[:, columns].astype(F32))
    inverse_own = side_by_side(inv_ref[...])

    def part_copy(k):
        return pltpu.make_async_remote_copy(
            src_ref=part_out.at[k],
            dst_ref=part_in.at[k],
            send_sem=part_send.at[k],
            recv_sem=part_recv.at[k],
            device_id=(home * share + later[k], lat, lon),
            device_id_type=MESH,
        )

    def group_sum(k):
        values = msg[home * share + later[k], :most].astype(F32)
        for step in range(1, n_lat):
            group_copy(k, step).wait_recv()
            values = values + msg_in[k, step].astype(F32)
        return values

    def send_part(k):
        part_out[k] = group_sum(k).astype(BF16)
        part_copy(k).start()

    for k in range(n_lat - 1, len(sums_copies)):
        sums_copies[k].wait_recv()
        feature_sums = feature_sums + sums_in[k].astype(F32)
    feature_sums = feature_sums[:8]
    token = lax.broadcasted_iota(jnp.int32, (tokens, 1), 0)
    lane = lax.broadcasted_iota(jnp.int32, (tokens, 128), 1)
    line = jnp.right_shift(token, 7)
    pick = jnp.where(token - line * 128 == lane, 1.0, 0.0)
    means = lax.dot_general(
        pick,
        feature_sums,
        (((1,), (1,)), ((), ())),
        precision=lax.Precision.HIGHEST,
        preferred_element_type=F32,
    ) * (1.0 / size.width)
    which = lax.broadcasted_iota(jnp.int32, (tokens, 8), 1)
    mean_grad = jnp.sum(jnp.where(which == line, means, 0.0), axis=-1, keepdims=True)
    mean_cross = jnp.sum(jnp.where(which == line + 4, means, 0.0), axis=-1, keepdims=True)
    mean_grad_own, mean_cross_own = side_by_side(mean_grad), side_by_side(mean_cross)
    fixed = cot_own - inverse_own * (mean_grad_own + normed_own * mean_cross_own)

    def rest_sum(step):
        values = msg[((home + step) % n_lat) * share + place, most:].astype(F32)
        for near in range(1, share):
            rest_copy(step, near).wait_recv()
            values = values + rest_in[step, near].astype(F32)
        return values

    send_part(0)
    for step in all_steps[:-1]:
        rest_out[step] = rest_sum(step).astype(BF16)
        rest_part_copy(step).start()
    core_copy(0).wait_recv()
    weight_sum = grad[lat].astype(F32) + grad_in[0].astype(F32)
    if pairs == 2:
        pair_copy().wait_recv()
        weight_sum = weight_sum + mid_in[...].astype(F32)
    total_out[...] = weight_sum.astype(BF16)
    far_first = sorted(range(1, n_lon), key=lambda step: -min(step, n_lon - step))
    for step in far_first:
        line_copy(step).start()
    for k in range(1, share - 1):
        send_part(k)
    total = group_sum(share - 1)
    for copy in group_copies + sums_copies + rest_copies:
        copy.wait_send()
    for k in range(pairs):
        core_copy(k).wait_send()
    if pairs == 2:
        pair_copy().wait_send()
    for k in range(share - 1):
        part_copy(k).wait_recv()
        total = total + part_in[k].astype(F32)
    rest_total = rest_sum(0)
    for step in all_steps[:-1]:
        rest_part_copy(step).wait_recv()
        rest_total = rest_total + rest_part[step].astype(F32)
    total = jnp.concatenate([total, rest_total], axis=0)

    latent_out[...] = fixed + inverse_own * total[:half]

    weights = total_out[lon].astype(F32)
    for step in reversed(far_first):
        line_copy(step).wait_recv()
        weights = weights + total_in[step].astype(F32)
    weight_out[...] = weights

    for k in range(share - 1):
        part_copy(k).wait_send()
    for step in all_steps[:-1]:
        rest_part_copy(step).wait_send()
    for step in far_first:
        line_copy(step).wait_send()


def finish_kernel(size, packed_ref, weight_ref, latent_out, qkv_out, proj_out):
    latent = packed_ref[...]
    other = pltpu.roll(latent, HD, 1)
    lines = size.rows * LEVELS // 2
    for k in range(2 * lines):
        start = (k % lines) * size.cols
        values = (latent, other)[k // lines][start : start + size.cols, :HD]
        latent_out[k % LEVELS, k // LEVELS] = values.astype(BF16)
    qkv_out[...] = weight_ref[:, : 3 * HD]
    proj_out[...] = weight_ref[:, 3 * HD :]


def finish(size, packed, weights):
    vmem = pl.BlockSpec(memory_space=pltpu.VMEM)
    return pl.pallas_call(
        functools.partial(finish_kernel, size),
        out_shape=(
            jax.ShapeDtypeStruct((LEVELS, size.rows, size.cols, HD), BF16),
            jax.ShapeDtypeStruct((size.chunk, 3 * HD), F32),
            jax.ShapeDtypeStruct((size.chunk, HD), F32),
        ),
        in_specs=[vmem, vmem],
        out_specs=(vmem, vmem, vmem),
    )(packed, weights)


def layer(size, lat_shift, lon_shift, arrays, key, value, merge, wqkv, proj):
    tokens, packed = size.tokens, size.packed
    atmos, land = arrays[0], arrays[1]
    vmem = pl.BlockSpec(memory_space=pltpu.VMEM)
    smem = pl.BlockSpec(memory_space=pltpu.SMEM)
    factor = (tokens * size.group) ** (-0.5)
    wide = 4 * HD
    dma = pltpu.SemaphoreType.DMA
    low = -(-(WIN_LAT - 1) * size.row_tokens // 16) * 16
    high = tokens - (size.rows - WIN_LAT + 1) * size.row_tokens // 16 * 16
    one_row = size.row_tokens // 16 * 16
    middle = -(-(size.rows - 1) * size.row_tokens // 16) * 16 - one_row
    return pl.pallas_call(
        functools.partial(layer_kernel, size, factor),
        out_shape=(
            jax.ShapeDtypeStruct((size.half, 128), F32),
            jax.ShapeDtypeStruct((size.chunk, wide), F32),
        ),
        in_specs=[smem, smem] + [vmem] * len(arrays) + [pl.BlockSpec(memory_space=pl.ANY)] * 7,
        out_specs=(vmem, vmem),
        scratch_shapes=[
            pltpu.VMEM((4 * size.block_rows, size.fine_total), BF16),
            pltpu.VMEM(key.shape, BF16),
            pltpu.VMEM(key.shape, BF16),
            pltpu.VMEM(merge.shape, BF16),
            pltpu.VMEM((tokens, size.slots * size.block_rows), BF16),
            pltpu.VMEM(wqkv.shape, BF16),
            pltpu.VMEM(proj.shape, BF16),
            pltpu.VMEM((tokens, size.width), BF16),
            pltpu.VMEM((size.patches, LINES, atmos.shape[3]), BF16),
            pltpu.VMEM((size.patch_rows, land.shape[2]), F32),
            pltpu.VMEM((LINES, key.shape[0]), F32),
            pltpu.VMEM((size.fine_total, key.shape[0]), F32),
            pltpu.VMEM((size.block_rows, size.width), BF16),
            pltpu.VMEM((size.slots, size.block_rows, size.width), BF16),
            pltpu.VMEM((tokens, size.width), F32),
            pltpu.VMEM((tokens, 128), F32),
            pltpu.VMEM((tokens, size.width), BF16),
            pltpu.VMEM((size.slots * size.block_rows, 3 * HD), BF16),
            pltpu.VMEM((tokens, 3 * HD), F32),
            pltpu.VMEM((tokens, wide), F32),
            pltpu.VMEM((tokens, wide), BF16),
            pltpu.VMEM((low, wide), BF16),
            pltpu.VMEM((high, wide), BF16),
            pltpu.VMEM((high, wide), BF16),
            pltpu.VMEM((middle, wide), BF16),
            pltpu.VMEM((2 * packed, wide), F32),
            pltpu.VMEM((2 * packed, wide), BF16),
            pltpu.VMEM((packed - one_row, wide), BF16),
            pltpu.VMEM((low, wide), BF16),
            pltpu.VMEM((low, wide), BF16),
            pltpu.VMEM((packed, wide), BF16),
            pltpu.VMEM((size.enc, packed, 128), BF16),
            pltpu.VMEM((size.share, size.lat, packed - 48, 128), BF16),
            pltpu.VMEM((size.share, packed - 48, 128), BF16),
            pltpu.VMEM((size.share, packed - 48, 128), BF16),
            pltpu.VMEM((size.lat, size.lon, size.chunk, wide), BF16),
            pltpu.VMEM((size.lat // 2, size.lon, size.chunk, wide), BF16),
            pltpu.VMEM((size.lon, size.chunk, wide), BF16),
            pltpu.VMEM((size.lon, size.chunk, wide), BF16),
            pltpu.VMEM((size.lon, size.chunk, wide), BF16),
            pltpu.VMEM((size.lon, size.chunk, wide), BF16),
            dma((7,)),
            dma((size.share,)),
            dma((2 * size.slots,)),
            dma((size.slots,)),
            dma((4,)),
            dma((4,)),
            dma((4,)),
            dma((4,)),
            dma((size.share, size.lat)),
            dma((size.share, size.lat)),
            dma((size.share,)),
            dma((size.share,)),
            dma((size.lat,)),
            dma((size.lat,)),
            dma((size.lon,)),
            dma((size.lon,)),
            pltpu.VMEM((2, 16, 128), BF16),
            pltpu.VMEM((size.lat + size.share - 2, 16, 128), BF16),
            dma((size.lat + size.share - 2,)),
            dma((size.lat + size.share - 2,)),
            dma((size.lat * size.share,)),
            dma((size.slots,)),
            pltpu.VMEM((size.lat, size.share, 48, 128), BF16),
            pltpu.VMEM((size.lat, 48, 128), BF16),
            pltpu.VMEM((size.lat, 48, 128), BF16),
            dma((size.lat, size.share)),
            dma((size.lat, size.share)),
        ],
        compiler_params=pltpu.CompilerParams(
            collective_id=0, has_side_effects=True, vmem_limit_bytes=56 * 1024 * 1024
        ),
    )(
        lat_shift,
        lon_shift,
        *arrays,
        jnp.asarray(merge_order(size), BF16),
        key,
        value,
        merge,
        jnp.asarray(block_order(size), BF16),
        wqkv,
        proj,
    )


def local(
    atmos,
    land_sea,
    level_count,
    atm_weight,
    land_weight,
    level_embed,
    latent_query,
    key_weight,
    value_weight,
    merge_weight,
    lat_shift,
    lon_shift,
    qkv_weight,
    proj_weight,
    cotangent,
):
    size = Sizes(
        lax.axis_size("enc"),
        lax.axis_size("lat"),
        lax.axis_size("lon"),
        atmos.shape[0],
        atmos.shape[1],
        merge_weight.shape[1],
    )
    arrays = (
        atmos,
        land_sea,
        level_count,
        atm_weight,
        land_weight,
        level_embed,
        latent_query,
        cotangent,
    )
    packed, weights = layer(
        size,
        lat_shift,
        lon_shift,
        arrays,
        key_weight,
        value_weight,
        merge_weight,
        qkv_weight.T,
        proj_weight,
    )
    latent, grad_qkv, grad_proj = finish(size, packed, weights)
    return latent, grad_qkv, grad_proj.T


def solution(mesh):
    return jax.shard_map(
        local,
        mesh=mesh,
        in_specs=(
            P("enc", ("lon", "lat"), None, None),
            P("enc", ("lon", "lat"), None),
            P("enc", ("lon", "lat")),
            P(),
            P(),
            P(),
            P(),
            P(),
            P(),
            P(),
            P(),
            P(),
            P(None, "enc"),
            P("enc", None),
            P(None, "lat", "lon", None),
        ),
        out_specs=(
            P(None, "lat", "lon", "enc"),
            P(("lat", "lon"), "enc"),
            P("enc", ("lat", "lon")),
        ),
        check_vma=False,
    )
```
